32 devices in a mesh: band: 16 (over z, y, core), grp: 2 (over x).
Axes of the slice: x: 2, y: 2, z: 4, core: 2. Of those that a mesh axis runs over, the one named last changes fastest.
Arguments:
- tokens: bfloat16 [2, 16, 1536, 512], P('grp', 'band'), may hold values from -6 to 6
- row_place: int32 [2, 16], P('grp', 'band'), may hold values from 0 to 7, as said below
- row_width: int32 [2, 16], P('grp', 'band'), may hold values from 96 to 192, as said below
- cotangent: bfloat16 [2, 16, 1536, 512], P('grp', 'band'), may hold values from -6 to 6
- chan_embed: bfloat16 [3, 512], replicated, may hold values from -3 to 3
- w_query: bfloat16 [512, 512], replicated, may hold values from -0.25 to 0.25
- w_key: bfloat16 [512, 512], replicated, may hold values from -0.25 to 0.25
- w_value: bfloat16 [512, 512], replicated, may hold values from -0.25 to 0.25
- w_out: bfloat16 [512, 512], replicated, may hold values from -4 to 4
- w_in: bfloat16 [512, 2048], replicated, may hold values from -0.25 to 0.25
- bias_in: bfloat16 [2048], replicated, may hold values from -3 to 3
- w_back: bfloat16 [2048, 512], replicated, may hold values from -0.125 to 0.125
- bias_back: bfloat16 [512], replicated, may hold values from -3 to 3
- gain_first: bfloat16 [512], replicated, may hold values from 0.099609375 to 1.8984375
- shift_first: bfloat16 [512], replicated, may hold values from -2 to 2
- gain_second: bfloat16 [512], replicated, may hold values from 0.099609375 to 1.8984375
- shift_second: bfloat16 [512], replicated, may hold values from -2 to 2
Outputs:
- layer_out: bfloat16 [2, 16, 1536, 512], P('grp', 'band')
- grad_tokens: bfloat16 [2, 16, 1536, 512], P('grp', 'band')
- grad_query: float32 [512, 512], P('band')
- grad_key: float32 [512, 512], P('band')
- grad_value: float32 [512, 512], P('band')
- grad_out: float32 [512, 512], P('band')
- grad_in: float32 [512, 2048], P('band')
- grad_bias_in: float32 [2048], P('band')
- grad_back: float32 [2048, 512], P('band')
- grad_bias_back: float32 [512], P('band')
- grad_gain_first: float32 [512], P('band')
- grad_shift_first: float32 [512], P('band')
- grad_gain_second: float32 [512], P('band')
- grad_shift_second: float32 [512], P('band')
- grad_embed: float32 [3, 512], P(None, 'band')
The draws below stay inside these ranges and needn't reach their ends.
Inputs may be any that keep to these rules, and one draw needn't show every extreme that they name: The block rows of each group hold images one after another; the first one has begun 2 or 3 block rows above the first block row and the last one may be cut short. A tall image has 8 block rows and a short one 8 / 2, and row_place numbers an image's block rows from 0. In every group the first image is tall and the second is short. No image begins at the first, the middle or the last block row of a group. `row_width`: 192 on the block rows of tall images and 96 on those of short ones; the other channel positions of a row are padding.
All inputs are finite; a program needn't handle non-finite values.
Results may differ from the reference program's by a relative error of at most 0.012.
The reference program's roundings to bfloat16 on the way count: a program that leaves them out, or rounds other values in their place, can miss the bound.
Values may be sent and summed in bfloat16 or wider, within the bound.
A program may use at most 256 MiB of HBM per device.

```python
import jax
import jax.numpy as jnp
from jax import lax

D = 512
HEADS = 8
HEAD_DIM = 64
FF = 2048
ROW_POS = 192
BLOCK_ROWS = 8
BLOCK_COLS = 32
FLANK_COLS = 16
TALL_ROWS = 8
GROUPS = 2
STACK_ROWS = 16
BLOCK_LEN = 1536


def image_layout(key):
    offset_key = jax.random.fold_in(key, 101)
    flag_key = jax.random.fold_in(key, 202)
    offset = jax.random.randint(offset_key, (GROUPS, 1), 2, 4).astype(jnp.int32)
    tall_flag = jax.random.randint(flag_key, (GROUPS, STACK_ROWS), 0, 2).astype(jnp.int32)
    row_index = jnp.arange(STACK_ROWS, dtype=jnp.int32)
    tall_flag = jnp.where(row_index[None, :] == 0, 1, jnp.where(row_index[None, :] == 1, 0, tall_flag))
    lengths = TALL_ROWS // 2 + TALL_ROWS // 2 * tall_flag
    starts = jnp.cumsum(lengths, axis=1) - lengths - offset
    covered = (starts[:, None, :] <= row_index[None, :, None]).astype(jnp.int32)
    image_index = jnp.sum(covered, axis=2) - 1
    start_of = jnp.take_along_axis(starts, image_index, axis=1)
    tall_of = jnp.take_along_axis(tall_flag, image_index, axis=1)
    return (row_index[None, :] - start_of, ROW_POS // 2 + ROW_POS // 2 * tall_of)


def draw_row_place(key, part):
    layout = image_layout(key)
    return layout[0].astype(jnp.int32)


def draw_row_width(key, part):
    layout = image_layout(key)
    return layout[1].astype(jnp.int32)


def level_of(key, extent, split, smallest, high):
    loudness, own = 1.0, jax.random.fold_in(key, 6)
    for dim, parts in split:
        steps = jnp.exp(jax.random.uniform(jax.random.fold_in(own, dim), (parts,), jnp.float32, smallest / len(split), high / len(split)))
        loudness = loudness * jnp.repeat(steps, extent[dim] // parts).reshape([-1 if axis == dim else 1 for axis in range(len(extent))])
    return loudness


def normal_values(stream_key, shape, deviation, limit, cuts=(), held_as=jnp.bfloat16):
    array = deviation * jax.random.normal(stream_key, shape, jnp.float32)
    if cuts:
        array = array * level_of(stream_key, shape, cuts, -0.22, 0.18)
    return jnp.clip(array, -limit, limit).astype(held_as)


def setup_inputs(seed: int = 0) -> dict:
    seeds = jax.random.split(jax.random.key(seed), 18)
    tokens = normal_values(seeds[0], (GROUPS, STACK_ROWS, BLOCK_LEN, D), 1.0, 6.0, ((0, 2), (1, 16)))
    row_place = draw_row_place(jax.random.fold_in(seeds[17], 71), 0)
    row_width = draw_row_width(jax.random.fold_in(seeds[17], 71), 0)
    cotangent = normal_values(seeds[3], (GROUPS, STACK_ROWS, BLOCK_LEN, D), 1.0, 6.0, ((0, 2), (1, 16)))
    chan_embed = normal_values(seeds[4], (3, D), 0.5, 3.0)
    w_query = normal_values(seeds[5], (D, D), D ** -0.5, 0.25)
    w_key = normal_values(seeds[6], (D, D), D ** -0.5, 0.25)
    w_value = normal_values(seeds[7], (D, D), D ** -0.5, 0.25)
    w_out = normal_values(seeds[8], (D, D), (max(D // 256, 1)) ** -0.5, 4.0)
    w_in = normal_values(seeds[9], (D, FF), D ** -0.5, 0.25)
    bias_in = normal_values(seeds[10], (FF,), 0.5, 3.0)
    w_back = normal_values(seeds[11], (FF, D), FF ** -0.5, 0.125)
    bias_back = normal_values(seeds[12], (D,), 0.5, 3.0)
    gain_first = jnp.clip(1.0 + 0.18 * jax.random.normal(seeds[13], (D,), jnp.float32), 0.099609375, 1.8984375).astype(jnp.bfloat16)
    shift_first = normal_values(seeds[14], (D,), 0.3, 2.0)
    gain_second = jnp.clip(1.0 + 0.18 * jax.random.normal(seeds[15], (D,), jnp.float32), 0.099609375, 1.8984375).astype(jnp.bfloat16)
    shift_second = normal_values(seeds[16], (D,), 0.3, 2.0)
    return dict(tokens=tokens, row_place=row_place, row_width=row_width, cotangent=cotangent, chan_embed=chan_embed, w_query=w_query, w_key=w_key, w_value=w_value, w_out=w_out, w_in=w_in, bias_in=bias_in, w_back=w_back, bias_back=bias_back, gain_first=gain_first, shift_first=shift_first, gain_second=gain_second, shift_second=shift_second)


norm_eps = 1e-06
big_negative = -1e+30

@jax.custom_vjp
def low(v):
    return lax.optimization_barrier(v.astype(jnp.bfloat16)).astype(jnp.float32)

@jax.custom_vjp
def low_back(v):
    return v

def low_keep(v):
    return (low(v), None)

def low_pass(kept, grad):
    return (grad,)

def back_keep(v):
    return (v, None)

def back_low(kept, grad):
    return (low(grad),)
low.defvjp(low_keep, low_pass)
low_back.defvjp(back_keep, back_low)

def high_dot(left, right):
    return jnp.dot(left, right, precision=lax.Precision.HIGHEST)

def layer_norm(values, gain_vec, shift_vec):
    center = values - lax.optimization_barrier(jnp.mean(values, axis=-1, keepdims=True))
    spread = lax.optimization_barrier(jnp.mean(center * center, axis=-1, keepdims=True))
    return center * lax.rsqrt(spread + norm_eps) * gain_vec + shift_vec

def window_mask(row_place, row_width):
    windows = ROW_POS // BLOCK_COLS
    span_cols = BLOCK_COLS + 2 * FLANK_COLS
    queries = jnp.arange(BLOCK_ROWS * BLOCK_COLS, dtype=jnp.int32)
    memory = jnp.arange(2 * BLOCK_ROWS * span_cols, dtype=jnp.int32)
    starts = jnp.arange(windows, dtype=jnp.int32) * BLOCK_COLS
    query_row = (queries // BLOCK_COLS)[None, :, None]
    query_col = starts[:, None, None] + (queries % BLOCK_COLS)[None, :, None]
    memory_row = (memory // span_cols)[None, None, :] - BLOCK_ROWS
    memory_col = starts[:, None, None] - FLANK_COLS + (memory % span_cols)[None, None, :]
    col_limit = row_width[:, None, None, None]
    inside = (memory_col >= 0)[None] & (memory_col[None] < col_limit)
    upper_ok = (memory_row < 0)[None] & (row_place[:, None, None, None] > 0)
    earlier = (memory_row >= 0) & ((memory_row < query_row) | (memory_row == query_row) & (memory_col <= query_col))
    itself = (memory_row == query_row) & (memory_col == query_col)
    return inside & (upper_ok | earlier[None]) | itself[None]

def gather_windows(upper_rows, lower_rows):
    count = upper_rows.shape[0]
    chans = upper_rows.shape[-1]
    windows = ROW_POS // BLOCK_COLS
    span_cols = BLOCK_COLS + 2 * FLANK_COLS
    stacked = jnp.concatenate([upper_rows.reshape(count, BLOCK_ROWS, ROW_POS, chans), lower_rows.reshape(count, BLOCK_ROWS, ROW_POS, chans)], axis=1)
    padded = jnp.pad(stacked, ((0, 0), (0, 0), (FLANK_COLS, FLANK_COLS), (0, 0)))
    pieces = [padded[:, :, window * BLOCK_COLS:window * BLOCK_COLS + span_cols] for window in range(windows)]
    return jnp.stack(pieces, axis=1).reshape(count, windows, 2 * BLOCK_ROWS * span_cols, chans)

def to_blocks(flat_rows):
    count = flat_rows.shape[0]
    chans = flat_rows.shape[-1]
    windows = ROW_POS // BLOCK_COLS
    parted = flat_rows.reshape(count, BLOCK_ROWS, windows, BLOCK_COLS, chans)
    return parted.transpose(0, 2, 1, 3, 4).reshape(count, windows, BLOCK_ROWS * BLOCK_COLS, chans)

def from_blocks(blocks):
    count = blocks.shape[0]
    chans = blocks.shape[-1]
    windows = ROW_POS // BLOCK_COLS
    parted = blocks.reshape(count, windows, BLOCK_ROWS, BLOCK_COLS, chans)
    return parted.transpose(0, 2, 1, 3, 4).reshape(count, BLOCK_ROWS * ROW_POS, chans)

def attend_rows(pieces):
    query_rows, upper_key, key_rows, upper_value, value_rows, place_one, width_one = pieces
    allowed = window_mask(place_one[None], width_one[None])[0]
    query_blk = to_blocks(query_rows[None])[0]
    key_mem = gather_windows(upper_key[None], key_rows[None])[0]
    value_mem = gather_windows(upper_value[None], value_rows[None])[0]
    windows = query_blk.shape[0]
    query_heads = query_blk.reshape(windows, -1, HEADS, HEAD_DIM)
    key_heads = key_mem.reshape(windows, -1, HEADS, HEAD_DIM)
    value_heads = value_mem.reshape(windows, -1, HEADS, HEAD_DIM)
    scores = low_back(jnp.einsum('wqhe,wkhe->whqk', query_heads, key_heads, precision=lax.Precision.HIGHEST) * HEAD_DIM ** (-0.5))
    scores = jnp.where(allowed[:, None], scores, big_negative)
    peak = lax.optimization_barrier(jnp.max(scores, axis=-1, keepdims=True))
    raised = jnp.exp(scores - peak)
    probs = low(raised / lax.optimization_barrier(jnp.sum(raised, axis=-1, keepdims=True)))
    mixed = jnp.einsum('whqk,wkhe->wqhe', probs, value_heads, precision=lax.Precision.HIGHEST)
    return from_blocks(mixed.reshape(windows, -1, HEADS * HEAD_DIM)[None])[0]

def layer_forward(inputs, params, places, widths):
    chan_embed, w_query, w_key, w_value, w_out, w_in, bias_in, w_back, bias_back, gain_first, shift_first, gain_second, shift_second = params
    stack_len = inputs.shape[0]
    start = (inputs.reshape(stack_len, BLOCK_LEN // 3, 3, D) + chan_embed).reshape(-1, D)
    start_low = low(start)
    start_rows = start_low.reshape(stack_len, BLOCK_LEN, D)
    upper_start = jnp.concatenate([jnp.zeros_like(start_rows[:1]), start_rows[:-1]], axis=0).reshape(-1, D)
    query_all = low(low_back(high_dot(start_low, w_query))).reshape(stack_len, BLOCK_LEN, D)
    key_all = low(low_back(high_dot(start_low, w_key))).reshape(stack_len, BLOCK_LEN, D)
    value_all = low(low_back(high_dot(start_low, w_value))).reshape(stack_len, BLOCK_LEN, D)
    upper_key = low(low_back(high_dot(upper_start, w_key))).reshape(stack_len, BLOCK_LEN, D)
    upper_value = low(low_back(high_dot(upper_start, w_value))).reshape(stack_len, BLOCK_LEN, D)
    mixed = lax.map(jax.checkpoint(attend_rows), (query_all, upper_key, key_all, upper_value, value_all, places, widths))
    attn_low = low(low_back(mixed.reshape(-1, D)))
    branch = low_back(high_dot(attn_low, w_out))
    normed = layer_norm(start + branch, gain_first, shift_first)
    normed_low = low(normed)
    hidden_pre = low_back(high_dot(normed_low, w_in) + bias_in)
    activated = low(jax.nn.gelu(hidden_pre))
    ffn_out = low_back(high_dot(activated, w_back) + bias_back)
    return layer_norm(normed + ffn_out, gain_second, shift_second).reshape(stack_len, BLOCK_LEN, D)

def reference(tokens, row_place, row_width, cotangent, chan_embed, w_query, w_key, w_value, w_out, w_in, bias_in, w_back, bias_back, gain_first, shift_first, gain_second, shift_second):
    params = tuple((weight.astype(jnp.float32) for weight in (chan_embed, w_query, w_key, w_value, w_out, w_in, bias_in, w_back, bias_back, gain_first, shift_first, gain_second, shift_second)))

    def group_step(carried, pieces):
        tokens_one, places, widths, cot_one = pieces

        def forward(inputs, weights):
            return layer_forward(inputs, weights, places, widths)
        result, pullback = jax.vjp(forward, tokens_one.astype(jnp.float32), params)
        grad_inputs, grad_weights = pullback(cot_one.astype(jnp.float32))
        carried = tuple((before + added for before, added in zip(carried, grad_weights)))
        return (carried, (result.astype(jnp.bfloat16), grad_inputs.astype(jnp.bfloat16)))
    zeros_start = tuple((jnp.zeros_like(weight) for weight in params))
    summed, (layer_out, grad_tokens) = lax.scan(group_step, zeros_start, (tokens, row_place, row_width, cotangent))
    return (layer_out, grad_tokens, summed[1], summed[2], summed[3], summed[4], summed[5], summed[6], summed[7], summed[8], summed[9], summed[10], summed[11], summed[12], summed[0])
```

```python
import functools

import jax
import jax.numpy as jnp
from jax import lax
from jax.experimental import pallas as pl
from jax.experimental.pallas import tpu as pltpu
from jax.sharding import PartitionSpec as P

HEAD_DIM = 64
ROW_POS = 192
BLOCK_ROWS = 8
BLOCK_COLS = 32
FLANK_COLS = 16
WINDOWS = ROW_POS // BLOCK_COLS
BLOCKS = ROW_POS // FLANK_COLS
TILE = BLOCK_ROWS * FLANK_COLS
QUERIES = 2 * TILE
SPAN = 4 * TILE
LEN = BLOCK_ROWS * ROW_POS
PADDED = LEN + 2 * TILE

norm_eps = 1e-06
big_negative = -1e30
F32 = jnp.float32
BF16 = jnp.bfloat16
GELU_SCALE = 0.7978845608028654
GELU_CUBE = 0.044715


def dot(left, right):
    return jnp.dot(left, right, preferred_element_type=F32)


def dot_nt(left, right):
    return lax.dot_general(left, right, (((1,), (1,)), ((), ())), preferred_element_type=F32)


def iota(shape, dim):
    return lax.broadcasted_iota(jnp.int32, shape, dim)


def identity(size):
    return jnp.where(iota((size, size), 0) == iota((size, size), 1), 1.0, 0.0).astype(BF16)


def lanes(start, size):
    return pl.ds(pl.multiple_of(start, 128), size)


def transposed(eye, value):
    step = eye.shape[0]
    parts = [
        dot_nt(eye, value[:, at : at + step]).astype(BF16) for at in range(0, value.shape[1], step)
    ]
    return jnp.concatenate(parts, axis=0)


def column(eye, row):
    step = eye.shape[0]
    ones = jnp.ones((128, step), BF16)
    parts = [
        dot_nt(jnp.where(eye > 0, row[:, at : at + step], 0).astype(BF16), ones)
        for at in range(0, row.shape[1], step)
    ]
    return jnp.concatenate(parts, axis=0)


def wide(value):
    return jnp.concatenate([value, value], axis=1)


def halves(value):
    return value[:, :128] + value[:, 128:]


def lane_sums(value):
    ones = jnp.ones((8, 128), BF16)
    high = value.astype(BF16)
    rest = value - high.astype(F32)
    middle = rest.astype(BF16)
    low = (rest - middle.astype(F32)).astype(BF16)
    return dot_nt(ones, high) + dot_nt(ones, middle) + dot_nt(ones, low)


def fill_embed(embed_ref, rows_ref):
    embed = embed_ref[...].astype(F32)
    channel = lax.rem(iota(rows_ref.shape, 0), 3)
    rows_ref[...] = jnp.where(
        channel == 0, embed[0:1], jnp.where(channel == 1, embed[1:2], embed[2:3])
    )


def block_rows(rows_ref, block):
    return rows_ref[:, pl.ds(pl.multiple_of(block * FLANK_COLS, FLANK_COLS), FLANK_COLS), :]


def raw_window(rows_ref, window):
    parts = [block_rows(rows_ref, 2 * window + half).reshape(TILE, -1) for half in range(2)]
    return jnp.concatenate(parts, axis=0)


def embed_window(embed_rows, window):
    parts = []
    for half in range(2):
        at = pl.multiple_of((2 * window + half) * FLANK_COLS, FLANK_COLS)
        part = embed_rows[pl.ds(at, FLANK_COLS), :][None]
        parts.append(jnp.broadcast_to(part, (BLOCK_ROWS,) + part.shape[1:]).reshape(TILE, -1))
    return jnp.concatenate(parts, axis=0)


def start_window(rows_ref, embed_rows, window):
    return raw_window(rows_ref, window).astype(F32) + embed_window(embed_rows, window)


def norm_stats(value):
    center = value - jnp.mean(value, axis=0, keepdims=True)
    spread = jnp.mean(center * center, axis=0, keepdims=True)
    inverse = lax.rsqrt(spread + norm_eps)
    return center * inverse, inverse


def norm_back(normed, inverse, grad, gain):
    scaled = grad * gain
    first = jnp.mean(scaled, axis=0, keepdims=True)
    second = jnp.mean(scaled * normed, axis=0, keepdims=True)
    return (scaled - first - normed * second) * inverse


def vmem():
    return pl.BlockSpec(memory_space=pltpu.VMEM)


def smem():
    return pl.BlockSpec(memory_space=pltpu.SMEM)


def hbm():
    return pl.BlockSpec(memory_space=pl.ANY)


LIMIT = 60 * 1024 * 1024


def head_of_pair(value, half):
    keep = (iota(value.shape, 0) // HEAD_DIM) == half
    return jnp.where(keep, value, jnp.zeros_like(value))


def store_pairs(ref, at, value):
    for pair in range(value.shape[1] // 128):
        ref[pair, pl.ds(at, value.shape[0]), :] = value[:, pair * 128 : (pair + 1) * 128]


def clear_pads_rows(ref):
    pad = jnp.zeros((ref.shape[0], TILE, ref.shape[2]), ref.dtype)
    ref[:, 0:TILE, :] = pad
    ref[:, PADDED - TILE : PADDED, :] = pad


def clear_pads_lanes(ref):
    pad = jnp.zeros((ref.shape[0], TILE), ref.dtype)
    ref[:, 0:TILE] = pad
    ref[:, PADDED - TILE : PADDED] = pad


def attend_kernel(
    place_ref, width_ref, has_ref, tok_ref, up_ref, embed_ref, wq_ref, wk_ref, wv_ref,
    xt_ref, xut_ref, qt_ref, ot_ref, inv_ref, e_ref,
    embed_rows, wqt, wvt, keys, keys_up, vt, vt_up, bias_low, bias_up, e_buf, e_sem,
):
    eye = identity(256)
    fill_embed(embed_ref, embed_rows)
    wqt[...] = transposed(eye, wq_ref[...])
    wvt[...] = transposed(eye, wv_ref[...])
    clear_pads_rows(keys)
    clear_pads_rows(keys_up)
    clear_pads_lanes(vt)
    clear_pads_lanes(vt_up)
    has_up = has_ref[0, 0].astype(F32)
    place = place_ref[0, 0]
    width = width_ref[0, 0]

    @pl.loop(0, WINDOWS)
    def _(window):
        at = pl.multiple_of(window * QUERIES, QUERIES)
        padded_at = pl.multiple_of(window * QUERIES + TILE, TILE)
        low = start_window(tok_ref, embed_rows, window).astype(BF16)
        low_t = transposed(eye, low)
        xt_ref[:, pl.ds(at, QUERIES)] = low_t
        qt_ref[:, pl.ds(at, QUERIES)] = dot(wqt[...], low_t).astype(BF16) * BF16(0.125)
        store_pairs(keys, padded_at, dot(low, wk_ref[...]).astype(BF16))
        vt[:, pl.ds(padded_at, QUERIES)] = dot(wvt[...], low_t).astype(BF16)
        upper = (start_window(up_ref, embed_rows, window) * has_up).astype(BF16)
        upper_t = transposed(eye, upper)
        xut_ref[:, pl.ds(at, QUERIES)] = upper_t
        store_pairs(keys_up, padded_at, dot(upper, wk_ref[...]).astype(BF16))
        vt_up[:, pl.ds(padded_at, QUERIES)] = dot(wvt[...], upper_t).astype(BF16)

    def e_copy(window, slot):
        return pltpu.make_async_copy(e_buf.at[slot], e_ref.at[window], e_sem.at[slot])

    @pl.loop(0, WINDOWS)
    def _(window):
        at = pl.multiple_of(window * QUERIES, QUERIES)
        slot = lax.rem(window, 2)

        @pl.when(window >= 2)
        def _():
            e_copy(window - 2, slot).wait()

        shape = (SPAN, QUERIES)
        memory, query = iota(shape, 0), iota(shape, 1)
        memory_col = (memory // TILE) * FLANK_COLS + memory % FLANK_COLS - FLANK_COLS
        query_col = (query // TILE) * FLANK_COLS + query % FLANK_COLS
        memory_row = (memory % TILE) // FLANK_COLS
        query_row = (query % TILE) // FLANK_COLS
        column_at = memory_col + window * BLOCK_COLS
        inside = (column_at >= 0) & (column_at < width)
        earlier = (memory_row < query_row) | ((memory_row == query_row) & (memory_col <= query_col))
        itself = (memory_row == query_row) & (memory_col == query_col)
        bias_low[...] = jnp.where((inside & earlier) | itself, 0.0, big_negative)
        bias_up[...] = jnp.where(inside & (place > 0), 0.0, big_negative)

        @pl.loop(0, 4)
        def _(pair):
            feats = pl.ds(pl.multiple_of(pair * 128, 128), 128)
            q_pair = qt_ref[feats, pl.ds(at, QUERIES)]
            span = pl.ds(at, SPAN)
            k_low = keys[pair, span, :]
            k_up = keys_up[pair, span, :]
            for half in range(2):
                q_head = head_of_pair(q_pair, half)
                s_up = dot(k_up, q_head) + bias_up[...]
                s_low = dot(k_low, q_head) + bias_low[...]
                peak = jnp.maximum(
                    jnp.max(s_up, axis=0, keepdims=True), jnp.max(s_low, axis=0, keepdims=True)
                )
                r_up = jnp.exp(s_up - peak)
                r_low = jnp.exp(s_low - peak)
                total = jnp.sum(r_up, axis=0, keepdims=True) + jnp.sum(r_low, axis=0, keepdims=True)
                e_up = r_up.astype(BF16)
                e_low = r_low.astype(BF16)
                head = 2 * pair + half
                e_buf[slot, head, 0:SPAN, :] = e_up
                e_buf[slot, head, SPAN : 2 * SPAN, :] = e_low
                mine = pl.ds(pl.multiple_of(pair * 128 + half * HEAD_DIM, HEAD_DIM), HEAD_DIM)
                mixed = dot(vt_up[mine, span], e_up) + dot(vt[mine, span], e_low)
                inverse = 1.0 / total
                ot_ref[mine, pl.ds(at, QUERIES)] = (mixed * inverse).astype(BF16)
                inv_ref[pl.ds(head, 1), pl.ds(at, QUERIES)] = inverse

        e_copy(window, slot).start()

    for last in range(2):
        e_copy(WINDOWS - 2 + last, last).wait()


def feed_kernel(
    tok_ref, cot_ref, embed_ref, ot_ref, inv_ref, wo_ref, wi_ref, bi_ref, wb_ref, bb_ref,
    g1_ref, s1_ref, g2_ref, s2_ref,
    out_ref, dr1_ref, dot_ref, dd_ref, gout_ref, gin_ref, gback_ref, small_ref, gbi_ref,
    embed_rows, wot, wit, wbt, cols, bi_col, acc, acc_bi, n1_buf, y1_buf, slope, yl, df, da, hl, dh,
):
    eye = identity(256)
    fill_embed(embed_ref, embed_rows)
    wot[...] = transposed(eye, wo_ref[...])
    wit[...] = transposed(eye, wi_ref[...])
    wbt[...] = transposed(eye, wb_ref[...])
    for index, ref in enumerate((bb_ref, g1_ref, s1_ref, g2_ref, s2_ref)):
        cols[index] = column(eye, ref[...])
    bi_col[...] = column(eye, bi_ref[...])
    acc[...] = jnp.zeros_like(acc)
    acc_bi[...] = jnp.zeros_like(acc_bi)
    ff = wi_ref.shape[1]
    part = 512

    @pl.loop(0, WINDOWS)
    def _(window):
        here = pl.ds(pl.multiple_of(window * QUERIES, QUERIES), QUERIES)
        raw = raw_window(tok_ref, window)
        embed = embed_window(embed_rows, window).astype(BF16)
        start = jnp.concatenate(
            [
                dot_nt(eye, raw[:, half * 256 : half * 256 + 256])
                + dot_nt(eye, embed[:, half * 256 : half * 256 + 256])
                for half in range(2)
            ],
            axis=0,
        )
        n1, inv1 = norm_stats(start + dot(wot[...], ot_ref[:, here]))
        y1 = n1 * wide(cols[1]) + wide(cols[2])
        low = y1.astype(BF16)
        n1_buf[...] = n1
        y1_buf[...] = y1
        yl[:, here] = low

        @pl.loop(0, ff // part)
        def _(index):
            rows = pl.ds(pl.multiple_of(index * part, part), part)
            u = dot(wit[rows, :], low) + wide(bi_col[rows, :])
            square = u * u
            t = jnp.tanh(GELU_SCALE * u * (1.0 + GELU_CUBE * square))
            half_up = 0.5 * (1.0 + t)
            hl[rows, here] = (u * half_up).astype(BF16)
            slope[rows, :] = half_up + (0.5 * GELU_SCALE) * u * (1.0 - t * t) * (
                1.0 + 3.0 * GELU_CUBE * square
            )

        f = dot(wbt[...], hl[:, here]) + wide(cols[0])
        n2, inv2 = norm_stats(y1_buf[...] + f)
        g2 = wide(cols[3])
        result = (n2 * g2 + wide(cols[4])).astype(BF16)
        result = dot_nt(eye, result).astype(BF16)
        for half in range(2):
            at = pl.multiple_of((2 * window + half) * FLANK_COLS, FLANK_COLS)
            out_ref[:, pl.ds(at, FLANK_COLS), :] = result[half * TILE : half * TILE + TILE].reshape(
                BLOCK_ROWS, FLANK_COLS, -1
            )
        raw_cot = raw_window(cot_ref, window)
        cot = jnp.concatenate(
            [dot_nt(eye, raw_cot[:, half * 256 : half * 256 + 256]) for half in range(2)], axis=0
        )
        acc[0] += halves(cot * n2)
        acc[1] += halves(cot)
        dr2 = norm_back(n2, inv2, cot, g2)
        df_low = dr2.astype(BF16)
        acc[2] += halves(df_low.astype(F32))
        df[:, here] = df_low

        @pl.loop(0, ff // part)
        def _(index):
            rows = pl.ds(pl.multiple_of(index * part, part), part)
            dh_low = (dot(wb_ref[rows, :], df_low) * slope[rows, :]).astype(BF16)
            dh[rows, here] = dh_low
            acc_bi[rows, :] += halves(dh_low.astype(F32))

        dy1 = dr2 + dot(wi_ref[...], dh[:, here])
        n1 = n1_buf[...]
        acc[3] += halves(dy1 * n1)
        acc[4] += halves(dy1)
        dr1 = norm_back(n1, inv1, dy1, wide(cols[1]))
        dr1_ref[:, here] = dr1
        da_low = dr1.astype(BF16)
        da[:, here] = da_low
        d_o = dot(wo_ref[...], da_low)
        product = d_o * ot_ref[:, here].astype(F32)
        for head in range(8):
            rows = slice(head * HEAD_DIM, head * HEAD_DIM + HEAD_DIM)
            inverse = inv_ref[head : head + 1, here]
            dot_ref[rows, here] = (d_o[rows] * inverse).astype(BF16)
            dd_ref[head : head + 1, here] = (
                jnp.sum(product[rows], axis=0, keepdims=True) * inverse
            )

    @pl.loop(0, ff // 256)
    def _(index):
        rows = pl.ds(pl.multiple_of(index * 256, 256), 256)
        gback_ref[rows, :] = dot_nt(hl[rows, :], df[...])
        gin_ref[:, rows] = dot_nt(yl[...], dh[rows, :])

    gout_ref[...] = dot_nt(ot_ref[...], da[...])
    for index in range(5):
        small_ref[index : index + 1, :] = lane_sums(acc[index])[0:1]
    gbi_ref[...] = lane_sums(acc_bi[...])[0:1]


def back_kernel(
    has_ref, tok_ref, up_ref, embed_ref, wq_ref, wk_ref, wv_ref, xt_ref, xut_ref, qt_ref,
    e_ref, dot_ref, dd_ref, dr1_ref,
    dx_ref, dxu_ref, gq_ref, gk_ref, gv_ref,
    embed_rows, wkt, vals, vals_up, kt, kt_up, dqt, dkt, dvt, dkt_up, dvt_up, e_buf, e_sem,
):
    eye = identity(256)
    fill_embed(embed_ref, embed_rows)
    wkt[...] = transposed(eye, wk_ref[...])
    clear_pads_rows(vals)
    clear_pads_rows(vals_up)
    clear_pads_lanes(kt)
    clear_pads_lanes(kt_up)
    for ref in (dkt, dvt, dkt_up, dvt_up):
        ref[...] = jnp.zeros_like(ref)
    has_up = has_ref[0, 0].astype(F32)

    def e_copy(window, slot):
        return pltpu.make_async_copy(e_ref.at[window], e_buf.at[slot], e_sem.at[slot])

    e_copy(0, 0).start()

    @pl.loop(0, WINDOWS)
    def _(window):
        here = pl.ds(pl.multiple_of(window * QUERIES, QUERIES), QUERIES)
        padded_at = pl.multiple_of(window * QUERIES + TILE, TILE)
        low = start_window(tok_ref, embed_rows, window).astype(BF16)
        store_pairs(vals, padded_at, dot(low, wv_ref[...]).astype(BF16))
        kt[:, pl.ds(padded_at, QUERIES)] = dot(wkt[...], xt_ref[:, here]).astype(BF16)
        upper = (start_window(up_ref, embed_rows, window) * has_up).astype(BF16)
        store_pairs(vals_up, padded_at, dot(upper, wv_ref[...]).astype(BF16))
        kt_up[:, pl.ds(padded_at, QUERIES)] = dot(wkt[...], xut_ref[:, here]).astype(BF16)

    @pl.loop(0, WINDOWS)
    def _(window):
        at = pl.multiple_of(window * QUERIES, QUERIES)
        here = pl.ds(at, QUERIES)
        span = pl.ds(at, SPAN)
        slot = lax.rem(window, 2)

        @pl.when(window + 1 < WINDOWS)
        def _():
            e_copy(window + 1, 1 - slot).start()

        e_copy(window, slot).wait()

        @pl.loop(0, 4)
        def _(pair):
            feats = pl.ds(pl.multiple_of(pair * 128, 128), 128)
            do_pair = dot_ref[feats, here]
            v_low = vals[pair, span, :]
            v_up = vals_up[pair, span, :]
            for half in range(2):
                head = 2 * pair + half
                mine = pl.ds(pl.multiple_of(pair * 128 + half * HEAD_DIM, HEAD_DIM), HEAD_DIM)
                do_head = head_of_pair(do_pair, half)
                inner = dd_ref[pl.ds(head, 1), here]
                e_up = e_buf[slot, head, 0:SPAN, :]
                e_low = e_buf[slot, head, SPAN : 2 * SPAN, :]
                ds_up = (e_up.astype(F32) * (dot(v_up, do_head) - inner)).astype(BF16)
                ds_low = (e_low.astype(F32) * (dot(v_low, do_head) - inner)).astype(BF16)
                dq = dot(kt_up[mine, span], ds_up) + dot(kt[mine, span], ds_low)
                dqt[mine, here] = (dq * 0.125).astype(BF16)
                q_head = qt_ref[mine, here]
                do_mine = dot_ref[mine, here]
                dkt[mine, span] += dot_nt(q_head, ds_low)
                dkt_up[mine, span] += dot_nt(q_head, ds_up)
                dvt[mine, span] += dot_nt(do_mine, e_low)
                dvt_up[mine, span] += dot_nt(do_mine, e_up)

    inner = slice(TILE, PADDED - TILE)
    xt, xut = xt_ref[...], xut_ref[...]
    gq_ref[...] = dot_nt(xt, dqt[...])
    dk_low, dv_low = dkt[:, inner].astype(BF16), dvt[:, inner].astype(BF16)
    dk_up, dv_up = dkt_up[:, inner].astype(BF16), dvt_up[:, inner].astype(BF16)
    gk_ref[...] = dot_nt(xt, dk_low) + dot_nt(xut, dk_up)
    gv_ref[...] = dot_nt(xt, dv_low) + dot_nt(xut, dv_up)
    dxu_ref[...] = (dot(wk_ref[...], dk_up) + dot(wv_ref[...], dv_up)).astype(BF16)
    dx_ref[...] = (
        dr1_ref[...] + dot(wq_ref[...], dqt[...]) + dot(wk_ref[...], dk_low) + dot(wv_ref[...], dv_low)
    )


def finish_kernel(dx_ref, below_ref, gt_ref, ge_ref):
    eye = identity(256)
    sums = [0.0, 0.0, 0.0]
    for window in range(WINDOWS):
        here = slice(window * QUERIES, window * QUERIES + QUERIES)
        dx = dx_ref[:, here] + below_ref[:, here].astype(F32)
        for half in range(2):
            kind = (2 * window + half) % 3
            sums[kind] = sums[kind] + dx[:, half * TILE : half * TILE + TILE]
        rows = dot_nt(eye, dx.astype(BF16)).astype(BF16)
        for half in range(2):
            at = (2 * window + half) * FLANK_COLS
            gt_ref[:, at : at + FLANK_COLS, :] = rows[half * TILE : half * TILE + TILE].reshape(
                BLOCK_ROWS, FLANK_COLS, -1
            )
    lane = iota(sums[0].shape, 1) % FLANK_COLS
    for channel in range(3):
        total = 0.0
        for kind in range(3):
            total = total + jnp.where((lane + kind) % 3 == channel, sums[kind], 0.0)
        ge_ref[channel : channel + 1, :] = lane_sums(total)[0:1]


def passed_along(value, axis, steps):
    count = lax.axis_size(axis)
    leading, last = (max(0, -steps), min(count, count - steps))
    return lax.ppermute(value, axis, [(source, source + steps) for source in range(leading, last)])


def shards(
    tokens, row_place, row_width, cotangent, chan_embed, w_query, w_key, w_value, w_out, w_in,
    bias_in, w_back, bias_back, gain_first, shift_first, gain_second, shift_second,
):
    width = tokens.shape[3]
    ff = w_in.shape[1]
    tok = tokens.reshape(BLOCK_ROWS, ROW_POS, width)
    cot = cotangent.reshape(BLOCK_ROWS, ROW_POS, width)
    up = passed_along(tok, "band", 1)
    has_up = (lax.axis_index("band") > 0).astype(jnp.int32).reshape(1, 1)
    shape = jax.ShapeDtypeStruct
    params = pltpu.CompilerParams(vmem_limit_bytes=LIMIT)
    xt, xut, qt, ot, inv, e_all = pl.pallas_call(
        attend_kernel,
        name="attend_forward",
        out_shape=(
            shape((width, LEN), BF16),
            shape((width, LEN), BF16),
            shape((width, LEN), BF16),
            shape((width, LEN), BF16),
            shape((8, LEN), F32),
            shape((WINDOWS, 8, 2 * SPAN, QUERIES), BF16),
        ),
        in_specs=[smem()] * 3 + [vmem()] * 6,
        out_specs=(vmem(), vmem(), vmem(), vmem(), vmem(), hbm()),
        scratch_shapes=[
            pltpu.VMEM((ROW_POS, width), F32),
            pltpu.VMEM((width, width), BF16),
            pltpu.VMEM((width, width), BF16),
            pltpu.VMEM((4, PADDED, 128), BF16),
            pltpu.VMEM((4, PADDED, 128), BF16),
            pltpu.VMEM((width, PADDED), BF16),
            pltpu.VMEM((width, PADDED), BF16),
            pltpu.VMEM((SPAN, QUERIES), F32),
            pltpu.VMEM((SPAN, QUERIES), F32),
            pltpu.VMEM((2, 8, 2 * SPAN, QUERIES), BF16),
            pltpu.SemaphoreType.DMA((2,)),
        ],
        compiler_params=params,
    )(row_place, row_width, has_up, tok, up, chan_embed, w_query, w_key, w_value)
    row = lambda value: value.reshape(1, -1)
    layer_out, dr1, do_t, dd, g_out, g_in, g_back, small, g_bias_in = pl.pallas_call(
        feed_kernel,
        name="feed_forward_and_back",
        out_shape=(
            shape((BLOCK_ROWS, ROW_POS, width), BF16),
            shape((width, LEN), F32),
            shape((width, LEN), BF16),
            shape((8, LEN), F32),
            shape((width, width), F32),
            shape((width, ff), F32),
            shape((ff, width), F32),
            shape((5, width), F32),
            shape((1, ff), F32),
        ),
        in_specs=[vmem()] * 14,
        out_specs=(vmem(),) * 9,
        scratch_shapes=[
            pltpu.VMEM((ROW_POS, width), F32),
            pltpu.VMEM((width, width), BF16),
            pltpu.VMEM((ff, width), BF16),
            pltpu.VMEM((width, ff), BF16),
            pltpu.VMEM((5, width, 128), F32),
            pltpu.VMEM((ff, 128), F32),
            pltpu.VMEM((5, width, 128), F32),
            pltpu.VMEM((ff, 128), F32),
            pltpu.VMEM((width, QUERIES), F32),
            pltpu.VMEM((width, QUERIES), F32),
            pltpu.VMEM((ff, QUERIES), F32),
            pltpu.VMEM((width, LEN), BF16),
            pltpu.VMEM((width, LEN), BF16),
            pltpu.VMEM((width, LEN), BF16),
            pltpu.VMEM((ff, LEN), BF16),
            pltpu.VMEM((ff, LEN), BF16),
        ],
        compiler_params=params,
    )(
        tok, cot, chan_embed, ot, inv, w_out, w_in, row(bias_in), w_back, row(bias_back),
        row(gain_first), row(shift_first), row(gain_second), row(shift_second),
    )
    dx, dxu, g_query, g_key, g_value = pl.pallas_call(
        back_kernel,
        name="attend_backward",
        out_shape=(
            shape((width, LEN), F32),
            shape((width, LEN), BF16),
            shape((width, width), F32),
            shape((width, width), F32),
            shape((width, width), F32),
        ),
        in_specs=[smem()] + [vmem()] * 9 + [hbm()] + [vmem()] * 3,
        out_specs=(vmem(),) * 5,
        scratch_shapes=[
            pltpu.VMEM((ROW_POS, width), F32),
            pltpu.VMEM((width, width), BF16),
            pltpu.VMEM((4, PADDED, 128), BF16),
            pltpu.VMEM((4, PADDED, 128), BF16),
            pltpu.VMEM((width, PADDED), BF16),
            pltpu.VMEM((width, PADDED), BF16),
            pltpu.VMEM((width, LEN), BF16),
            pltpu.VMEM((width, PADDED), F32),
            pltpu.VMEM((width, PADDED), F32),
            pltpu.VMEM((width, PADDED), F32),
            pltpu.VMEM((width, PADDED), F32),
            pltpu.VMEM((2, 8, 2 * SPAN, QUERIES), BF16),
            pltpu.SemaphoreType.DMA((2,)),
        ],
        compiler_params=params,
    )(has_up, tok, up, chan_embed, w_query, w_key, w_value, xt, xut, qt, e_all, do_t, dd, dr1)
    below = passed_along(dxu, "band", -1)
    grad_tokens, g_embed = pl.pallas_call(
        finish_kernel,
        name="finish",
        out_shape=(shape((BLOCK_ROWS, ROW_POS, width), BF16), shape((3, width), F32)),
        in_specs=[vmem()] * 2,
        out_specs=(vmem(),) * 2,
        compiler_params=params,
    )(dx, below)

    def shared(grad):
        part = lax.psum_scatter(grad.astype(BF16), "band", scatter_dimension=0, tiled=True)
        return lax.psum(part.astype(F32), "grp")

    band_index = lax.axis_index("band")
    band_size = lax.axis_size("band")

    def share_of(full_sum, axis_dim):
        size = full_sum.shape[axis_dim] // band_size
        return lax.dynamic_slice_in_dim(full_sum, band_index * size, size, axis_dim)

    small_sum, bias_in_sum, embed_sum = lax.psum((small, g_bias_in, g_embed), ("band", "grp"))
    vector = lambda index: share_of(small_sum[index], 0)
    return (
        layer_out.reshape(tokens.shape),
        grad_tokens.reshape(tokens.shape),
        shared(g_query),
        shared(g_key),
        shared(g_value),
        shared(g_out),
        shared(g_in),
        share_of(bias_in_sum[0], 0),
        shared(g_back),
        vector(2),
        vector(3),
        vector(4),
        vector(0),
        vector(1),
        share_of(embed_sum, 1),
    )


def solution(mesh):
    tall = P("grp", "band", None, None)
    return jax.shard_map(
        shards,
        mesh=mesh,
        in_specs=(tall, P("grp", "band"), P("grp", "band"), tall) + (P(),) * 13,
        out_specs=(tall, tall)
        + (P("band", None),) * 5
        + (P("band"), P("band", None))
        + (P("band"),) * 5
        + (P(None, "band"),),
        check_vma=False,
    )
```

```python
import functools

import jax
import jax.numpy as jnp
from jax import lax
from jax.experimental import pallas as pl
from jax.experimental.pallas import tpu as pltpu
from jax.sharding import PartitionSpec as P

HEAD_DIM = 64
ROW_POS = 192
BLOCK_ROWS = 8
BLOCK_COLS = 32
FLANK_COLS = 16
WINDOWS = ROW_POS // BLOCK_COLS
BLOCKS = ROW_POS // FLANK_COLS
TILE = BLOCK_ROWS * FLANK_COLS
QUERIES = 2 * TILE
SPAN = 4 * TILE
LEN = BLOCK_ROWS * ROW_POS
PADDED = LEN + 2 * TILE

norm_eps = 1e-06
big_negative = -1e30
F32 = jnp.float32
BF16 = jnp.bfloat16
GELU_SCALE = 0.7978845608028654
GELU_CUBE = 0.044715


def dot(left, right):
    return jnp.dot(left, right, preferred_element_type=F32)


def dot_nt(left, right):
    return lax.dot_general(left, right, (((1,), (1,)), ((), ())), preferred_element_type=F32)


def iota(shape, dim):
    return lax.broadcasted_iota(jnp.int32, shape, dim)


def identity(size):
    return jnp.where(iota((size, size), 0) == iota((size, size), 1), 1.0, 0.0).astype(BF16)


def lanes(start, size):
    return pl.ds(pl.multiple_of(start, 128), size)


def transposed(eye, value):
    step = eye.shape[0]
    parts = [
        dot_nt(eye, value[:, at : at + step]).astype(BF16) for at in range(0, value.shape[1], step)
    ]
    return jnp.concatenate(parts, axis=0)


def column(eye, row):
    step = eye.shape[0]
    ones = jnp.ones((128, step), BF16)
    parts = [
        dot_nt(jnp.where(eye > 0, row[:, at : at + step], 0).astype(BF16), ones)
        for at in range(0, row.shape[1], step)
    ]
    return jnp.concatenate(parts, axis=0)


def wide(value):
    return jnp.concatenate([value, value], axis=1)


def halves(value):
    return value[:, :128] + value[:, 128:]


def lane_sums(value):
    ones = jnp.ones((8, 128), BF16)
    high = value.astype(BF16)
    rest = value - high.astype(F32)
    middle = rest.astype(BF16)
    low = (rest - middle.astype(F32)).astype(BF16)
    return dot_nt(ones, high) + dot_nt(ones, middle) + dot_nt(ones, low)


def fill_embed(embed_ref, rows_ref):
    embed = embed_ref[...].astype(F32)
    channel = lax.rem(iota(rows_ref.shape, 0), 3)
    rows_ref[...] = jnp.where(
        channel == 0, embed[0:1], jnp.where(channel == 1, embed[1:2], embed[2:3])
    )


def block_rows(rows_ref, block):
    return rows_ref[:, pl.ds(pl.multiple_of(block * FLANK_COLS, FLANK_COLS), FLANK_COLS), :]


def raw_window(rows_ref, window):
    parts = [block_rows(rows_ref, 2 * window + half).reshape(TILE, -1) for half in range(2)]
    return jnp.concatenate(parts, axis=0)


def embed_window(embed_rows, window):
    parts = []
    for half in range(2):
        at = pl.multiple_of((2 * window + half) * FLANK_COLS, FLANK_COLS)
        part = embed_rows[pl.ds(at, FLANK_COLS), :][None]
        parts.append(jnp.broadcast_to(part, (BLOCK_ROWS,) + part.shape[1:]).reshape(TILE, -1))
    return jnp.concatenate(parts, axis=0)


def start_window(rows_ref, embed_rows, window):
    return raw_window(rows_ref, window).astype(F32) + embed_window(embed_rows, window)


def norm_stats(value):
    center = value - jnp.mean(value, axis=0, keepdims=True)
    spread = jnp.mean(center * center, axis=0, keepdims=True)
    inverse = lax.rsqrt(spread + norm_eps)
    return center * inverse, inverse


def norm_back(normed, inverse, grad, gain):
    scaled = grad * gain
    first = jnp.mean(scaled, axis=0, keepdims=True)
    second = jnp.mean(scaled * normed, axis=0, keepdims=True)
    return (scaled - first - normed * second) * inverse


def vmem():
    return pl.BlockSpec(memory_space=pltpu.VMEM)


def smem():
    return pl.BlockSpec(memory_space=pltpu.SMEM)


def hbm():
    return pl.BlockSpec(memory_space=pl.ANY)


LIMIT = 60 * 1024 * 1024


def head_of_pair(value, half):
    keep = (iota(value.shape, 0) // HEAD_DIM) == half
    return jnp.where(keep, value, jnp.zeros_like(value))


def store_pairs(ref, at, value):
    for pair in range(value.shape[1] // 128):
        ref[pair, pl.ds(at, value.shape[0]), :] = value[:, pair * 128 : (pair + 1) * 128]


def clear_pads_rows(ref):
    pad = jnp.zeros((ref.shape[0], TILE, ref.shape[2]), ref.dtype)
    ref[:, 0:TILE, :] = pad
    ref[:, PADDED - TILE : PADDED, :] = pad


def clear_pads_lanes(ref):
    pad = jnp.zeros((ref.shape[0], TILE), ref.dtype)
    ref[:, 0:TILE] = pad
    ref[:, PADDED - TILE : PADDED] = pad


def reversed_bits(index, count):
    place, bit = 0, 1
    while bit < count:
        place = place + (index // bit) % 2 * (count // (2 * bit))
        bit *= 2
    return place


def levels(count):
    return count.bit_length() - 1


class Reduction:
    def __init__(self, buf, recv, across, send_sem, recv_sem, band, grp, size, groups):
        self.buf, self.recv, self.across = buf, recv, across
        self.send_sem, self.recv_sem = send_sem, recv_sem
        self.band, self.grp, self.size, self.groups = band, grp, size, groups
        self.levels = levels(size)

    def region(self, stage):
        start = 0
        for level in range(stage):
            start = start + (self.band // (1 << level)) % 2 * (self.size >> (level + 1))
        return start

    def copies(self, stage):
        if stage < self.levels:
            half = self.size >> (stage + 1)
            bit = (self.band // (1 << stage)) % 2
            source = self.region(stage) + (1 - bit) * half
            return [
                pltpu.make_async_remote_copy(
                    src_ref=self.buf.at[pl.ds(source, half)],
                    dst_ref=self.recv.at[pl.ds(half, half)],
                    send_sem=self.send_sem(stage),
                    recv_sem=self.recv_sem(stage),
                    device_id=(self.band + (1 << stage) * (1 - 2 * bit), self.grp),
                    device_id_type=pl.DeviceIdType.MESH,
                )
            ]
        return [
            pltpu.make_async_remote_copy(
                src_ref=self.buf.at[self.region(self.levels)],
                dst_ref=self.across.at[step],
                send_sem=self.send_sem(self.levels + step - 1),
                recv_sem=self.recv_sem(self.levels + step - 1),
                device_id=(self.band, (self.grp + step) % self.groups),
                device_id_type=pl.DeviceIdType.MESH,
            )
            for step in range(1, self.groups)
        ]

    def start(self, stage):
        for copy in self.copies(stage):
            copy.start()

    def advance(self, stage):
        for copy in self.copies(stage):
            copy.wait()
        half = self.size >> (stage + 1)
        keep = self.region(stage + 1)

        @pl.loop(0, half)
        def _(index):
            total = self.buf[keep + index].astype(F32) + self.recv[half + index].astype(F32)
            self.buf[keep + index] = total.astype(BF16)

        self.start(stage + 1)

    def finish(self):
        for copy in self.copies(self.levels):
            copy.wait()
        self.across[0] = self.buf[self.region(self.levels)]
        total = 0.0
        for member in range(self.groups):
            total = total + self.across[(self.grp + self.groups - member) % self.groups].astype(F32)
        return total


class SmallSum:
    def __init__(self, buf, recv, send_sem, recv_sem, band, grp, size, groups):
        self.buf, self.recv, self.send_sem, self.recv_sem = buf, recv, send_sem, recv_sem
        self.band, self.grp, self.size, self.groups = band, grp, size, groups
        self.levels = levels(size)

    def copies(self, stage):
        if stage < self.levels:
            bit = (self.band // (1 << stage)) % 2
            partners = [(stage, (self.band + (1 << stage) * (1 - 2 * bit), self.grp))]
        else:
            partners = [
                (self.levels + step - 1, (self.band, (self.grp + step) % self.groups))
                for step in range(1, self.groups)
            ]
        return [
            pltpu.make_async_remote_copy(
                src_ref=self.buf.at[stage],
                dst_ref=self.recv.at[slot],
                send_sem=self.send_sem.at[slot],
                recv_sem=self.recv_sem.at[slot],
                device_id=partner,
                device_id_type=pl.DeviceIdType.MESH,
            )
            for slot, partner in partners
        ]

    def start(self, stage):
        for copy in self.copies(stage):
            copy.start()

    def advance(self, stage):
        for copy in self.copies(stage):
            copy.wait()
        self.buf[stage + 1] = self.buf[stage] + self.recv[stage]
        self.start(stage + 1)

    def finish(self):
        for copy in self.copies(self.levels):
            copy.wait()
        mine = self.buf[self.levels]
        total = 0.0
        for member in range(self.groups):
            step = (self.grp + self.groups - member) % self.groups
            slot = jnp.where(step == 0, 0, self.levels + step - 1)
            total = total + jnp.where(step == 0, mine, self.recv[slot])
        return total


def attend_kernel(
    place_ref, width_ref, has_ref, tok_ref, up_ref, embed_ref, wq_ref, wk_ref, wv_ref,
    xt_ref, xut_ref, qt_ref, ot_ref, inv_ref, e_ref,
    embed_rows, wqt, wvt, keys, keys_up, vt, vt_up, bias_low, bias_up, e_buf, e_sem,
):
    eye = identity(256)
    fill_embed(embed_ref, embed_rows)
    wqt[...] = transposed(eye, wq_ref[...])
    wvt[...] = transposed(eye, wv_ref[...])
    clear_pads_rows(keys)
    clear_pads_rows(keys_up)
    clear_pads_lanes(vt)
    clear_pads_lanes(vt_up)
    has_up = has_ref[0, 0].astype(F32)
    place = place_ref[0, 0]
    width = width_ref[0, 0]

    @pl.loop(0, WINDOWS)
    def _(window):
        at = pl.multiple_of(window * QUERIES, QUERIES)
        padded_at = pl.multiple_of(window * QUERIES + TILE, TILE)
        low = start_window(tok_ref, embed_rows, window).astype(BF16)
        low_t = transposed(eye, low)
        xt_ref[:, pl.ds(at, QUERIES)] = low_t
        qt_ref[:, pl.ds(at, QUERIES)] = dot(wqt[...], low_t).astype(BF16) * BF16(0.125)
        store_pairs(keys, padded_at, dot(low, wk_ref[...]).astype(BF16))
        vt[:, pl.ds(padded_at, QUERIES)] = dot(wvt[...], low_t).astype(BF16)
        upper = (start_window(up_ref, embed_rows, window) * has_up).astype(BF16)
        upper_t = transposed(eye, upper)
        xut_ref[:, pl.ds(at, QUERIES)] = upper_t
        store_pairs(keys_up, padded_at, dot(upper, wk_ref[...]).astype(BF16))
        vt_up[:, pl.ds(padded_at, QUERIES)] = dot(wvt[...], upper_t).astype(BF16)

    def e_copy(window, slot):
        return pltpu.make_async_copy(e_buf.at[slot], e_ref.at[window], e_sem.at[slot])

    @pl.loop(0, WINDOWS)
    def _(window):
        at = pl.multiple_of(window * QUERIES, QUERIES)
        slot = lax.rem(window, 2)

        @pl.when(window >= 2)
        def _():
            e_copy(window - 2, slot).wait()

        shape = (SPAN, QUERIES)
        memory, query = iota(shape, 0), iota(shape, 1)
        memory_col = (memory // TILE) * FLANK_COLS + memory % FLANK_COLS - FLANK_COLS
        query_col = (query // TILE) * FLANK_COLS + query % FLANK_COLS
        memory_row = (memory % TILE) // FLANK_COLS
        query_row = (query % TILE) // FLANK_COLS
        column_at = memory_col + window * BLOCK_COLS
        inside = (column_at >= 0) & (column_at < width)
        earlier = (memory_row < query_row) | ((memory_row == query_row) & (memory_col <= query_col))
        itself = (memory_row == query_row) & (memory_col == query_col)
        bias_low[...] = jnp.where((inside & earlier) | itself, 0.0, big_negative)
        bias_up[...] = jnp.where(inside & (place > 0), 0.0, big_negative)

        @pl.loop(0, 4)
        def _(pair):
            feats = pl.ds(pl.multiple_of(pair * 128, 128), 128)
            q_pair = qt_ref[feats, pl.ds(at, QUERIES)]
            span = pl.ds(at, SPAN)
            k_low = keys[pair, span, :]
            k_up = keys_up[pair, span, :]
            for half in range(2):
                q_head = head_of_pair(q_pair, half)
                s_up = dot(k_up, q_head) + bias_up[...]
                s_low = dot(k_low, q_head) + bias_low[...]
                peak = jnp.maximum(
                    jnp.max(s_up, axis=0, keepdims=True), jnp.max(s_low, axis=0, keepdims=True)
                )
                r_up = jnp.exp(s_up - peak)
                r_low = jnp.exp(s_low - peak)
                total = jnp.sum(r_up, axis=0, keepdims=True) + jnp.sum(r_low, axis=0, keepdims=True)
                e_up = r_up.astype(BF16)
                e_low = r_low.astype(BF16)
                head = 2 * pair + half
                e_buf[slot, head, 0:SPAN, :] = e_up
                e_buf[slot, head, SPAN : 2 * SPAN, :] = e_low
                mine = pl.ds(pl.multiple_of(pair * 128 + half * HEAD_DIM, HEAD_DIM), HEAD_DIM)
                mixed = dot(vt_up[mine, span], e_up) + dot(vt[mine, span], e_low)
                inverse = 1.0 / total
                ot_ref[mine, pl.ds(at, QUERIES)] = (mixed * inverse).astype(BF16)
                inv_ref[pl.ds(head, 1), pl.ds(at, QUERIES)] = inverse

        e_copy(window, slot).start()

    for last in range(2):
        e_copy(WINDOWS - 2 + last, last).wait()


def feed_kernel(
    tok_ref, cot_ref, embed_ref, ot_ref, inv_ref, wo_ref, wi_ref, wb_ref, vec_ref,
    out_ref, dr1_ref, dot_ref, dd_ref, gin_ref, gbo_ref, small_ref,
    embed_rows, wot, wit, wbt, cols, bi_col, acc, acc_bi, n1_buf, y1_buf, slope, yl, df, da, hl, dh,
):
    eye = identity(256)
    fill_embed(embed_ref, embed_rows)
    wot[...] = transposed(eye, wo_ref[...])
    wit[...] = transposed(eye, wi_ref[...])
    wbt[...] = transposed(eye, wb_ref[...])
    ff = wi_ref.shape[1]
    width = wi_ref.shape[0]
    for index in range(5):
        at = ff + index * width
        cols[index] = column(eye, vec_ref[:, at : at + width])
    bi_col[...] = column(eye, vec_ref[:, 0:ff])
    acc[...] = jnp.zeros_like(acc)
    acc_bi[...] = jnp.zeros_like(acc_bi)
    part = 512

    @pl.loop(0, WINDOWS)
    def _(window):
        here = pl.ds(pl.multiple_of(window * QUERIES, QUERIES), QUERIES)
        raw = raw_window(tok_ref, window)
        embed = embed_window(embed_rows, window).astype(BF16)
        start = jnp.concatenate(
            [
                dot_nt(eye, raw[:, half * 256 : half * 256 + 256])
                + dot_nt(eye, embed[:, half * 256 : half * 256 + 256])
                for half in range(2)
            ],
            axis=0,
        )
        n1, inv1 = norm_stats(start + dot(wot[...], ot_ref[:, here]))
        y1 = n1 * wide(cols[1]) + wide(cols[2])
        low = y1.astype(BF16)
        n1_buf[...] = n1
        y1_buf[...] = y1
        yl[:, here] = low

        @pl.loop(0, ff // part)
        def _(index):
            rows = pl.ds(pl.multiple_of(index * part, part), part)
            u = dot(wit[rows, :], low) + wide(bi_col[rows, :])
            square = u * u
            t = jnp.tanh(GELU_SCALE * u * (1.0 + GELU_CUBE * square))
            half_up = 0.5 * (1.0 + t)
            hl[rows, here] = (u * half_up).astype(BF16)
            slope[rows, :] = half_up + (0.5 * GELU_SCALE) * u * (1.0 - t * t) * (
                1.0 + 3.0 * GELU_CUBE * square
            )

        f = dot(wbt[...], hl[:, here]) + wide(cols[0])
        n2, inv2 = norm_stats(y1_buf[...] + f)
        g2 = wide(cols[3])
        result = (n2 * g2 + wide(cols[4])).astype(BF16)
        result = dot_nt(eye, result).astype(BF16)
        for half in range(2):
            at = pl.multiple_of((2 * window + half) * FLANK_COLS, FLANK_COLS)
            out_ref[:, pl.ds(at, FLANK_COLS), :] = result[half * TILE : half * TILE + TILE].reshape(
                BLOCK_ROWS, FLANK_COLS, -1
            )
        raw_cot = raw_window(cot_ref, window)
        cot = jnp.concatenate(
            [dot_nt(eye, raw_cot[:, half * 256 : half * 256 + 256]) for half in range(2)], axis=0
        )
        acc[0] += halves(cot * n2)
        acc[1] += halves(cot)
        dr2 = norm_back(n2, inv2, cot, g2)
        df_low = dr2.astype(BF16)
        acc[2] += halves(df_low.astype(F32))
        df[:, here] = df_low

        @pl.loop(0, ff // part)
        def _(index):
            rows = pl.ds(pl.multiple_of(index * part, part), part)
            dh_low = (dot(wb_ref[rows, :], df_low) * slope[rows, :]).astype(BF16)
            dh[rows, here] = dh_low
            acc_bi[rows, :] += halves(dh_low.astype(F32))

        dy1 = dr2 + dot(wi_ref[...], dh[:, here])
        n1 = n1_buf[...]
        acc[3] += halves(dy1 * n1)
        acc[4] += halves(dy1)
        dr1 = norm_back(n1, inv1, dy1, wide(cols[1]))
        dr1_ref[:, here] = dr1
        da_low = dr1.astype(BF16)
        da[:, here] = da_low
        d_o = dot(wo_ref[...], da_low)
        product = d_o * ot_ref[:, here].astype(F32)
        for head in range(8):
            rows = slice(head * HEAD_DIM, head * HEAD_DIM + HEAD_DIM)
            inverse = inv_ref[head : head + 1, here]
            dot_ref[rows, here] = (d_o[rows] * inverse).astype(BF16)
            dd_ref[head : head + 1, here] = (
                jnp.sum(product[rows], axis=0, keepdims=True) * inverse
            )

    count, back_rows, share = gin_ref.shape[0], ff // gin_ref.shape[0], gin_ref.shape[1]

    @pl.loop(0, ff // 256)
    def _(index):
        rows = pl.ds(pl.multiple_of(index * 256, 256), 256)
        back = dot_nt(hl[rows, :], df[...]).astype(BF16)
        shares = 256 // back_rows
        for part in range(shares):
            gbo_ref[reversed_bits(index * shares + part, count), 0:back_rows, :] = back[
                part * back_rows : part * back_rows + back_rows
            ]
        into = dot_nt(yl[...], dh[rows, :]).astype(BF16)
        for owner in range(count):
            gin_ref[reversed_bits(owner, count), :, rows] = into[owner * share : owner * share + share]

    out = dot_nt(ot_ref[...], da[...]).astype(BF16)
    for owner in range(count):
        gbo_ref[reversed_bits(owner, count), back_rows:, :] = out[
            owner * share : owner * share + share
        ]
    small_ref[...] = jnp.zeros_like(small_ref)
    for index in range(5):
        small_ref[index : index + 1, :] = lane_sums(acc[index])[0:1]
    bias = lane_sums(acc_bi[...])[0:1]
    for index in range(ff // width):
        small_ref[5 + index : 6 + index, :] = bias[:, index * width : (index + 1) * width]


def back_kernel(
    tok_ref, embed_ref, wq_ref, wk_ref, wv_ref, xt_ref, xut_ref, qt_ref, dot_ref, dd_ref, dr1_ref,
    small_in, e_ref, gin_hbm, gbo_hbm,
    gt_ref, qkv_ref, gin_ref, gbo_ref, small_ref,
    wkt, vals, vals_up, kt, kt_up, dq_up, dqt, dkt, dvt, dkt_up, dvt_up, dk_acc, dv_acc,
    dxu, below, e_buf, e_sem, load_sem,
    gin_buf, gin_recv, gin_across, gbo_buf, gbo_recv, gbo_across, qkv_buf, qkv_recv, qkv_across,
    small_buf, small_recv,
    in_ss, in_rs, bo_ss, bo_rs, qkv_ss, qkv_rs, small_ss, small_rs, halo_ss, halo_rs,
    *, size, groups,
):
    band, grp = lax.axis_index("band"), lax.axis_index("grp")
    depth = levels(size)
    MESH = pl.DeviceIdType.MESH
    barrier = pltpu.get_barrier_semaphore()
    for level in range(depth):
        bit = (band // (1 << level)) % 2
        pl.semaphore_signal(
            barrier, inc=1, device_id=(band + (1 << level) * (1 - 2 * bit), grp), device_id_type=MESH
        )
    for step in range(1, groups):
        pl.semaphore_signal(
            barrier, inc=1, device_id=(band, (grp + step) % groups), device_id_type=MESH
        )

    @pl.when((band % 2 == 1) & (band < size - 1))
    def _():
        pl.semaphore_signal(barrier, inc=1, device_id=(band + 1, grp), device_id_type=MESH)

    load_in = pltpu.make_async_copy(gin_hbm, gin_buf, load_sem.at[0])
    load_bo = pltpu.make_async_copy(gbo_hbm, gbo_buf, load_sem.at[1])
    load_bo.start()
    load_in.start()
    above = jnp.where((band % 2 == 0) & (band > 0), 1, 0)
    pl.semaphore_wait(barrier, depth + groups - 1 + above)

    def reduction(buf, recv, across, ss, rs):
        return Reduction(buf, recv, across, ss, rs, band, grp, size, groups)

    sum_in = reduction(gin_buf, gin_recv, gin_across, lambda k: in_ss.at[k], lambda k: in_rs.at[k])
    sum_bo = reduction(gbo_buf, gbo_recv, gbo_across, lambda k: bo_ss.at[k], lambda k: bo_rs.at[k])

    def sum_qkv(pair):
        return reduction(
            qkv_buf.at[pair], qkv_recv.at[pair], qkv_across.at[pair],
            lambda k: qkv_ss.at[pair, k], lambda k: qkv_rs.at[pair, k],
        )

    sum_small = SmallSum(
        small_buf, small_recv, small_ss, small_rs, band, grp, size, groups
    )
    halo = pltpu.make_async_remote_copy(
        src_ref=dxu, dst_ref=below, send_sem=halo_ss, recv_sem=halo_rs,
        device_id=(jnp.maximum(band - 1, 0), grp), device_id_type=MESH,
    )

    def e_copy(step, slot, part):
        pair, window = step // WINDOWS, step % WINDOWS
        return pltpu.make_async_copy(
            e_ref.at[window, pl.ds(2 * pair, 2), pl.ds(part * SPAN, SPAN)],
            e_buf.at[slot],
            e_sem.at[slot],
        )

    slots = e_buf.shape[0]
    steps = 4 * WINDOWS
    for step in range(slots - 1):
        e_copy(step, step, 0).start()

    eye = identity(256)
    wkt[...] = transposed(eye, wk_ref[...])
    clear_pads_rows(vals)
    clear_pads_rows(vals_up)
    clear_pads_lanes(kt)
    clear_pads_lanes(kt_up)
    load_bo.wait()
    sum_bo.start(0)

    @pl.loop(0, WINDOWS)
    def _(window):
        here = pl.ds(pl.multiple_of(window * QUERIES, QUERIES), QUERIES)
        padded_at = pl.multiple_of(window * QUERIES + TILE, TILE)
        low = transposed(eye, xt_ref[:, here])
        store_pairs(vals, padded_at, dot(low, wv_ref[...]).astype(BF16))
        kt[:, pl.ds(padded_at, QUERIES)] = dot(wkt[...], xt_ref[:, here]).astype(BF16)
        upper = transposed(eye, xut_ref[:, here])
        store_pairs(vals_up, padded_at, dot(upper, wv_ref[...]).astype(BF16))
        kt_up[:, pl.ds(padded_at, QUERIES)] = dot(wkt[...], xut_ref[:, here]).astype(BF16)

    load_in.wait()
    sum_in.start(0)

    def half_step(step, part, v_rows, k_cols):
        pair, window = step // WINDOWS, step % WINDOWS
        at = pl.multiple_of(window * QUERIES, QUERIES)
        here, span = pl.ds(at, QUERIES), pl.ds(at, SPAN)
        slot = step % slots
        ahead = step + slots - 1

        @pl.when(ahead < steps)
        def _():
            e_copy(ahead, ahead % slots, part).start()

        @pl.when(window == 0)
        def _():
            dk_acc[...] = jnp.zeros_like(dk_acc)
            dv_acc[...] = jnp.zeros_like(dv_acc)

        e_copy(step, slot, part).wait()
        feats = pl.ds(pl.multiple_of(pair * 128, 128), 128)
        do_pair = dot_ref[feats, here]
        values = v_rows[pair, span, :]
        for half in range(2):
            head = 2 * pair + half
            mine = pl.ds(pl.multiple_of(pair * 128 + half * HEAD_DIM, HEAD_DIM), HEAD_DIM)
            rows = pl.ds(half * HEAD_DIM, HEAD_DIM)
            inner = dd_ref[pl.ds(head, 1), here]
            e = e_buf[slot, half]
            ds = (e.astype(F32) * (dot(values, head_of_pair(do_pair, half)) - inner)).astype(BF16)
            dq = dot(k_cols[mine, span], ds)
            if part == 0:
                dq_up[mine, here] = dq
            else:
                dqt[mine, here] = ((dq + dq_up[mine, here]) * 0.125).astype(BF16)
            dk_acc[rows, span] += dot_nt(qt_ref[mine, here], ds)
            dv_acc[rows, span] += dot_nt(dot_ref[mine, here], e)

    @pl.loop(0, steps)
    def _(step):
        half_step(step, 0, vals_up, kt_up)

        @pl.when(step % WINDOWS == WINDOWS - 1)
        def _():
            feats = pl.ds(pl.multiple_of(step // WINDOWS * 128, 128), 128)
            dkt_up[feats, :] = dk_acc[:, TILE : PADDED - TILE].astype(BF16)
            dvt_up[feats, :] = dv_acc[:, TILE : PADDED - TILE].astype(BF16)

        @pl.when(step == 1)
        def _():
            sum_bo.advance(0)
            sum_in.advance(0)

        @pl.when(step == 14)
        def _():
            sum_bo.advance(1)

        @pl.when(step == 23)
        def _():
            sum_bo.advance(2)

    for step in range(slots - 1):
        e_copy(step, step, 1).start()

    dxu[...] = (dot(wk_ref[...], dkt_up[...]) + dot(wv_ref[...], dvt_up[...])).astype(BF16)

    @pl.when(band > 0)
    def _():
        halo.start()

    @pl.loop(0, steps)
    def _(step):
        half_step(step, 1, vals, kt)
        pair, window = step // WINDOWS, step % WINDOWS

        for stage in range(depth):

            @pl.when((pair > 0) & (window == stage + 5 - depth))
            def _(stage=stage):
                sum_qkv(pair - 1).advance(stage)

        @pl.when((pair > 0) & (window == 5))
        def _():
            qkv_ref[pair - 1] = sum_qkv(pair - 1).finish()

        @pl.when(window == WINDOWS - 1)
        def _():
            feats = pl.ds(pl.multiple_of(pair * 128, 128), 128)
            dkt[feats, :] = dk_acc[:, TILE : PADDED - TILE].astype(BF16)
            dvt[feats, :] = dv_acc[:, TILE : PADDED - TILE].astype(BF16)
            xt, xut = xt_ref[...], xut_ref[...]
            grads = (
                dot_nt(xt, dqt[feats, :]),
                dot_nt(xt, dkt[feats, :]) + dot_nt(xut, dkt_up[feats, :]),
                dot_nt(xt, dvt[feats, :]) + dot_nt(xut, dvt_up[feats, :]),
            )
            share = qkv_buf.shape[2]
            for index, grad in enumerate(grads):
                low = grad.astype(BF16)
                for owner in range(size):
                    qkv_buf[pair, reversed_bits(owner, size), :, index * 128 : index * 128 + 128] = (
                        low[owner * share : owner * share + share]
                    )
            sum_qkv(pair).start(0)

        @pl.when(step == 2)
        def _():
            sum_in.advance(1)

        @pl.when(step == 5)
        def _():
            sum_bo.advance(3)

        @pl.when(step == 9)
        def _():
            sum_in.advance(2)

        @pl.when(step == 10)
        def _():
            gbo_ref[...] = sum_bo.finish()

        @pl.when(step == 15)
        def _():
            sum_in.advance(3)

        @pl.when(step == 20)
        def _():
            gin_ref[...] = sum_in.finish()

    shape = (16, LEN)
    channel = (iota(shape, 1) // TILE + iota(shape, 1) % FLANK_COLS) % 3
    chosen = jnp.where(channel + 9 == iota(shape, 0), 1.0, 0.0).astype(BF16)

    def split(value):
        high = value.astype(BF16)
        return high, (value - high.astype(F32)).astype(BF16)

    sums = jnp.zeros((16, dr1_ref.shape[0]), F32)
    for piece in split(dr1_ref[...]):
        sums += dot_nt(chosen, piece)
    for grads, weight in ((dqt, wq_ref), (dkt, wk_ref), (dvt, wv_ref)):
        for piece in split(dot_nt(chosen, grads[...])):
            sums += dot_nt(piece, weight[...])
    sums += dot_nt(chosen, dxu[...]) * jnp.where(band > 0, 1.0, 0.0)
    small_buf[0] = small_in[...] + sums
    sum_small.start(0)

    @pl.when(band < size - 1)
    def _():
        halo.wait_recv()

    @pl.when(band > 0)
    def _():
        halo.wait_send()

    @pl.when(band == size - 1)
    def _():
        below[...] = jnp.zeros_like(below)

    @pl.loop(0, WINDOWS)
    def _(window):
        here = pl.ds(pl.multiple_of(window * QUERIES, QUERIES), QUERIES)
        dx = (
            dr1_ref[:, here]
            + dot(wq_ref[...], dqt[:, here])
            + dot(wk_ref[...], dkt[:, here])
            + dot(wv_ref[...], dvt[:, here])
            + below[:, here].astype(F32)
        )
        rows = dot_nt(eye, dx.astype(BF16)).astype(BF16)
        for half in range(2):
            at = pl.multiple_of((2 * window + half) * FLANK_COLS, FLANK_COLS)
            gt_ref[:, pl.ds(at, FLANK_COLS), :] = rows[half * TILE : half * TILE + TILE].reshape(
                BLOCK_ROWS, FLANK_COLS, -1
            )

        for stage in range(depth):

            @pl.when(window == stage + 5 - depth)
            def _(stage=stage):
                sum_qkv(3).advance(stage)
                sum_small.advance(stage)

        @pl.when(window == 5)
        def _():
            qkv_ref[3] = sum_qkv(3).finish()
            small_ref[...] = sum_small.finish()


def passed_along(value, axis, steps):
    count = lax.axis_size(axis)
    leading, last = (max(0, -steps), min(count, count - steps))
    return lax.ppermute(value, axis, [(source, source + steps) for source in range(leading, last)])


def shards(
    tokens, row_place, row_width, cotangent, chan_embed, w_query, w_key, w_value, w_out, w_in,
    bias_in, w_back, bias_back, gain_first, shift_first, gain_second, shift_second,
):
    width = tokens.shape[3]
    ff = w_in.shape[1]
    tok = tokens.reshape(BLOCK_ROWS, ROW_POS, width)
    cot = cotangent.reshape(BLOCK_ROWS, ROW_POS, width)
    up = passed_along(tok, "band", 1)
    has_up = (lax.axis_index("band") > 0).astype(jnp.int32).reshape(1, 1)
    shape = jax.ShapeDtypeStruct
    params = pltpu.CompilerParams(vmem_limit_bytes=LIMIT)
    xt, xut, qt, ot, inv, e_all = pl.pallas_call(
        attend_kernel,
        name="attend_forward",
        out_shape=(
            shape((width, LEN), BF16),
            shape((width, LEN), BF16),
            shape((width, LEN), BF16),
            shape((width, LEN), BF16),
            shape((8, LEN), F32),
            shape((WINDOWS, 8, 2 * SPAN, QUERIES), BF16),
        ),
        in_specs=[smem()] * 3 + [vmem()] * 6,
        out_specs=(vmem(), vmem(), vmem(), vmem(), vmem(), hbm()),
        scratch_shapes=[
            pltpu.VMEM((ROW_POS, width), F32),
            pltpu.VMEM((width, width), BF16),
            pltpu.VMEM((width, width), BF16),
            pltpu.VMEM((4, PADDED, 128), BF16),
            pltpu.VMEM((4, PADDED, 128), BF16),
            pltpu.VMEM((width, PADDED), BF16),
            pltpu.VMEM((width, PADDED), BF16),
            pltpu.VMEM((SPAN, QUERIES), F32),
            pltpu.VMEM((SPAN, QUERIES), F32),
            pltpu.VMEM((2, 8, 2 * SPAN, QUERIES), BF16),
            pltpu.SemaphoreType.DMA((2,)),
        ],
        compiler_params=params,
    )(row_place, row_width, has_up, tok, up, chan_embed, w_query, w_key, w_value)
    size, groups = lax.axis_size("band"), lax.axis_size("grp")
    share, back_share = width // size, ff // size
    vectors = jnp.concatenate(
        [bias_in, bias_back, gain_first, shift_first, gain_second, shift_second]
    ).reshape(1, -1)
    layer_out, dr1, do_t, dd, g_in, g_bo, small = pl.pallas_call(
        feed_kernel,
        name="feed_forward_and_back",
        out_shape=(
            shape((BLOCK_ROWS, ROW_POS, width), BF16),
            shape((width, LEN), F32),
            shape((width, LEN), BF16),
            shape((8, LEN), F32),
            shape((size, share, ff), BF16),
            shape((size, back_share + share, width), BF16),
            shape((16, width), F32),
        ),
        in_specs=[vmem()] * 9,
        out_specs=(vmem(),) * 7,
        scratch_shapes=[
            pltpu.VMEM((ROW_POS, width), F32),
            pltpu.VMEM((width, width), BF16),
            pltpu.VMEM((ff, width), BF16),
            pltpu.VMEM((width, ff), BF16),
            pltpu.VMEM((5, width, 128), F32),
            pltpu.VMEM((ff, 128), F32),
            pltpu.VMEM((5, width, 128), F32),
            pltpu.VMEM((ff, 128), F32),
            pltpu.VMEM((width, QUERIES), F32),
            pltpu.VMEM((width, QUERIES), F32),
            pltpu.VMEM((ff, QUERIES), F32),
            pltpu.VMEM((width, LEN), BF16),
            pltpu.VMEM((width, LEN), BF16),
            pltpu.VMEM((width, LEN), BF16),
            pltpu.VMEM((ff, LEN), BF16),
            pltpu.VMEM((ff, LEN), BF16),
        ],
        compiler_params=params,
    )(tok, cot, chan_embed, ot, inv, w_out, w_in, w_back, vectors)
    dma = pltpu.SemaphoreType.DMA
    stages = levels(size) + groups - 1
    grad_tokens, g_qkv, g_in, g_bo, small = pl.pallas_call(
        functools.partial(back_kernel, size=size, groups=groups),
        name="attend_backward",
        out_shape=(
            shape((BLOCK_ROWS, ROW_POS, width), BF16),
            shape((4, share, 384), F32),
            shape((share, ff), F32),
            shape((back_share + share, width), F32),
            shape((16, width), F32),
        ),
        in_specs=[vmem()] * 12 + [hbm()] * 3,
        out_specs=(vmem(),) * 5,
        scratch_shapes=[
            pltpu.VMEM((width, width), BF16),
            pltpu.VMEM((4, PADDED, 128), BF16),
            pltpu.VMEM((4, PADDED, 128), BF16),
            pltpu.VMEM((width, PADDED), BF16),
            pltpu.VMEM((width, PADDED), BF16),
            pltpu.VMEM((width, LEN), F32),
            pltpu.VMEM((width, LEN), BF16),
            pltpu.VMEM((width, LEN), BF16),
            pltpu.VMEM((width, LEN), BF16),
            pltpu.VMEM((width, LEN), BF16),
            pltpu.VMEM((width, LEN), BF16),
            pltpu.VMEM((128, PADDED), F32),
            pltpu.VMEM((128, PADDED), F32),
            pltpu.VMEM((width, LEN), BF16),
            pltpu.VMEM((width, LEN), BF16),
            pltpu.VMEM((4, 2, SPAN, QUERIES), BF16),
            dma((4,)),
            dma((2,)),
            pltpu.VMEM((size, share, ff), BF16),
            pltpu.VMEM((size, share, ff), BF16),
            pltpu.VMEM((groups, share, ff), BF16),
            pltpu.VMEM((size, back_share + share, width), BF16),
            pltpu.VMEM((size, back_share + share, width), BF16),
            pltpu.VMEM((groups, back_share + share, width), BF16),
            pltpu.VMEM((4, size, share, 384), BF16),
            pltpu.VMEM((4, size, share, 384), BF16),
            pltpu.VMEM((4, groups, share, 384), BF16),
            pltpu.VMEM((levels(size) + 1, 16, width), F32),
            pltpu.VMEM((stages, 16, width), F32),
            dma((stages,)),
            dma((stages,)),
            dma((stages,)),
            dma((stages,)),
            dma((4, stages)),
            dma((4, stages)),
            dma((stages,)),
            dma((stages,)),
            dma,
            dma,
        ],
        compiler_params=pltpu.CompilerParams(
            vmem_limit_bytes=LIMIT, collective_id=0, has_side_effects=True
        ),
    )(
        tok, chan_embed, w_query, w_key, w_value, xt, xut, qt, do_t, dd, dr1, small, e_all, g_in, g_bo,
    )
    band = lax.axis_index("band")
    qkv = g_qkv.reshape(4, share, 3, 128).transpose(2, 1, 0, 3).reshape(3, share, width)
    mine = lax.dynamic_slice_in_dim(small, band * share, share, 1)
    bias_in_sum = lax.dynamic_slice_in_dim(
        small[5 : 5 + ff // width].reshape(ff), band * back_share, back_share, 0
    )
    return (
        layer_out.reshape(tokens.shape),
        grad_tokens.reshape(tokens.shape),
        qkv[0],
        qkv[1],
        qkv[2],
        g_bo[back_share:],
        g_in,
        bias_in_sum,
        g_bo[:back_share],
        mine[2],
        mine[3],
        mine[4],
        mine[0],
        mine[1],
        mine[9:12],
    )


def solution(mesh):
    tall = P("grp", "band", None, None)
    return jax.shard_map(
        shards,
        mesh=mesh,
        in_specs=(tall, P("grp", "band"), P("grp", "band"), tall) + (P(),) * 13,
        out_specs=(tall, tall)
        + (P("band", None),) * 5
        + (P("band"), P("band", None))
        + (P("band"),) * 5
        + (P(None, "band"),),
        check_vma=False,
    )
```

```python
import functools

import jax
import jax.numpy as jnp
from jax import lax
from jax.experimental import pallas as pl
from jax.experimental.pallas import tpu as pltpu
from jax.sharding import PartitionSpec as P

HEAD_DIM = 64
ROW_POS = 192
BLOCK_ROWS = 8
BLOCK_COLS = 32
FLANK_COLS = 16
WINDOWS = ROW_POS // BLOCK_COLS
BLOCKS = ROW_POS // FLANK_COLS
TILE = BLOCK_ROWS * FLANK_COLS
QUERIES = 2 * TILE
SPAN = 4 * TILE
LEN = BLOCK_ROWS * ROW_POS
PADDED = LEN + 2 * TILE

norm_eps = 1e-06
big_negative = -1e30
F32 = jnp.float32
BF16 = jnp.bfloat16
LOG2_E = 1.4426950408889634
GELU_SCALE = 0.7978845608028654
GELU_CUBE = 0.044715


def dot(left, right):
    return jnp.dot(left, right, preferred_element_type=F32)


def dot_nt(left, right):
    return lax.dot_general(left, right, (((1,), (1,)), ((), ())), preferred_element_type=F32)


def iota(shape, dim):
    return lax.broadcasted_iota(jnp.int32, shape, dim)


def identity(size):
    return jnp.where(iota((size, size), 0) == iota((size, size), 1), 1.0, 0.0).astype(BF16)


def lanes(start, size):
    return pl.ds(pl.multiple_of(start, 128), size)


def transposed(eye, value):
    step = eye.shape[0]
    parts = [
        dot_nt(eye, value[:, at : at + step]).astype(BF16) for at in range(0, value.shape[1], step)
    ]
    return jnp.concatenate(parts, axis=0)


def column(eye, row):
    step = eye.shape[0]
    ones = jnp.ones((128, step), BF16)
    parts = [
        dot_nt(jnp.where(eye > 0, row[:, at : at + step], 0).astype(BF16), ones)
        for at in range(0, row.shape[1], step)
    ]
    return jnp.concatenate(parts, axis=0)


def wide(value):
    return jnp.concatenate([value, value], axis=1)


def halves(value):
    return value[:, :128] + value[:, 128:]


def lane_sums(value):
    ones = jnp.ones((8, 128), BF16)
    high = value.astype(BF16)
    rest = value - high.astype(F32)
    middle = rest.astype(BF16)
    low = (rest - middle.astype(F32)).astype(BF16)
    return dot_nt(ones, high) + dot_nt(ones, middle) + dot_nt(ones, low)


def fill_embed(embed_ref, rows_ref):
    embed = embed_ref[...].astype(F32)
    channel = lax.rem(iota(rows_ref.shape, 0), 3)
    rows_ref[...] = jnp.where(
        channel == 0, embed[0:1], jnp.where(channel == 1, embed[1:2], embed[2:3])
    )


def block_rows(rows_ref, block):
    return rows_ref[:, pl.ds(pl.multiple_of(block * FLANK_COLS, FLANK_COLS), FLANK_COLS), :]


def raw_window(rows_ref, window):
    parts = [block_rows(rows_ref, 2 * window + half).reshape(TILE, -1) for half in range(2)]
    return jnp.concatenate(parts, axis=0)


def embed_window(embed_rows, window):
    parts = []
    for half in range(2):
        at = pl.multiple_of((2 * window + half) * FLANK_COLS, FLANK_COLS)
        part = embed_rows[pl.ds(at, FLANK_COLS), :][None]
        parts.append(jnp.broadcast_to(part, (BLOCK_ROWS,) + part.shape[1:]).reshape(TILE, -1))
    return jnp.concatenate(parts, axis=0)


def start_window(rows_ref, embed_rows, window):
    return raw_window(rows_ref, window).astype(F32) + embed_window(embed_rows, window)


def norm_stats(value):
    center = value - jnp.mean(value, axis=0, keepdims=True)
    spread = jnp.mean(center * center, axis=0, keepdims=True)
    inverse = lax.rsqrt(spread + norm_eps)
    return center * inverse, inverse


def norm_back(normed, inverse, grad, gain):
    scaled = grad * gain
    first = jnp.mean(scaled, axis=0, keepdims=True)
    second = jnp.mean(scaled * normed, axis=0, keepdims=True)
    return (scaled - first - normed * second) * inverse


def vmem():
    return pl.BlockSpec(memory_space=pltpu.VMEM)


def smem():
    return pl.BlockSpec(memory_space=pltpu.SMEM)


def hbm():
    return pl.BlockSpec(memory_space=pl.ANY)


LIMIT = 60 * 1024 * 1024


def head_of_pair(value, half):
    keep = (iota(value.shape, 0) // HEAD_DIM) == half
    return jnp.where(keep, value, jnp.zeros_like(value))


def store_pairs(ref, at, value):
    for pair in range(value.shape[1] // 128):
        ref[pair, pl.ds(at, value.shape[0]), :] = value[:, pair * 128 : (pair + 1) * 128]


def clear_pads_rows(ref):
    pad = jnp.zeros((ref.shape[0], TILE, ref.shape[2]), ref.dtype)
    ref[:, 0:TILE, :] = pad
    ref[:, PADDED - TILE : PADDED, :] = pad


def clear_pads_lanes(ref):
    pad = jnp.zeros((ref.shape[0], TILE), ref.dtype)
    ref[:, 0:TILE] = pad
    ref[:, PADDED - TILE : PADDED] = pad


def reversed_bits(index, count):
    place, bit = 0, 1
    while bit < count:
        place = place + (index // bit) % 2 * (count // (2 * bit))
        bit *= 2
    return place


def levels(count):
    return count.bit_length() - 1


class Reduction:
    def __init__(self, buf, recv, across, gathered, send_sem, recv_sem, band, grp, size, groups):
        self.buf, self.recv, self.across, self.gathered = buf, recv, across, gathered
        self.send_sem, self.recv_sem = send_sem, recv_sem
        self.band, self.grp, self.size, self.groups = band, grp, size, groups
        depth = levels(size)
        bits = [("bit", level) for level in range(depth)]
        if gathered is None:
            self.stages = bits + [("sum", depth)]
        else:
            self.stages = bits[:1] + [("split", 1)] + bits[1:] + [("gather", depth)]
        self.depth = depth
        self.part = buf.shape[2] // groups

    def start_of(self, bits):
        start = 0
        for level in range(bits):
            start = start + (self.band // (1 << level)) % 2 * (self.size >> (level + 1))
        return start

    def columns_of(self, member):
        return pl.ds(pl.multiple_of(member * self.part, 128), self.part)

    def columns(self, stage):
        split = [kind for kind, _ in self.stages[:stage]].count("split")
        return self.columns_of(self.grp) if split else slice(None)

    def view(self, ref, first, count, columns):
        rows = pl.ds(first, count)
        return ref.at[rows] if columns == slice(None) else ref.at[rows, :, columns]

    def copies(self, stage):
        kind, bits = self.stages[stage]
        columns = self.columns(stage)
        pieces = []
        if kind == "bit":
            half = self.size >> (bits + 1)
            bit = (self.band // (1 << bits)) % 2
            pieces.append(
                (
                    self.view(self.buf, self.start_of(bits) + (1 - bit) * half, half, columns),
                    self.view(self.recv, half, half, columns),
                    bits,
                    (self.band + (1 << bits) * (1 - 2 * bit), self.grp),
                )
            )
        for step in range(1, self.groups):
            partner = (self.grp + step) % self.groups
            place = (self.band, partner)
            if kind == "sum":
                source, target = self.buf.at[self.start_of(bits)], self.across.at[step]
                pieces.append((source, target, self.depth + step - 1, place))
            if kind == "split":
                source = self.view(
                    self.buf, self.start_of(bits), self.size >> bits, self.columns_of(partner)
                )
                pieces.append((source, self.across.at[step - 1], self.depth + step - 1, place))
            if kind == "gather":
                source, target = self.gathered.at[0], self.gathered.at[step]
                pieces.append((source, target, self.depth + self.groups + step - 2, place))
        return [
            pltpu.make_async_remote_copy(
                src_ref=source,
                dst_ref=target,
                send_sem=self.send_sem(sem),
                recv_sem=self.recv_sem(sem),
                device_id=place,
                device_id_type=pl.DeviceIdType.MESH,
            )
            for source, target, sem, place in pieces
        ]

    def start(self, stage):
        for copy in self.copies(stage):
            copy.start()

    def advance(self, stage):
        for copy in self.copies(stage):
            copy.wait()
        kind, bits = self.stages[stage]
        if kind == "bit":
            columns = self.columns(stage)
            half, keep = self.size >> (bits + 1), self.start_of(bits + 1)

            @pl.loop(0, half)
            def _(index):
                total = self.buf[keep + index, :, columns].astype(F32)
                total = total + self.recv[half + index, :, columns].astype(F32)
                self.buf[keep + index, :, columns] = total.astype(BF16)
        else:
            columns = self.columns_of(self.grp)
            keep = self.start_of(bits)

            @pl.loop(0, self.size >> bits)
            def _(index):
                total = self.buf[keep + index, :, columns].astype(F32)
                for step in range(self.groups - 1):
                    total = total + self.across[step, index].astype(F32)
                self.buf[keep + index, :, columns] = total.astype(BF16)

        if self.stages[stage + 1][0] == "gather":
            self.gathered[0] = self.buf[self.start_of(self.depth), :, self.columns_of(self.grp)].astype(
                F32
            )
        self.start(stage + 1)

    def finish(self, out):
        last = len(self.stages) - 1
        for copy in self.copies(last):
            copy.wait()
        if self.stages[last][0] == "sum":
            self.across[0] = self.buf[self.start_of(self.depth)]
            total = 0.0
            for member in range(self.groups):
                step = (self.grp + self.groups - member) % self.groups
                total = total + self.across[step].astype(F32)
            out(total)
        else:
            for step in range(self.groups):
                member = (self.grp + self.groups - step) % self.groups
                out(self.gathered[step], self.columns_of(member))


class SmallSum:
    def __init__(self, buf, recv, send_sem, recv_sem, band, grp, size, groups):
        self.buf, self.recv, self.send_sem, self.recv_sem = buf, recv, send_sem, recv_sem
        self.band, self.grp, self.size, self.groups = band, grp, size, groups
        self.levels = levels(size)

    def copies(self, stage):
        if stage < self.levels:
            bit = (self.band // (1 << stage)) % 2
            partners = [(stage, (self.band + (1 << stage) * (1 - 2 * bit), self.grp))]
        else:
            partners = [
                (self.levels + step - 1, (self.band, (self.grp + step) % self.groups))
                for step in range(1, self.groups)
            ]
        return [
            pltpu.make_async_remote_copy(
                src_ref=self.buf.at[stage],
                dst_ref=self.recv.at[slot],
                send_sem=self.send_sem.at[slot],
                recv_sem=self.recv_sem.at[slot],
                device_id=partner,
                device_id_type=pl.DeviceIdType.MESH,
            )
            for slot, partner in partners
        ]

    def start(self, stage):
        for copy in self.copies(stage):
            copy.start()

    def advance(self, stage):
        for copy in self.copies(stage):
            copy.wait()
        self.buf[stage + 1] = self.buf[stage] + self.recv[stage]
        self.start(stage + 1)

    def finish(self):
        for copy in self.copies(self.levels):
            copy.wait()
        mine = self.buf[self.levels]
        total = 0.0
        for member in range(self.groups):
            step = (self.grp + self.groups - member) % self.groups
            slot = jnp.where(step == 0, 0, self.levels + step - 1)
            total = total + jnp.where(step == 0, mine, self.recv[slot])
        return total


def attend_kernel(
    place_ref, width_ref, tok_ref, embed_ref, wq_ref, wk_ref, wv_ref,
    xt_ref, xut_ref, qt_ref, ot_ref, inv_ref, e_ref,
    embed_rows, up, wqt, wvt, qs, keys, keys_up, vt, vt_up, bias_low, bias_up, ones_row,
    e_buf, e_sem, up_ss, up_rs,
    *, size,
):
    band, grp = lax.axis_index("band"), lax.axis_index("grp")
    barrier = pltpu.get_barrier_semaphore()

    @pl.when(band > 0)
    def _():
        pl.semaphore_signal(
            barrier, inc=1, device_id=(band - 1, grp), device_id_type=pl.DeviceIdType.MESH
        )

    def up_copy(window):
        cols = pl.ds(pl.multiple_of(window * BLOCK_COLS, BLOCK_COLS), BLOCK_COLS)
        return pltpu.make_async_remote_copy(
            src_ref=tok_ref.at[:, cols, :],
            dst_ref=up.at[:, cols, :],
            send_sem=up_ss.at[window],
            recv_sem=up_rs.at[window],
            device_id=(jnp.minimum(band + 1, size - 1), grp),
            device_id_type=pl.DeviceIdType.MESH,
        )

    @pl.when(band < size - 1)
    def _():
        pl.semaphore_wait(barrier, 1)
        for window in range(WINDOWS):
            up_copy(window).start()

    @pl.when(band == 0)
    def _():
        up[...] = jnp.zeros_like(up)

    eye = identity(256)
    fill_embed(embed_ref, embed_rows)
    wqt[...] = transposed(eye, wq_ref[...])
    wvt[...] = transposed(eye, wv_ref[...])
    clear_pads_rows(keys)
    clear_pads_rows(keys_up)
    vt[...] = jnp.zeros_like(vt)
    vt_up[...] = jnp.zeros_like(vt_up)
    sums = jnp.where(iota((16, PADDED), 0) == 0, 1.0, 0.0).astype(BF16)
    for head in range(8):
        vt[head, HEAD_DIM:, :] = sums
        vt_up[head, HEAD_DIM:, :] = sums
    ones_row[...] = jnp.where(iota(ones_row.shape, 0) == 0, 1.0, 0.0).astype(BF16)
    has_up = jnp.where(band > 0, 1.0, 0.0)
    def store_heads(ref, at, value):
        for head in range(8):
            ref[head, 0:HEAD_DIM, pl.ds(at, QUERIES)] = value[
                head * HEAD_DIM : head * HEAD_DIM + HEAD_DIM
            ]

    @pl.loop(0, WINDOWS)
    def _(window):
        at = pl.multiple_of(window * QUERIES, QUERIES)
        padded_at = pl.multiple_of(window * QUERIES + TILE, TILE)
        low = start_window(tok_ref, embed_rows, window).astype(BF16)
        low_t = transposed(eye, low)
        xt_ref[:, pl.ds(at, QUERIES)] = low_t
        q_low = dot(wqt[...], low_t).astype(BF16)
        qt_ref[:, pl.ds(at, QUERIES)] = q_low * BF16(0.125)
        qs[:, pl.ds(at, QUERIES)] = (q_low.astype(F32) * (0.125 * LOG2_E)).astype(BF16)
        store_pairs(keys, padded_at, dot(low, wk_ref[...]).astype(BF16))
        store_heads(vt, padded_at, dot(wvt[...], low_t).astype(BF16))

    def prepare_upper(window):
        @pl.when(band > 0)
        def _():
            up_copy(window).wait_recv()

        at = pl.multiple_of(window * QUERIES, QUERIES)
        padded_at = pl.multiple_of(window * QUERIES + TILE, TILE)
        upper = (start_window(up, embed_rows, window) * has_up).astype(BF16)
        upper_t = transposed(eye, upper)
        xut_ref[:, pl.ds(at, QUERIES)] = upper_t
        store_pairs(keys_up, padded_at, dot(upper, wk_ref[...]).astype(BF16))
        store_heads(vt_up, padded_at, dot(wvt[...], upper_t).astype(BF16))

    place = place_ref[0, 0]
    width = width_ref[0, 0]
    shape = (SPAN, QUERIES)
    memory, query = iota(shape, 0), iota(shape, 1)
    memory_col = (memory // TILE) * FLANK_COLS + memory % FLANK_COLS - FLANK_COLS
    query_col = (query // TILE) * FLANK_COLS + query % FLANK_COLS
    memory_row = (memory % TILE) // FLANK_COLS
    query_row = (query % TILE) // FLANK_COLS

    def prepare_masks(window):
        column_at = memory_col + window * BLOCK_COLS
        inside = (column_at >= 0) & (column_at < width)
        earlier = (memory_row < query_row) | ((memory_row == query_row) & (memory_col <= query_col))
        itself = (memory_row == query_row) & (memory_col == query_col)
        bias_low[...] = jnp.where((inside & earlier) | itself, 0.0, big_negative)
        first = iota(bias_up.shape, 1) == 0
        closed = jnp.where(inside[:, 0:128] & (place > 0), 0.0, big_negative)
        bias_up[...] = jnp.where(first, closed, 0.0).astype(BF16)

    def e_copy(window):
        slot = window % 2
        return pltpu.make_async_copy(e_buf.at[slot], e_ref.at[window], e_sem.at[slot])

    prepare_upper(0)

    @pl.loop(0, WINDOWS)
    def _(window):
        @pl.when(window < WINDOWS - 1)
        def _():
            prepare_upper(window + 1)

        prepare_masks(window)

        @pl.when(window > 1)
        def _():
            e_copy(window - 2).wait()

        slot = window % 2
        at = pl.multiple_of(window * QUERIES, QUERIES)
        here, span = pl.ds(at, QUERIES), pl.ds(at, SPAN)

        def scores(head):
            pair = head // 2
            q_head = head_of_pair(qs[pair * 128 : pair * 128 + 128, here], head % 2)
            upper = dot(
                jnp.concatenate([keys_up[pair, span, :], bias_up[...]], axis=1),
                jnp.concatenate([q_head, ones_row[...]], axis=0),
            )
            lower = dot(keys[pair, span, :], q_head) + bias_low[...]
            shape = (SPAN // 8, 8, QUERIES)
            top = jnp.maximum(
                jnp.max(upper.reshape(shape), axis=0), jnp.max(lower.reshape(shape), axis=0)
            )
            return upper, lower, jnp.max(top, axis=0, keepdims=True)

        def mix(head, e_up, e_low):
            mixed = dot(vt_up[head, :, span], e_up) + dot(vt[head, :, span], e_low)
            inverse = 1.0 / mixed[HEAD_DIM : HEAD_DIM + 1]
            rows = slice(head * HEAD_DIM, head * HEAD_DIM + HEAD_DIM)
            ot_ref[rows, here] = (mixed[0:HEAD_DIM] * inverse).astype(BF16)
            inv_ref[head : head + 1, here] = inverse

        current, raised = scores(0), None
        for head in range(8):
            upcoming = scores(head + 1) if head < 7 else None
            upper, lower, peak = current
            e_up = jnp.exp2(upper - peak).astype(BF16)
            e_low = jnp.exp2(lower - peak).astype(BF16)
            e_buf[slot, head, 0:SPAN, :] = e_up
            e_buf[slot, head, SPAN : 2 * SPAN, :] = e_low
            if head > 0:
                mix(head - 1, *raised)
            raised = (e_up, e_low)
            current = upcoming
        mix(7, *raised)
        e_copy(window).start()

    for window in range(WINDOWS - 2, WINDOWS):
        e_copy(window).wait()

    @pl.when(band < size - 1)
    def _():
        for window in range(WINDOWS):
            up_copy(window).wait_send()


def feed_kernel(
    tok_ref, cot_ref, embed_ref, ot_ref, inv_ref, wo_ref, wi_ref, wb_ref, vec_ref,
    out_ref, dr1_ref, dot_ref, dd_ref, gin_ref, gbo_ref, small_ref,
    embed_rows, wot, wit, wbt, cols, bi_col, acc, acc_bi, n1_buf, y1_buf, slope, yl, df, da, hl, dh,
):
    eye = identity(256)
    fill_embed(embed_ref, embed_rows)
    wot[...] = transposed(eye, wo_ref[...])
    wit[...] = transposed(eye, wi_ref[...])
    wbt[...] = transposed(eye, wb_ref[...])
    ff = wi_ref.shape[1]
    width = wi_ref.shape[0]
    for index in range(5):
        at = ff + index * width
        cols[index] = column(eye, vec_ref[:, at : at + width])
    bi_col[...] = column(eye, vec_ref[:, 0:ff])
    acc[...] = jnp.zeros_like(acc)
    acc_bi[...] = jnp.zeros_like(acc_bi)
    part = 256

    @pl.loop(0, WINDOWS)
    def _(window):
        here = pl.ds(pl.multiple_of(window * QUERIES, QUERIES), QUERIES)
        raw = raw_window(tok_ref, window)
        embed = embed_window(embed_rows, window).astype(BF16)
        start = jnp.concatenate(
            [
                dot_nt(eye, raw[:, half * 256 : half * 256 + 256])
                + dot_nt(eye, embed[:, half * 256 : half * 256 + 256])
                for half in range(2)
            ],
            axis=0,
        )
        n1, inv1 = norm_stats(start + dot(wot[...], ot_ref[:, here]))
        y1 = n1 * wide(cols[1]) + wide(cols[2])
        low = y1.astype(BF16)
        n1_buf[...] = n1
        y1_buf[...] = y1
        yl[:, here] = low

        for index in range(ff // part):
            rows = pl.ds(index * part, part)
            u = dot(wit[rows, :], low) + wide(bi_col[rows, :])
            square = u * u
            t = jnp.tanh(GELU_SCALE * u * (1.0 + GELU_CUBE * square))
            half_up = 0.5 * (1.0 + t)
            hl[rows, here] = (u * half_up).astype(BF16)
            slope[rows, :] = half_up + (0.5 * GELU_SCALE) * u * (1.0 - t * t) * (
                1.0 + 3.0 * GELU_CUBE * square
            )

        f = dot(wbt[...], hl[:, here]) + wide(cols[0])
        n2, inv2 = norm_stats(y1_buf[...] + f)
        g2 = wide(cols[3])
        result = (n2 * g2 + wide(cols[4])).astype(BF16)
        result = dot_nt(eye, result).astype(BF16)
        for half in range(2):
            at = pl.multiple_of((2 * window + half) * FLANK_COLS, FLANK_COLS)
            out_ref[:, pl.ds(at, FLANK_COLS), :] = result[half * TILE : half * TILE + TILE].reshape(
                BLOCK_ROWS, FLANK_COLS, -1
            )
        raw_cot = raw_window(cot_ref, window)
        cot = jnp.concatenate(
            [dot_nt(eye, raw_cot[:, half * 256 : half * 256 + 256]) for half in range(2)], axis=0
        )
        acc[0] += halves(cot * n2)
        acc[1] += halves(cot)
        dr2 = norm_back(n2, inv2, cot, g2)
        df_low = dr2.astype(BF16)
        acc[2] += halves(df_low.astype(F32))
        df[:, here] = df_low

        for index in range(ff // part):
            rows = pl.ds(index * part, part)
            dh_low = (dot(wb_ref[rows, :], df_low) * slope[rows, :]).astype(BF16)
            dh[rows, here] = dh_low
            acc_bi[rows, :] += halves(dh_low.astype(F32))

        dy1 = dr2 + dot(wi_ref[...], dh[:, here])
        n1 = n1_buf[...]
        acc[3] += halves(dy1 * n1)
        acc[4] += halves(dy1)
        dr1 = norm_back(n1, inv1, dy1, wide(cols[1]))
        dr1_ref[:, here] = dr1
        da_low = dr1.astype(BF16)
        da[:, here] = da_low
        d_o = dot(wo_ref[...], da_low)
        product = d_o * ot_ref[:, here].astype(F32)
        for head in range(8):
            rows = slice(head * HEAD_DIM, head * HEAD_DIM + HEAD_DIM)
            inverse = inv_ref[head : head + 1, here]
            dot_ref[rows, here] = (d_o[rows] * inverse).astype(BF16)
            dd_ref[head : head + 1, here] = (
                jnp.sum(product[rows], axis=0, keepdims=True) * inverse
            )

    count, back_rows, share = gin_ref.shape[0], ff // gin_ref.shape[0], gin_ref.shape[1]

    @pl.loop(0, ff // 256)
    def _(index):
        rows = pl.ds(pl.multiple_of(index * 256, 256), 256)
        back = dot_nt(hl[rows, :], df[...]).astype(BF16)
        shares = 256 // back_rows
        for part in range(shares):
            gbo_ref[reversed_bits(index * shares + part, count), 0:back_rows, :] = back[
                part * back_rows : part * back_rows + back_rows
            ]
        into = dot_nt(yl[...], dh[rows, :]).astype(BF16)
        for owner in range(count):
            gin_ref[reversed_bits(owner, count), :, rows] = into[owner * share : owner * share + share]

    out = dot_nt(ot_ref[...], da[...]).astype(BF16)
    for owner in range(count):
        gbo_ref[reversed_bits(owner, count), back_rows:, :] = out[
            owner * share : owner * share + share
        ]
    small_ref[...] = jnp.zeros_like(small_ref)
    for index in range(5):
        small_ref[index : index + 1, :] = lane_sums(acc[index])[0:1]
    bias = lane_sums(acc_bi[...])[0:1]
    for index in range(ff // width):
        small_ref[5 + index : 6 + index, :] = bias[:, index * width : (index + 1) * width]


def back_kernel(
    wq_ref, wk_ref, wv_ref, xt_ref, xut_ref, qt_ref, dot_ref, dd_ref, dr1_ref,
    small_in, e_ref, gin_hbm, gbo_hbm,
    gt_ref, qkv_ref, gin_ref, gbo_ref, small_ref,
    wkt, w3, w2, vals, vals_up, kt, kt_up, dq_up, d3, d2, dk_acc, dv_acc,
    dxu, below, e_buf, e_sem, load_sem,
    gin_buf, gin_recv, gin_across, gin_parts, gbo_buf, gbo_recv, gbo_across,
    qkv_buf, qkv_recv, qkv_across, small_buf, small_recv,
    in_ss, in_rs, bo_ss, bo_rs, qkv_ss, qkv_rs, small_ss, small_rs, halo_ss, halo_rs,
    *, size, groups,
):
    band, grp = lax.axis_index("band"), lax.axis_index("grp")
    depth = levels(size)
    MESH = pl.DeviceIdType.MESH
    barrier = pltpu.get_barrier_semaphore()
    for level in range(depth):
        bit = (band // (1 << level)) % 2
        pl.semaphore_signal(
            barrier, inc=1, device_id=(band + (1 << level) * (1 - 2 * bit), grp), device_id_type=MESH
        )
    for step in range(1, groups):
        pl.semaphore_signal(
            barrier, inc=1, device_id=(band, (grp + step) % groups), device_id_type=MESH
        )

    @pl.when((band % 2 == 1) & (band < size - 1))
    def _():
        pl.semaphore_signal(barrier, inc=1, device_id=(band + 1, grp), device_id_type=MESH)

    load_in = pltpu.make_async_copy(gin_hbm, gin_buf, load_sem.at[0])
    load_bo = pltpu.make_async_copy(gbo_hbm, gbo_buf, load_sem.at[1])
    load_bo.start()
    load_in.start()

    def e_copies(pair, part):
        return [
            pltpu.make_async_copy(
                e_ref.at[window, pl.ds(2 * pair, 2), pl.ds(part * SPAN, SPAN)],
                e_buf.at[pair % 2, window],
                e_sem.at[pair % 2, window],
            )
            for window in range(WINDOWS)
        ]

    for copy in e_copies(0, 0):
        copy.start()
    above = jnp.where((band % 2 == 0) & (band > 0), 1, 0)
    pl.semaphore_wait(barrier, depth + groups - 1 + above)

    sum_in = Reduction(
        gin_buf, gin_recv, gin_across, gin_parts,
        lambda k: in_ss.at[k], lambda k: in_rs.at[k], band, grp, size, groups,
    )
    sum_bo = Reduction(
        gbo_buf, gbo_recv, gbo_across, None,
        lambda k: bo_ss.at[k], lambda k: bo_rs.at[k], band, grp, size, groups,
    )

    def sum_qkv(pair):
        return Reduction(
            qkv_buf.at[pair], qkv_recv.at[pair], qkv_across.at[pair], None,
            lambda k: qkv_ss.at[pair, k], lambda k: qkv_rs.at[pair, k], band, grp, size, groups,
        )

    sum_small = SmallSum(small_buf, small_recv, small_ss, small_rs, band, grp, size, groups)

    def halo(window):
        here = pl.ds(pl.multiple_of(window * QUERIES, QUERIES), QUERIES)
        return pltpu.make_async_remote_copy(
            src_ref=dxu.at[:, here], dst_ref=below.at[:, here],
            send_sem=halo_ss.at[window], recv_sem=halo_rs.at[window],
            device_id=(jnp.maximum(band - 1, 0), grp), device_id_type=MESH,
        )

    def write_in(value, columns):
        gin_ref[:, columns] = value

    def write_bo(value):
        gbo_ref[...] = value

    def write_qkv(pair):
        def write(value):
            qkv_ref[pair] = value

        return write

    eye = identity(256)
    wkt[...] = transposed(eye, wk_ref[...])
    for pair in range(4):
        cols = slice(pair * 128, pair * 128 + 128)
        for index, ref in enumerate((wq_ref, wk_ref, wv_ref)):
            w3[:, pair * 384 + index * 128 : pair * 384 + index * 128 + 128] = ref[:, cols]
        for index, ref in enumerate((wk_ref, wv_ref)):
            w2[:, pair * 256 + index * 128 : pair * 256 + index * 128 + 128] = ref[:, cols]
    clear_pads_rows(vals)
    clear_pads_rows(vals_up)
    clear_pads_lanes(kt)
    clear_pads_lanes(kt_up)
    load_bo.wait()
    sum_bo.start(0)
    load_in.wait()
    sum_in.start(0)

    @pl.loop(0, WINDOWS)
    def _(window):
        here = pl.ds(pl.multiple_of(window * QUERIES, QUERIES), QUERIES)
        padded_at = pl.multiple_of(window * QUERIES + TILE, TILE)
        low = transposed(eye, xt_ref[:, here])
        upper = transposed(eye, xut_ref[:, here])
        store_pairs(vals, padded_at, dot(low, wv_ref[...]).astype(BF16))
        kt[:, pl.ds(padded_at, QUERIES)] = dot(wkt[...], xt_ref[:, here]).astype(BF16)
        store_pairs(vals_up, padded_at, dot(upper, wv_ref[...]).astype(BF16))
        kt_up[:, pl.ds(padded_at, QUERIES)] = dot(wkt[...], xut_ref[:, here]).astype(BF16)

    sum_bo.advance(0)
    sum_in.advance(0)

    def pass_over(pair, part, v_rows, k_cols):
        for copy in e_copies(pair, part):
            copy.wait()
        dk_acc[...] = jnp.zeros_like(dk_acc)
        dv_acc[...] = jnp.zeros_like(dv_acc)
        feats = pl.ds(pl.multiple_of(pair * 128, 128), 128)
        items = [(window, half) for window in range(WINDOWS) for half in range(2)]

        def limits(window):
            first = TILE if window == 0 else 0
            last = SPAN - TILE if window == WINDOWS - 1 else SPAN
            return first, last

        def grad_probs(window, half):
            first, last = limits(window)
            here = slice(window * QUERIES, window * QUERIES + QUERIES)
            rows = slice(window * QUERIES + first, window * QUERIES + last)
            return dot(v_rows[pair, rows, :], head_of_pair(dot_ref[feats, here], half))

        upcoming = grad_probs(*items[0])
        for index, (window, half) in enumerate(items):
            current = upcoming
            if index + 1 < len(items):
                upcoming = grad_probs(*items[index + 1])
            first, last = limits(window)
            here = slice(window * QUERIES, window * QUERIES + QUERIES)
            span = slice(window * QUERIES + first, window * QUERIES + last)
            mine = pl.ds(pl.multiple_of(pair * 128 + half * HEAD_DIM, HEAD_DIM), HEAD_DIM)
            rows = slice(half * HEAD_DIM, half * HEAD_DIM + HEAD_DIM)
            e = e_buf[pair % 2, window, half, first:last, :]
            inner = dd_ref[pl.ds(2 * pair + half, 1), here]
            ds = (e.astype(F32) * (current - inner)).astype(BF16)
            dq = dot(k_cols[mine, span], ds)
            if part == 0:
                dq_up[mine, here] = dq
            else:
                at = pl.multiple_of(pair * 384 + half * HEAD_DIM, HEAD_DIM)
                d3[pl.ds(at, HEAD_DIM), here] = ((dq + dq_up[mine, here]) * 0.125).astype(BF16)
            dk_acc[rows, span] += dot_nt(qt_ref[mine, here], ds)
            dv_acc[rows, span] += dot_nt(dot_ref[mine, here], e)

    inside = slice(TILE, PADDED - TILE)

    @pl.loop(0, 4)
    def _(pair):
        @pl.when(pair < 3)
        def _():
            for copy in e_copies(pair + 1, 0):
                copy.start()

        @pl.when(pair == 3)
        def _():
            for copy in e_copies(0, 1):
                copy.start()

        pass_over(pair, 0, vals_up, kt_up)
        at = pl.multiple_of(pair * 256, 256)
        d2[pl.ds(at, 128), :] = dk_acc[:, inside].astype(BF16)
        d2[pl.ds(at + 128, 128), :] = dv_acc[:, inside].astype(BF16)

        @pl.when(pair == 2)
        def _():
            sum_in.advance(1)

    sum_bo.advance(1)
    for window in range(WINDOWS):
        here = slice(window * QUERIES, window * QUERIES + QUERIES)
        dxu[:, here] = dot(w2[...], d2[:, here]).astype(BF16)

        @pl.when(band > 0)
        def _(window=window):
            halo(window).start()

    @pl.loop(0, 4)
    def _(pair):
        @pl.when(pair < 3)
        def _():
            for copy in e_copies(pair + 1, 1):
                copy.start()

        pass_over(pair, 1, vals, kt)

        @pl.when(pair == 0)
        def _():
            sum_bo.advance(2)
            sum_in.advance(2)

        @pl.when(pair == 1)
        def _():
            sum_bo.advance(3)
            sum_in.advance(3)

        @pl.when(pair == 2)
        def _():
            sum_bo.finish(write_bo)
            sum_in.advance(4)

        @pl.when(pair == 3)
        def _():
            sum_in.finish(write_in)

        for earlier in range(3):
            for stage in range(3 - earlier):

                @pl.when(pair == earlier + 1 + stage)
                def _(earlier=earlier, stage=stage):
                    sum_qkv(earlier).advance(stage)

        at = pl.multiple_of(pair * 384, 128)
        d3[pl.ds(at + 128, 128), :] = dk_acc[:, inside].astype(BF16)
        d3[pl.ds(at + 256, 128), :] = dv_acc[:, inside].astype(BF16)
        grads = dot_nt(xt_ref[...], d3[pl.ds(at, 384), :])
        grads_up = dot_nt(xut_ref[...], d2[pl.ds(pl.multiple_of(pair * 256, 256), 256), :])
        share = qkv_buf.shape[2]
        low_q = grads[:, 0:128].astype(BF16)
        low_kv = (grads[:, 128:384] + grads_up).astype(BF16)
        for owner in range(size):
            rows = slice(owner * share, owner * share + share)
            qkv_buf[pair, reversed_bits(owner, size), :, 0:128] = low_q[rows]
            qkv_buf[pair, reversed_bits(owner, size), :, 128:384] = low_kv[rows]
        sum_qkv(pair).start(0)

    shape = (16, LEN)
    channel = (iota(shape, 1) // TILE + iota(shape, 1) % FLANK_COLS) % 3
    chosen = jnp.where(channel + 9 == iota(shape, 0), 1.0, 0.0).astype(BF16)
    sums = dot_nt(chosen, dr1_ref[...].astype(BF16))
    totals = dot_nt(chosen, d3[...])
    high = totals.astype(BF16)
    sums += dot_nt(high, w3[...]) + dot_nt((totals - high.astype(F32)).astype(BF16), w3[...])
    sums += dot_nt(chosen, dxu[...]) * jnp.where(band > 0, 1.0, 0.0)
    small_buf[0] = small_in[...] + sums
    sum_small.start(0)

    @pl.when(band == size - 1)
    def _():
        below[...] = jnp.zeros_like(below)

    chains = [(sum_qkv(pair), write_qkv(pair), 3 - pair) for pair in range(4)]

    @pl.loop(0, WINDOWS)
    def _(window):
        @pl.when(band < size - 1)
        def _():
            halo(window).wait_recv()

        here = pl.ds(pl.multiple_of(window * QUERIES, QUERIES), QUERIES)
        dx = dr1_ref[:, here] + dot(w3[...], d3[:, here]) + below[:, here].astype(F32)
        rows = dot_nt(eye, dx.astype(BF16)).astype(BF16)
        for half in range(2):
            at = pl.multiple_of((2 * window + half) * FLANK_COLS, FLANK_COLS)
            gt_ref[:, pl.ds(at, FLANK_COLS), :] = rows[half * TILE : half * TILE + TILE].reshape(
                BLOCK_ROWS, FLANK_COLS, -1
            )

        for turn in range(depth + 1):

            @pl.when(window == turn + 5 - depth)
            def _(turn=turn):
                for chain, write, done in chains:
                    stage = done + turn
                    if stage < depth:
                        chain.advance(stage)
                    if stage == depth:
                        chain.finish(write)
                if turn < depth:
                    sum_small.advance(turn)
                else:
                    small_ref[...] = sum_small.finish()

    @pl.when(band > 0)
    def _():
        for window in range(WINDOWS):
            halo(window).wait_send()


def emit_kernel(
    qkv_ref, gin_ref, gbo_ref, small_ref,
    gq, gk, gv, gout, gin, gbi, gback, gbb, gg1, gs1, gg2, gs2, gemb,
    *, size,
):
    for pair in range(4):
        for index, ref in enumerate((gq, gk, gv)):
            ref[:, pair * 128 : pair * 128 + 128] = qkv_ref[pair, :, index * 128 : index * 128 + 128]
    back_share = gback.shape[0]
    gback[...] = gbo_ref[0:back_share]
    gout[...] = gbo_ref[back_share:]
    gin[...] = gin_ref[...]
    band = lax.axis_index("band")
    share = gout.shape[0]
    mine = 0.0
    for owner in range(size):
        mine = mine + jnp.where(band == owner, small_ref[:, owner * share : owner * share + share], 0.0)
    for row, ref in ((2, gbb), (3, gg1), (4, gs1), (0, gg2), (1, gs2)):
        ref[...] = mine[row : row + 1]
    gemb[...] = mine[9:12]
    per_row = small_ref.shape[1] // back_share
    bias = 0.0
    for owner in range(size):
        at = owner % per_row * back_share
        row = small_ref[5 + owner // per_row : 6 + owner // per_row, at : at + back_share]
        bias = bias + jnp.where(band == owner, row, 0.0)
    gbi[...] = bias


def shards(
    tokens, row_place, row_width, cotangent, chan_embed, w_query, w_key, w_value, w_out, w_in,
    bias_in, w_back, bias_back, gain_first, shift_first, gain_second, shift_second,
):
    width = tokens.shape[3]
    ff = w_in.shape[1]
    tok = tokens.reshape(BLOCK_ROWS, ROW_POS, width)
    cot = cotangent.reshape(BLOCK_ROWS, ROW_POS, width)
    shape = jax.ShapeDtypeStruct
    size, groups = lax.axis_size("band"), lax.axis_size("grp")
    dma = pltpu.SemaphoreType.DMA
    params = pltpu.CompilerParams(vmem_limit_bytes=LIMIT)
    xt, xut, qt, ot, inv, e_all = pl.pallas_call(
        functools.partial(attend_kernel, size=size),
        name="attend_forward",
        out_shape=(
            shape((width, LEN), BF16),
            shape((width, LEN), BF16),
            shape((width, LEN), BF16),
            shape((width, LEN), BF16),
            shape((8, LEN), F32),
            shape((WINDOWS, 8, 2 * SPAN, QUERIES), BF16),
        ),
        in_specs=[smem()] * 2 + [vmem()] * 5,
        out_specs=(vmem(), vmem(), vmem(), vmem(), vmem(), hbm()),
        scratch_shapes=[
            pltpu.VMEM((ROW_POS, width), F32),
            pltpu.VMEM((BLOCK_ROWS, ROW_POS, width), BF16),
            pltpu.VMEM((width, width), BF16),
            pltpu.VMEM((width, width), BF16),
            pltpu.VMEM((width, LEN), BF16),
            pltpu.VMEM((4, PADDED, 128), BF16),
            pltpu.VMEM((4, PADDED, 128), BF16),
            pltpu.VMEM((8, HEAD_DIM + 16, PADDED), BF16),
            pltpu.VMEM((8, HEAD_DIM + 16, PADDED), BF16),
            pltpu.VMEM((SPAN, QUERIES), F32),
            pltpu.VMEM((SPAN, 128), BF16),
            pltpu.VMEM((128, QUERIES), BF16),
            pltpu.VMEM((2, 8, 2 * SPAN, QUERIES), BF16),
            dma((2,)),
            dma((WINDOWS,)),
            dma((WINDOWS,)),
        ],
        compiler_params=pltpu.CompilerParams(
            vmem_limit_bytes=LIMIT, collective_id=1, has_side_effects=True
        ),
    )(row_place, row_width, tok, chan_embed, w_query, w_key, w_value)
    share, back_share = width // size, ff // size
    vectors = jnp.concatenate(
        [bias_in, bias_back, gain_first, shift_first, gain_second, shift_second]
    ).reshape(1, -1)
    layer_out, dr1, do_t, dd, g_in, g_bo, small = pl.pallas_call(
        feed_kernel,
        name="feed_forward_and_back",
        out_shape=(
            shape((BLOCK_ROWS, ROW_POS, width), BF16),
            shape((width, LEN), F32),
            shape((width, LEN), BF16),
            shape((8, LEN), F32),
            shape((size, share, ff), BF16),
            shape((size, back_share + share, width), BF16),
            shape((16, width), F32),
        ),
        in_specs=[vmem()] * 9,
        out_specs=(vmem(),) * 7,
        scratch_shapes=[
            pltpu.VMEM((ROW_POS, width), F32),
            pltpu.VMEM((width, width), BF16),
            pltpu.VMEM((ff, width), BF16),
            pltpu.VMEM((width, ff), BF16),
            pltpu.VMEM((5, width, 128), F32),
            pltpu.VMEM((ff, 128), F32),
            pltpu.VMEM((5, width, 128), F32),
            pltpu.VMEM((ff, 128), F32),
            pltpu.VMEM((width, QUERIES), F32),
            pltpu.VMEM((width, QUERIES), F32),
            pltpu.VMEM((ff, QUERIES), F32),
            pltpu.VMEM((width, LEN), BF16),
            pltpu.VMEM((width, LEN), BF16),
            pltpu.VMEM((width, LEN), BF16),
            pltpu.VMEM((ff, LEN), BF16),
            pltpu.VMEM((ff, LEN), BF16),
        ],
        compiler_params=params,
    )(tok, cot, chan_embed, ot, inv, w_out, w_in, w_back, vectors)
    stages = levels(size) + 2 * (groups - 1)
    grad_tokens, g_qkv, g_in, g_bo, small = pl.pallas_call(
        functools.partial(back_kernel, size=size, groups=groups),
        name="attend_backward",
        out_shape=(
            shape((BLOCK_ROWS, ROW_POS, width), BF16),
            shape((4, share, 384), F32),
            shape((share, ff), F32),
            shape((back_share + share, width), F32),
            shape((16, width), F32),
        ),
        in_specs=[vmem()] * 10 + [hbm()] * 3,
        out_specs=(vmem(),) * 5,
        scratch_shapes=[
            pltpu.VMEM((width, width), BF16),
            pltpu.VMEM((width, 3 * width), BF16),
            pltpu.VMEM((width, 2 * width), BF16),
            pltpu.VMEM((4, PADDED, 128), BF16),
            pltpu.VMEM((4, PADDED, 128), BF16),
            pltpu.VMEM((width, PADDED), BF16),
            pltpu.VMEM((width, PADDED), BF16),
            pltpu.VMEM((width, LEN), F32),
            pltpu.VMEM((3 * width, LEN), BF16),
            pltpu.VMEM((2 * width, LEN), BF16),
            pltpu.VMEM((128, PADDED), F32),
            pltpu.VMEM((128, PADDED), F32),
            pltpu.VMEM((width, LEN), BF16),
            pltpu.VMEM((width, LEN), BF16),
            pltpu.VMEM((2, WINDOWS, 2, SPAN, QUERIES), BF16),
            dma((2, WINDOWS)),
            dma((2,)),
            pltpu.VMEM((size, share, ff), BF16),
            pltpu.VMEM((size, share, ff), BF16),
            pltpu.VMEM((groups - 1, size // 2, share, ff // groups), BF16),
            pltpu.VMEM((groups, share, ff // groups), F32),
            pltpu.VMEM((size, back_share + share, width), BF16),
            pltpu.VMEM((size, back_share + share, width), BF16),
            pltpu.VMEM((groups, back_share + share, width), BF16),
            pltpu.VMEM((4, size, share, 384), BF16),
            pltpu.VMEM((4, size, share, 384), BF16),
            pltpu.VMEM((4, groups, share, 384), BF16),
            pltpu.VMEM((levels(size) + 1, 16, width), F32),
            pltpu.VMEM((levels(size) + groups - 1, 16, width), F32),
            dma((stages,)),
            dma((stages,)),
            dma((stages,)),
            dma((stages,)),
            dma((4, stages)),
            dma((4, stages)),
            dma((stages,)),
            dma((stages,)),
            dma((WINDOWS,)),
            dma((WINDOWS,)),
        ],
        compiler_params=pltpu.CompilerParams(
            vmem_limit_bytes=LIMIT, collective_id=0, has_side_effects=True
        ),
    )(w_query, w_key, w_value, xt, xut, qt, do_t, dd, dr1, small, e_all, g_in, g_bo)
    vector = shape((1, share), F32)
    square = shape((share, width), F32)
    gq, gk, gv, gout, gin, gbi, gback, gbb, gg1, gs1, gg2, gs2, gemb = pl.pallas_call(
        functools.partial(emit_kernel, size=size),
        name="emit_shares",
        out_shape=(
            square, square, square, square, shape((share, ff), F32), shape((1, back_share), F32),
            shape((back_share, width), F32), vector, vector, vector, vector, vector,
            shape((3, share), F32),
        ),
        in_specs=[vmem()] * 4,
        out_specs=(vmem(),) * 13,
        compiler_params=pltpu.CompilerParams(vmem_limit_bytes=16 * 1024 * 1024),
    )(g_qkv, g_in, g_bo, small)
    return (
        layer_out.reshape(tokens.shape),
        grad_tokens.reshape(tokens.shape),
        gq, gk, gv, gout, gin, gbi.reshape(-1), gback,
        gbb.reshape(-1), gg1.reshape(-1), gs1.reshape(-1), gg2.reshape(-1), gs2.reshape(-1), gemb,
    )


def solution(mesh):
    tall = P("grp", "band", None, None)
    return jax.shard_map(
        shards,
        mesh=mesh,
        in_specs=(tall, P("grp", "band"), P("grp", "band"), tall) + (P(),) * 13,
        out_specs=(tall, tall)
        + (P("band", None),) * 5
        + (P("band"), P("band", None))
        + (P("band"),) * 5
        + (P(None, "band"),),
        check_vma=False,
    )
```

```python
import functools

import jax
import jax.numpy as jnp
from jax import lax
from jax.experimental import pallas as pl
from jax.experimental.pallas import tpu as pltpu
from jax.sharding import PartitionSpec as P

HEAD_DIM = 64
ROW_POS = 192
BLOCK_ROWS = 8
BLOCK_COLS = 32
FLANK_COLS = 16
WINDOWS = ROW_POS // BLOCK_COLS
BLOCKS = ROW_POS // FLANK_COLS
TILE = BLOCK_ROWS * FLANK_COLS
QUERIES = 2 * TILE
SPAN = 4 * TILE
LEN = BLOCK_ROWS * ROW_POS
PADDED = LEN + 2 * TILE

norm_eps = 1e-06
big_negative = -1e30
F32 = jnp.float32
BF16 = jnp.bfloat16
LOG2_E = 1.4426950408889634
GELU_SCALE = 0.7978845608028654
GELU_CUBE = 0.044715


def dot(left, right):
    return jnp.dot(left, right, preferred_element_type=F32)


def dot_nt(left, right):
    return lax.dot_general(left, right, (((1,), (1,)), ((), ())), preferred_element_type=F32)


def iota(shape, dim):
    return lax.broadcasted_iota(jnp.int32, shape, dim)


def identity(size):
    return jnp.where(iota((size, size), 0) == iota((size, size), 1), 1.0, 0.0).astype(BF16)


def transposed(eye, value):
    step = eye.shape[0]
    parts = [
        dot_nt(eye, value[:, at : at + step]).astype(BF16) for at in range(0, value.shape[1], step)
    ]
    return jnp.concatenate(parts, axis=0)


def column(eye, row):
    step = eye.shape[0]
    ones = jnp.ones((128, step), BF16)
    parts = [
        dot_nt(jnp.where(eye > 0, row[:, at : at + step], 0).astype(BF16), ones)
        for at in range(0, row.shape[1], step)
    ]
    return jnp.concatenate(parts, axis=0)


def wide(value):
    return jnp.concatenate([value, value], axis=1)


def halves(value):
    return value[:, :128] + value[:, 128:]


def fill_embed(embed_ref, rows_ref):
    embed = embed_ref[...].astype(F32)
    channel = lax.rem(iota(rows_ref.shape, 0), 3)
    rows_ref[...] = jnp.where(
        channel == 0, embed[0:1], jnp.where(channel == 1, embed[1:2], embed[2:3])
    ).astype(BF16)


def block_rows(rows_ref, block):
    return rows_ref[:, pl.ds(pl.multiple_of(block * FLANK_COLS, FLANK_COLS), FLANK_COLS), :]


def raw_window(rows_ref, window):
    parts = [block_rows(rows_ref, 2 * window + half).reshape(TILE, -1) for half in range(2)]
    return jnp.concatenate(parts, axis=0)


def embed_window(embed_rows, window):
    parts = []
    for half in range(2):
        at = pl.multiple_of((2 * window + half) * FLANK_COLS, FLANK_COLS)
        part = embed_rows[pl.ds(at, FLANK_COLS), :][None]
        parts.append(jnp.broadcast_to(part, (BLOCK_ROWS,) + part.shape[1:]).reshape(TILE, -1))
    return jnp.concatenate(parts, axis=0)


def start_window(rows_ref, embed_rows, window):
    return raw_window(rows_ref, window).astype(F32) + embed_window(embed_rows, window).astype(F32)


def norm_stats(value):
    center = value - jnp.mean(value, axis=0, keepdims=True)
    spread = jnp.mean(center * center, axis=0, keepdims=True)
    inverse = lax.rsqrt(spread + norm_eps)
    return center * inverse, inverse


def norm_back(normed, inverse, grad, gain):
    scaled = grad * gain
    first = jnp.mean(scaled, axis=0, keepdims=True)
    second = jnp.mean(scaled * normed, axis=0, keepdims=True)
    return (scaled - first - normed * second) * inverse


def vmem():
    return pl.BlockSpec(memory_space=pltpu.VMEM)


def smem():
    return pl.BlockSpec(memory_space=pltpu.SMEM)


def hbm():
    return pl.BlockSpec(memory_space=pl.ANY)


LIMIT = 62 * 1024 * 1024


def head_of_pair(value, half):
    keep = (iota(value.shape, 0) // HEAD_DIM) == half
    return jnp.where(keep, value, jnp.zeros_like(value))


def clear_pads_rows(ref):
    pad = jnp.zeros((ref.shape[0], TILE, ref.shape[2]), ref.dtype)
    ref[:, 0:TILE, :] = pad
    ref[:, PADDED - TILE : PADDED, :] = pad


def reversed_bits(index, count):
    place, bit = 0, 1
    while bit < count:
        place = place + (index // bit) % 2 * (count // (2 * bit))
        bit *= 2
    return place


def levels(count):
    return count.bit_length() - 1


def first_share(band, bits, count):
    start = 0
    for level in range(bits):
        start = start + (band // (1 << level)) % 2 * (count >> (level + 1))
    return start


class Reduction:
    def __init__(self, buf, shape, recv, later, across, gathered, send_sem, recv_sem, place):
        self.buf, self.recv, self.later = buf, recv, later
        self.across, self.gathered = across, gathered
        self.send_sem, self.recv_sem = send_sem, recv_sem
        self.band, self.grp, self.size, self.groups = place
        self.depth = depth = levels(self.size)
        self.rows = shape[0] // self.size
        self.stages = [("halve", 0)]
        if gathered is None:
            self.stages += [("direct", 1), ("sum", depth)]
        else:
            self.stages += [("split", 1)] + [("halve", bit) for bit in range(1, depth)]
            self.stages += [("gather", depth)]
        self.part = shape[1] // self.groups

    def start_of(self, bits):
        return first_share(self.band, bits, self.size)

    def columns_of(self, member):
        return pl.ds(pl.multiple_of(member * self.part, 128), self.part)

    def columns(self, stage):
        split = [kind for kind, _ in self.stages[:stage]].count("split")
        return self.columns_of(self.grp) if split else slice(None)

    def shares(self, first, count=1):
        return pl.ds(pl.multiple_of(first * self.rows, self.rows), count * self.rows)

    def landing(self, bits):
        return self.later if bits else self.recv

    def landing_rows(self, bits, index, count):
        return self.shares(index + (self.size >> (bits + 1) if bits else 0), count)

    def copies(self, stage):
        kind, bits = self.stages[stage]
        columns = self.columns(stage)
        pieces = []
        if kind == "halve":
            half = self.size >> (bits + 1)
            bit = (self.band // (1 << bits)) % 2
            pieces.append(
                (
                    self.buf.at[self.shares(self.start_of(bits) + (1 - bit) * half, half), columns],
                    self.landing(bits).at[self.landing_rows(bits, 0, half)],
                    bits,
                    (self.band + (1 << bits) * (1 - 2 * bit), self.grp),
                )
            )
        if kind == "direct":
            for step in range(1, self.size // 2):
                partner = (self.band + 2 * step) % self.size
                source = self.buf.at[self.shares(reversed_bits(partner, self.size))]
                place = (partner, self.grp)
                pieces.append((source, self.later.at[self.shares(step)], step, place))
        for step in range(1, self.groups):
            partner = (self.grp + step) % self.groups
            place = (self.band, partner)
            if kind == "sum":
                source, target = self.buf.at[self.shares(self.start_of(bits))], self.across.at[step]
                pieces.append((source, target, self.size // 2 + step - 1, place))
            if kind == "split":
                rows = self.shares(self.start_of(bits), self.size >> bits)
                source = self.buf.at[rows, self.columns_of(partner)]
                pieces.append((source, self.across.at[step - 1], self.depth + step - 1, place))
            if kind == "gather":
                source, target = self.gathered.at[0], self.gathered.at[step]
                pieces.append((source, target, self.depth + self.groups + step - 2, place))
        return [
            pltpu.make_async_remote_copy(
                src_ref=source,
                dst_ref=target,
                send_sem=self.send_sem(sem),
                recv_sem=self.recv_sem(sem),
                device_id=place,
                device_id_type=pl.DeviceIdType.MESH,
            )
            for source, target, sem, place in pieces
        ]

    def start(self, stage):
        for copy in self.copies(stage):
            copy.start()

    def advance(self, stage):
        for copy in self.copies(stage):
            copy.wait()
        kind, bits = self.stages[stage]
        if kind == "halve":
            columns = self.columns(stage)
            half, keep = self.size >> (bits + 1), self.start_of(bits + 1)

            @pl.loop(0, half)
            def _(index):
                mine = self.shares(keep + index)
                total = self.buf[mine, columns].astype(F32)
                total = total + self.landing(bits)[self.landing_rows(bits, index, 1), :].astype(F32)
                self.buf[mine, columns] = total.astype(BF16)
        elif kind == "direct":
            mine = self.shares(self.start_of(self.depth))
            total = self.buf[mine, :].astype(F32)
            for step in range(1, self.size // 2):
                total = total + self.later[step * self.rows : (step + 1) * self.rows, :].astype(F32)
            self.buf[mine, :] = total.astype(BF16)
        else:
            columns = self.columns_of(self.grp)
            keep = self.start_of(bits)

            @pl.loop(0, self.size >> bits)
            def _(index):
                mine = self.shares(keep + index)
                total = self.buf[mine, columns].astype(F32)
                for step in range(self.groups - 1):
                    total = total + self.across[step, self.shares(index), :].astype(F32)
                self.buf[mine, columns] = total.astype(BF16)

        if self.stages[stage + 1][0] == "gather":
            mine = self.shares(self.start_of(self.depth))
            self.gathered[0] = self.buf[mine, self.columns_of(self.grp)].astype(F32)
        self.start(stage + 1)

    def finish(self, out):
        last = len(self.stages) - 1
        for copy in self.copies(last):
            copy.wait()
        if self.stages[last][0] == "sum":
            self.across[0] = self.buf[self.shares(self.start_of(self.depth)), :]
            total = 0.0
            for member in range(self.groups):
                step = (self.grp + self.groups - member) % self.groups
                total = total + self.across[step].astype(F32)
            out(total)
        else:
            for step in range(self.groups):
                member = (self.grp + self.groups - step) % self.groups
                out(self.gathered[step], self.columns_of(member))


class SmallSum:
    def __init__(self, buf, recv, send_sem, recv_sem, place):
        self.buf, self.recv, self.send_sem, self.recv_sem = buf, recv, send_sem, recv_sem
        self.band, self.grp, self.size, self.groups = place

    def copies(self, stage):
        half = self.size // 2
        if stage == 0:
            partners = [(0, (self.band + 1 - 2 * (self.band % 2), self.grp))]
        elif stage == 1:
            partners = [
                (step, ((self.band + 2 * step) % self.size, self.grp)) for step in range(1, half)
            ]
        else:
            partners = [
                (half + step - 1, (self.band, (self.grp + step) % self.groups))
                for step in range(1, self.groups)
            ]
        return [
            pltpu.make_async_remote_copy(
                src_ref=self.buf.at[stage],
                dst_ref=self.recv.at[slot],
                send_sem=self.send_sem.at[slot],
                recv_sem=self.recv_sem.at[slot],
                device_id=partner,
                device_id_type=pl.DeviceIdType.MESH,
            )
            for slot, partner in partners
        ]

    def start(self, stage):
        for copy in self.copies(stage):
            copy.start()

    def advance(self, stage):
        for copy in self.copies(stage):
            copy.wait()
        total = self.buf[stage]
        for slot in (0,) if stage == 0 else range(1, self.size // 2):
            total = total + self.recv[slot]
        self.buf[stage + 1] = total
        self.start(stage + 1)

    def finish(self):
        for copy in self.copies(2):
            copy.wait()
        mine = self.buf[2]
        total = 0.0
        for member in range(self.groups):
            step = (self.grp + self.groups - member) % self.groups
            slot = jnp.where(step == 0, 0, self.size // 2 + step - 1)
            total = total + jnp.where(step == 0, mine, self.recv[slot])
        return total


def store_pairs(ref, at, value):
    for pair in range(value.shape[1] // 128):
        ref[pair, pl.ds(at, value.shape[0]), :] = value[:, pair * 128 : (pair + 1) * 128]


def store_heads(ref, at, value):
    for head in range(value.shape[0] // HEAD_DIM):
        rows = slice(head * HEAD_DIM, head * HEAD_DIM + HEAD_DIM)
        ref[head, 0:HEAD_DIM, pl.ds(at, value.shape[1])] = value[rows]


def clear_pads_lanes(ref):
    pad = jnp.zeros(ref.shape[:2] + (TILE,), ref.dtype)
    ref[:, :, 0:TILE] = pad
    ref[:, :, PADDED - TILE : PADDED] = pad


def gelu_and_slope(u):
    square = u * u
    cube = (GELU_SCALE * GELU_CUBE) * square
    h = 0.5 * jnp.tanh(u * (GELU_SCALE + cube)) + 0.5
    g = u * (2.0 * GELU_SCALE + 6.0 * cube)
    return u * h, h * (1.0 + (1.0 - h) * g)


class Steps:
    def __init__(self, reduction, write):
        self.reduction, self.write, self.stage = reduction, write, 0

    def __call__(self):
        if self.stage < len(self.reduction.stages) - 1:
            self.reduction.advance(self.stage)
            self.stage += 1

    def last(self):
        while self.stage < len(self.reduction.stages) - 1:
            self()
        self.reduction.finish(self.write)


def layer_kernel(
    place_ref, width_ref, embed_ref, bi_ref, bb_ref, g1_ref, s1_ref, g2_ref, s2_ref, tok_h, cot_h, wq_h, wk_h, wv_h, wo_h, wi_h, wb_h,
    out_h, gt_h, e_h, qkv_ref, gin_ref, gback_ref, gout_ref, small_ref,
    tok, side, w4, wta, wtb, ww, wt, xt, xut, qt, ot, da, rows_a, rows_b, cols_a, cols_b, hd,
    bias_low, bias_up, ones_row, embed_rows, cols, bi_col, n1_buf, d_o, acc, below,
    inv, dd,
    in_recv, in_later, in_across, in_parts, back_recv, back_later, back_across, back_parts,
    out_recv, out_later, out_across,
    qkv_recv, qkv_later, qkv_across, small_buf, small_recv, totals,
    load_sem, e_out_sem, e_in_sem, out_sem, up_ss, up_rs, halo_ss, halo_rs,
    in_ss, in_rs, back_ss, back_rs, go_ss, go_rs, qkv_ss, qkv_rs, small_ss, small_rs,
    *, size, groups, in_split, back_split,
):
    band, grp = lax.axis_index("band"), lax.axis_index("grp")
    place = (band, grp, size, groups)
    depth = levels(size)
    MESH = pl.DeviceIdType.MESH
    wq, wk, wv, wo = (w4.at[index] for index in range(4))
    wit, wb, wi, wbt = ww.at[0], ww.at[1], wt.at[0], wt.at[1]
    width, ff = wi_h.shape

    sources = (tok_h, wq_h, wk_h, wv_h, wo_h, wi_h, wb_h, cot_h)
    targets = (tok, wq, wk, wv, wo, wi, wb, side)
    loads = [
        pltpu.make_async_copy(source, target, load_sem.at[index])
        for index, (source, target) in enumerate(zip(sources, targets))
    ]
    for load in loads[:7]:
        load.start()
    barrier = pltpu.get_barrier_semaphore()
    odd = band % 2
    pl.semaphore_signal(barrier, inc=1, device_id=(band + 1 - 2 * odd, grp), device_id_type=MESH)
    for step in range(1, size // 2):
        pl.semaphore_signal(
            barrier, inc=1, device_id=((band + 2 * step) % size, grp), device_id_type=MESH
        )
    for step in range(1, groups):
        pl.semaphore_signal(
            barrier, inc=1, device_id=(band, (grp + step) % groups), device_id_type=MESH
        )
    beyond = (odd == 1) & (band < size - 1) | (odd == 0) & (band > 0)

    @pl.when(beyond)
    def _():
        pl.semaphore_signal(
            barrier, inc=1, device_id=(band + 2 * odd - 1, grp), device_id_type=MESH
        )

    pl.semaphore_wait(barrier, size // 2 + groups - 1 + jnp.where(beyond, 1, 0))

    def up_copy(window):
        columns = pl.ds(pl.multiple_of(window * BLOCK_COLS, BLOCK_COLS), BLOCK_COLS)
        return pltpu.make_async_remote_copy(
            src_ref=tok_h.at[:, columns, :], dst_ref=side.at[:, columns, :],
            send_sem=up_ss.at[window], recv_sem=up_rs.at[window],
            device_id=(jnp.minimum(band + 1, size - 1), grp), device_id_type=MESH,
        )

    def halo(window):
        here = pl.ds(pl.multiple_of(window * QUERIES, QUERIES), QUERIES)
        return pltpu.make_async_remote_copy(
            src_ref=dxu.at[:, here], dst_ref=below.at[:, here],
            send_sem=halo_ss.at[window], recv_sem=halo_rs.at[window],
            device_id=(jnp.maximum(band - 1, 0), grp), device_id_type=MESH,
        )

    @pl.when(band < size - 1)
    def _():
        for window in range(WINDOWS):
            up_copy(window).start()

    @pl.when(band == 0)
    def _():
        side[...] = jnp.zeros_like(side)

    keys, keys_up, vt, vt_up, qs = rows_a, rows_b, cols_a, cols_b, da
    eye = identity(256)
    fill_embed(embed_ref, embed_rows)
    clear_pads_rows(keys)
    clear_pads_rows(keys_up)
    clear_pads_lanes(vt)
    clear_pads_lanes(vt_up)
    sums = jnp.where(iota((16, PADDED), 0) == 0, 1.0, 0.0).astype(BF16)
    for head in range(8):
        vt[head, HEAD_DIM:, :] = sums
        vt_up[head, HEAD_DIM:, :] = sums
    ones_row[...] = jnp.where(iota(ones_row.shape, 0) == 0, 1.0, 0.0).astype(BF16)
    for load in loads[:4]:
        load.wait()
    wta[...] = transposed(eye, wq[...])
    wtb[...] = transposed(eye, wv[...])
    has_up = jnp.where(band > 0, 1.0, 0.0)

    @pl.loop(0, WINDOWS)
    def _(window):
        at = pl.multiple_of(window * QUERIES, QUERIES)
        padded_at = pl.multiple_of(window * QUERIES + TILE, TILE)
        low = start_window(tok, embed_rows, window).astype(BF16)
        low_t = transposed(eye, low)
        xt[:, pl.ds(at, QUERIES)] = low_t
        q_low = dot(wta[...], low_t).astype(BF16)
        store_pairs(keys, padded_at, dot(low, wk[...]).astype(BF16))
        store_heads(vt, padded_at, dot(wtb[...], low_t).astype(BF16))
        qt[:, pl.ds(at, QUERIES)] = q_low * BF16(0.125)
        qs[:, pl.ds(at, QUERIES)] = (q_low.astype(F32) * (0.125 * LOG2_E)).astype(BF16)

    def prepare_upper(window):
        @pl.when(band > 0)
        def _():
            up_copy(window).wait_recv()

        at = pl.multiple_of(window * QUERIES, QUERIES)
        padded_at = pl.multiple_of(window * QUERIES + TILE, TILE)
        upper = (start_window(side, embed_rows, window) * has_up).astype(BF16)
        upper_t = transposed(eye, upper)
        xut[:, pl.ds(at, QUERIES)] = upper_t
        store_pairs(keys_up, padded_at, dot(upper, wk[...]).astype(BF16))
        store_heads(vt_up, padded_at, dot(wtb[...], upper_t).astype(BF16))

    first_block = place_ref[0, 0] > 0
    row_limit = width_ref[0, 0]
    mask_shape = (SPAN, QUERIES)
    memory, query = iota(mask_shape, 0), iota(mask_shape, 1)
    memory_col = (memory // TILE) * FLANK_COLS + memory % FLANK_COLS - FLANK_COLS
    query_col = (query // TILE) * FLANK_COLS + query % FLANK_COLS
    memory_row = (memory % TILE) // FLANK_COLS
    query_row = (query % TILE) // FLANK_COLS

    def prepare_masks(window):
        column_at = memory_col + window * BLOCK_COLS
        inside = (column_at >= 0) & (column_at < row_limit)
        earlier = (memory_row < query_row) | ((memory_row == query_row) & (memory_col <= query_col))
        itself = (memory_row == query_row) & (memory_col == query_col)
        bias_low[...] = jnp.where((inside & earlier) | itself, 0.0, big_negative)
        first = iota(bias_up.shape, 1) == 0
        closed = jnp.where(inside[:, 0:128] & first_block, 0.0, big_negative)
        bias_up[...] = jnp.where(first, closed, 0.0).astype(BF16)

    def e_out(window, half):
        slot = window % 2
        return pltpu.make_async_copy(
            hd.at[slot, pl.ds(half * 2 * SPAN, 2 * SPAN), pl.ds(0, 4 * QUERIES)],
            e_h.at[window, half],
            e_out_sem.at[slot, half],
        )

    prepare_upper(0)

    @pl.loop(0, WINDOWS)
    def _(window):
        @pl.when(window < WINDOWS - 1)
        def _():
            prepare_upper(window + 1)

        prepare_masks(window)

        @pl.when(window > 1)
        def _():
            for half in range(2):
                e_out(window - 2, half).wait()

        slot = window % 2
        at = pl.multiple_of(window * QUERIES, QUERIES)
        here, span = pl.ds(at, QUERIES), pl.ds(at, SPAN)

        def scores(head):
            pair = head // 2
            q_head = head_of_pair(qs[pair * 128 : pair * 128 + 128, here], head % 2)
            upper = dot(
                jnp.concatenate([keys_up[pair, span, :], bias_up[...]], axis=1),
                jnp.concatenate([q_head, ones_row[...]], axis=0),
            )
            lower = dot(keys[pair, span, :], q_head) + bias_low[...]
            shape = (SPAN // 8, 8, QUERIES)
            top = jnp.maximum(
                jnp.max(upper.reshape(shape), axis=0), jnp.max(lower.reshape(shape), axis=0)
            )
            return upper, lower, jnp.max(top, axis=0, keepdims=True)

        def mix(head, e_up, e_low):
            mixed = dot(vt_up[head, :, span], e_up) + dot(vt[head, :, span], e_low)
            inverse = 1.0 / mixed[HEAD_DIM : HEAD_DIM + 1]
            rows = slice(head * HEAD_DIM, head * HEAD_DIM + HEAD_DIM)
            ot[rows, here] = (mixed[0:HEAD_DIM] * inverse).astype(BF16)
            inv[head : head + 1, here] = inverse

        current, raised = scores(0), None
        for head in range(8):
            upcoming = scores(head + 1) if head < 7 else None
            upper, lower, peak = current
            e_up = jnp.exp2(upper - peak).astype(BF16)
            e_low = jnp.exp2(lower - peak).astype(BF16)
            at_row, at_lane = head % 2 * 2 * SPAN, head // 2 * QUERIES
            hd[slot, at_row : at_row + SPAN, at_lane : at_lane + QUERIES] = e_up
            hd[slot, at_row + SPAN : at_row + 2 * SPAN, at_lane : at_lane + QUERIES] = e_low
            if head > 0:
                mix(head - 1, *raised)
            raised = (e_up, e_low)
            current = upcoming
        mix(7, *raised)
        for half in range(2):
            e_out(window, half).start()

    loads[7].start()
    for load in loads[4:7]:
        load.wait()
    wta[...] = transposed(eye, wo[...])
    wit[...] = transposed(eye, wi[...])
    wbt[...] = transposed(eye, wb[...])
    for index, ref in enumerate((bb_ref, g1_ref, s1_ref, g2_ref, s2_ref)):
        cols[index] = column(eye, ref[...].reshape(1, -1)).astype(BF16)
    bi_col[...] = column(eye, bi_ref[...].reshape(1, -1)).astype(BF16)
    acc[...] = jnp.zeros_like(acc)
    for window in range(WINDOWS - 2, WINDOWS):
        for half in range(2):
            e_out(window, half).wait()
    loads[7].wait()
    hl, dh = hd.at[0], hd.at[1]
    heads = width // HEAD_DIM

    def broadcast(index):
        return wide(cols[index].astype(F32))

    def gather(index, value):
        blocks = pl.ds(index * width // 128, width // 128)
        acc[blocks] += halves(value).reshape(width // 128, 128, 128)

    def out_copy(window):
        columns = pl.ds(pl.multiple_of(window * BLOCK_COLS, BLOCK_COLS), BLOCK_COLS)
        return pltpu.make_async_copy(
            tok.at[:, columns, :], out_h.at[:, columns, :], out_sem.at[window]
        )

    part = 256
    parts = [slice(at, at + part) for at in range(0, ff, part)]

    @pl.loop(0, WINDOWS)
    def _(window):
        here = pl.ds(pl.multiple_of(window * QUERIES, QUERIES), QUERIES)
        raw = raw_window(tok, window)
        embed = embed_window(embed_rows, window)
        start = jnp.concatenate(
            [
                dot_nt(eye, raw[:, half * 256 : half * 256 + 256])
                + dot_nt(eye, embed[:, half * 256 : half * 256 + 256])
                for half in range(2)
            ],
            axis=0,
        )
        n1, inv1 = norm_stats(start + dot(wta[...], ot[:, here]))
        y1 = n1 * broadcast(1) + broadcast(2)
        low = y1.astype(BF16)
        n1_buf[...] = n1
        cols_a[:, 0:HEAD_DIM, here] = low.reshape(heads, HEAD_DIM, QUERIES)

        upcoming = dot(wit[parts[0], :], low)
        for index, rows in enumerate(parts):
            u = upcoming + wide(bi_col[rows, :].astype(F32))
            if index + 1 < len(parts):
                upcoming = dot(wit[parts[index + 1], :], low)
            active, slope = gelu_and_slope(u)
            hl[rows, here] = active.astype(BF16)
            dh[rows, here] = slope.astype(BF16)

        f = dot(wbt[...], hl[:, here]) + broadcast(0)
        n2, inv2 = norm_stats(n1_buf[...] * broadcast(1) + broadcast(2) + f)
        g2 = broadcast(3)
        result = (n2 * g2 + broadcast(4)).astype(BF16)
        result = dot_nt(eye, result).astype(BF16)
        raw_cot = raw_window(side, window)
        for half in range(2):
            at = pl.multiple_of((2 * window + half) * FLANK_COLS, FLANK_COLS)
            tok[:, pl.ds(at, FLANK_COLS), :] = result[half * TILE : half * TILE + TILE].reshape(
                BLOCK_ROWS, FLANK_COLS, -1
            )
        cot = jnp.concatenate(
            [dot_nt(eye, raw_cot[:, half * 256 : half * 256 + 256]) for half in range(2)], axis=0
        )
        gather(0, cot * n2)
        gather(1, cot)
        dr2 = norm_back(n2, inv2, cot, g2)
        df_low = dr2.astype(BF16)
        cols_b[:, 0:HEAD_DIM, here] = df_low.reshape(heads, HEAD_DIM, QUERIES)

        upcoming = dot(wb[parts[0], :], df_low)
        for index, rows in enumerate(parts):
            current = upcoming
            if index + 1 < len(parts):
                upcoming = dot(wb[parts[index + 1], :], df_low)
            dh[rows, here] = (current * dh[rows, here].astype(F32)).astype(BF16)

        dy1 = dr2 + dot(wi[...], dh[:, here])
        n1 = n1_buf[...]
        gather(2, dy1 * n1)
        gather(3, dy1)
        dr1 = norm_back(n1, inv1, dy1, broadcast(1))
        da_low = dr1.astype(BF16)
        da[:, here] = da_low
        grad_o = dot(wo[...], da_low)
        product = grad_o * ot[:, here].astype(F32)
        for head in range(heads):
            rows = slice(head * HEAD_DIM, head * HEAD_DIM + HEAD_DIM)
            inverse = inv[head : head + 1, here]
            d_o[rows, here] = (grad_o[rows] * inverse).astype(BF16)
            dd[head : head + 1, here] = jnp.sum(product[rows], axis=0, keepdims=True) * inverse
        out_copy(window).start()

    small_buf[0] = jnp.zeros(small_buf.shape[1:], F32)
    ones = jnp.ones((8, 256), BF16)
    for index, row in enumerate((0, 1, 3, 4)):
        value = acc[pl.ds(index * width // 128, width // 128)].reshape(width, 128)
        high = value.astype(BF16)
        split = jnp.concatenate([high, (value - high.astype(F32)).astype(BF16)], axis=1)
        small_buf[0, row : row + 1, :] = dot_nt(ones, split)[0:1]

    def e_in(pair, part, window, half):
        if window < 4:
            target = ww.at[0, pl.ds(window * SPAN, SPAN), pl.ds(half * QUERIES, QUERIES)]
        else:
            at = (2 * (window - 4) + half) * QUERIES
            target = wt.at[1, :, pl.ds(at, QUERIES)]
        source = e_h.at[
            window, half, pl.ds(part * SPAN, SPAN), pl.ds(pl.multiple_of(pair * QUERIES, QUERIES), QUERIES)
        ]
        return pltpu.make_async_copy(source, target, e_in_sem.at[window, half])

    def e_tile(window, half, first, last):
        if window < 4:
            return ww[0, window * SPAN + first : window * SPAN + last, half * QUERIES : (half + 1) * QUERIES]
        at = (2 * (window - 4) + half) * QUERIES
        return wt[1, first:last, at : at + QUERIES]

    items = [(window, half) for window in range(WINDOWS) for half in range(2)]
    for window, half in items:
        e_in(0, 0, window, half).start()

    qkv_at = 3 * width
    gback, gin = ww.at[1], wt.at[0]
    gout = wt.at[1, :, pl.ds(4 * QUERIES, width)]
    sum_back = Reduction(
        gback, (ff, width), back_recv, back_later, back_across, back_parts if back_split else None,
        lambda k: back_ss.at[k], lambda k: back_rs.at[k], place,
    )
    sum_out = Reduction(
        gout, (width, width), out_recv, out_later, out_across, None,
        lambda k: go_ss.at[k], lambda k: go_rs.at[k], place,
    )
    sum_in = Reduction(
        gin, (width, ff), in_recv, in_later, in_across, in_parts if in_split else None,
        lambda k: in_ss.at[k], lambda k: in_rs.at[k], place,
    )

    def write_in(value, columns=slice(None)):
        gin_ref[:, columns] = value

    def write_back(value, columns=slice(None)):
        gback_ref[:, columns] = value

    def write_out(value):
        gout_ref[...] = value

    def write_qkv(pair):
        def write(value):
            qkv_ref[pair] = value

        return write

    def sum_qkv(pair):
        return Reduction(
            hd.at[1, pl.ds(qkv_at, width), pl.ds(pl.multiple_of(pair * 384, 128), 384)],
            (width, 384), qkv_recv.at[pair], qkv_later.at[pair], qkv_across.at[pair], None,
            lambda k: qkv_ss.at[pair, k], lambda k: qkv_rs.at[pair, k], place,
        )

    sum_small = SmallSum(small_buf, small_recv, small_ss, small_rs, place)
    share, back_share = width // size, ff // size
    ones_rows = jnp.where(iota((16, LEN), 0) == 0, 1.0, 0.0).astype(BF16)

    @pl.loop(0, ff // 256)
    def _(index):
        rows = pl.ds(pl.multiple_of(index * 256, 256), 256)
        df = cols_b[:, 0:HEAD_DIM, 0:LEN].reshape(width, LEN)
        grad = dot_nt(jnp.concatenate([hl[rows, :], ones_rows], axis=0), df)
        shares = 256 // back_share
        for piece in range(shares):
            at = reversed_bits(index * shares + piece, size) * back_share
            gback[pl.ds(pl.multiple_of(at, back_share), back_share), :] = grad[
                piece * back_share : (piece + 1) * back_share
            ].astype(BF16)
        small_buf[0, 2:3, :] = grad[256:257]

    sum_back.start(0)

    def scatter_shares(ref, grad, first_lane):
        low = grad.astype(BF16)
        for owner in range(size):
            at = pl.multiple_of(reversed_bits(owner, size) * share, share)
            ref[pl.ds(at, share), first_lane : first_lane + grad.shape[1]] = low[
                owner * share : owner * share + share
            ]

    scatter_shares(gout, dot_nt(ot[...], da[...]), 0)
    sum_out.start(0)
    step_back = Steps(sum_back, write_back)
    step_out = Steps(sum_out, write_out)
    step_in = Steps(sum_in, write_in)

    yl_rows = jnp.concatenate([cols_a[:, 0:HEAD_DIM, 0:LEN].reshape(width, LEN), ones_rows], axis=0)
    for index in range(ff // 256):
        at = index * 256
        grad = dot_nt(yl_rows, dh[at : at + 256, :])
        scatter_shares(gin, grad[0:width], at)
        row, lane = 5 + at // width, at % width
        small_buf[0, row : row + 1, lane : lane + 256] = grad[width : width + 1]
        if index == 1:
            step_back()
        if index == 3:
            step_out()
    sum_in.start(0)

    vals, vals_up, kt, kt_up = rows_a, rows_b, cols_a, cols_b
    w3 = ot
    d3, w2 = hd.at[0, pl.ds(0, 3 * width)], hd.at[0, pl.ds(3 * width, width), pl.ds(0, 2 * width)]
    d2, dxu = hd.at[1, pl.ds(0, 2 * width)], hd.at[1, pl.ds(2 * width, width)]
    wtb[...] = transposed(eye, wk[...])
    for pair in range(4):
        lanes = slice(pair * 128, pair * 128 + 128)
        for index, ref in enumerate((wq, wk, wv)):
            w3[:, pair * 384 + index * 128 : pair * 384 + index * 128 + 128] = ref[:, lanes]
        for index, ref in enumerate((wk, wv)):
            w2[:, pair * 256 + index * 128 : pair * 256 + index * 128 + 128] = ref[:, lanes]
    clear_pads_lanes(kt)
    clear_pads_lanes(kt_up)

    @pl.loop(0, WINDOWS)
    def _(window):
        @pl.when(window == 2)
        def _():
            step_in()

        here = pl.ds(pl.multiple_of(window * QUERIES, QUERIES), QUERIES)
        padded_at = pl.multiple_of(window * QUERIES + TILE, TILE)
        low = transposed(eye, xt[:, here])
        upper = transposed(eye, xut[:, here])
        store_pairs(vals, padded_at, dot(low, wv[...]).astype(BF16))
        store_heads(kt, padded_at, dot(wtb[...], xt[:, here]).astype(BF16))
        store_pairs(vals_up, padded_at, dot(upper, wv[...]).astype(BF16))
        store_heads(kt_up, padded_at, dot(wtb[...], xut[:, here]).astype(BF16))

    blocks = PADDED // 128

    shape = (8, LEN)
    channel = (iota(shape, 1) // TILE + iota(shape, 1) % FLANK_COLS) % 3
    chosen = jnp.where(channel == iota(shape, 0), 1.0, 0.0).astype(BF16)

    def pass_over(pair, part, v_rows, k_cols):
        for window, half in items:
            e_in(pair, part, window, half).wait()
        acc[...] = jnp.zeros_like(acc)
        feats = pl.ds(pl.multiple_of(pair * 128, 128), 128)
        follow = pair + 1
        next_pair, next_part = follow % 4, jnp.minimum(part + follow // 4, 1)

        def limits(window):
            first = TILE if window == 0 else 0
            last = SPAN - TILE if window == WINDOWS - 1 else SPAN
            return first, last

        def grad_probs(window, half):
            first, last = limits(window)
            here = slice(window * QUERIES, window * QUERIES + QUERIES)
            rows = slice(window * QUERIES + first, window * QUERIES + last)
            return dot(v_rows[pair, rows, :], head_of_pair(d_o[feats, here], half))

        def add_blocks(base, window, half, value):
            first, last = limits(window)
            rows = slice(half * HEAD_DIM, half * HEAD_DIM + HEAD_DIM)
            for at in range(first, last, 128):
                acc[base + (window * QUERIES + at) // 128, rows, :] += value[
                    :, at - first : at - first + 128
                ]

        upcoming = grad_probs(*items[0])
        for index, (window, half) in enumerate(items):
            current = upcoming
            if index + 1 < len(items):
                upcoming = grad_probs(*items[index + 1])
            first, last = limits(window)
            here = slice(window * QUERIES, window * QUERIES + QUERIES)
            span = slice(window * QUERIES + first, window * QUERIES + last)
            head = 2 * pair + half
            mine = pl.ds(pl.multiple_of(pair * 128 + half * HEAD_DIM, HEAD_DIM), HEAD_DIM)
            e = e_tile(window, half, first, last)
            ds = (e.astype(F32) * (current - dd[pl.ds(head, 1), here])).astype(BF16)
            dq = dot(k_cols[head, 0:HEAD_DIM, span], ds)
            at = pl.ds(pl.multiple_of(pair * 384 + half * HEAD_DIM, HEAD_DIM), HEAD_DIM)
            if part == 0:
                d3[at, here] = dq.astype(BF16)
            else:
                d3[at, here] = ((dq + d3[at, here].astype(F32)) * 0.125).astype(BF16)
            add_blocks(0, window, half, dot_nt(qt[mine, here], ds))
            add_blocks(blocks, window, half, dot_nt(d_o[mine, here], e))
            e_in(next_pair, next_part, window, half).start()

    def take_blocks(ref, at, base):
        for block in range(1, blocks - 1):
            ref[pl.ds(at, 128), block * 128 - 128 : block * 128] = acc[base + block].astype(BF16)

    @pl.loop(0, 4)
    def _(pair):
        pass_over(pair, 0, vals_up, kt_up)
        at = pl.multiple_of(pair * 256, 256)
        take_blocks(d2, at, 0)
        take_blocks(d2, at + 128, blocks)

        @pl.when(pair == 0)
        def _():
            step_back()
            step_out()

        @pl.when(pair == 2)
        def _():
            step_back()
            step_out()
            step_in()

        @pl.when(pair == 3)
        def _():
            step_back()

    for window in range(WINDOWS):
        here = slice(window * QUERIES, window * QUERIES + QUERIES)
        dxu[:, here] = dot(w2[...], d2[:, here]).astype(BF16)

        @pl.when(band > 0)
        def _(window=window):
            halo(window).start()

    @pl.loop(0, 4)
    def _(pair):
        pass_over(pair, 1, vals, kt)

        for turn in range(4):

            @pl.when(pair == turn)
            def _(turn=turn):
                if turn == 0:
                    step_back()
                if turn < 3:
                    step_in()
                if turn > 0:
                    sum_qkv(turn - 1).advance(0)

        at = pl.multiple_of(pair * 384, 128)
        take_blocks(d3, at + 128, 0)
        take_blocks(d3, at + 256, blocks)
        grads = dot_nt(xt[...], d3[pl.ds(at, 384), :])
        grads_up = dot_nt(xut[...], d2[pl.ds(pl.multiple_of(pair * 256, 256), 256), :])
        lanes = pl.ds(pl.multiple_of(pair * 384, 128), 128)
        low_q = grads[:, 0:128].astype(BF16)
        low_kv = (grads[:, 128:384] + grads_up).astype(BF16)
        for owner in range(size):
            rows = slice(owner * share, owner * share + share)
            to = pl.ds(pl.multiple_of(qkv_at + reversed_bits(owner, size) * share, share), share)
            hd[1, to, lanes] = low_q[rows]
            hd[1, to, pl.ds(pl.multiple_of(pair * 384 + 128, 128), 256)] = low_kv[rows]
        sum_qkv(pair).start(0)
        totals[pair] = dot_nt(chosen, d3[pl.ds(at, 384), :])

    small_buf[0, 9:12, :] = dot_nt(chosen, da[...])[0:3]
    small_buf[0, 12:15, :] = dot_nt(chosen, dxu[...])[0:3] * has_up
    for block in range(12):
        row, lane = 15 + block // 4 * 3, block % 4 * 128
        small_buf[0, row : row + 3, lane : lane + 128] = totals[
            block // 3, 0:3, block % 3 * 128 : block % 3 * 128 + 128
        ]
    sum_small.start(0)
    for window, half in items:
        e_in(0, 1, window, half).wait()

    @pl.when(band == size - 1)
    def _():
        below[...] = jnp.zeros_like(below)

    for window in range(WINDOWS):
        out_copy(window).wait()

    def gt_copy(window):
        columns = pl.ds(pl.multiple_of(window * BLOCK_COLS, BLOCK_COLS), BLOCK_COLS)
        return pltpu.make_async_copy(
            side.at[:, columns, :], gt_h.at[:, columns, :], out_sem.at[window]
        )

    @pl.loop(0, WINDOWS)
    def _(window):
        @pl.when(band < size - 1)
        def _():
            halo(window).wait_recv()

        here = pl.ds(pl.multiple_of(window * QUERIES, QUERIES), QUERIES)
        dx = da[:, here].astype(F32) + dot(w3[...], d3[:, here]) + below[:, here].astype(F32)
        rows = dot_nt(eye, dx.astype(BF16)).astype(BF16)
        for half in range(2):
            at = pl.multiple_of((2 * window + half) * FLANK_COLS, FLANK_COLS)
            side[:, pl.ds(at, FLANK_COLS), :] = rows[half * TILE : half * TILE + TILE].reshape(
                BLOCK_ROWS, FLANK_COLS, -1
            )
        gt_copy(window).start()

        @pl.when(window == 0)
        def _():
            sum_qkv(0).advance(1)

        @pl.when(window == 1)
        def _():
            sum_qkv(3).advance(0)
            sum_small.advance(0)

        @pl.when(window == 2)
        def _():
            sum_qkv(1).advance(1)

        @pl.when(window == 3)
        def _():
            sum_qkv(2).advance(1)
            step_back.last()

        @pl.when(window == 4)
        def _():
            step_out.last()
            step_in.last()
            sum_qkv(0).finish(write_qkv(0))

    sum_qkv(1).finish(write_qkv(1))
    sum_qkv(3).advance(1)
    sum_small.advance(1)
    sum_qkv(2).finish(write_qkv(2))
    sum_qkv(3).finish(write_qkv(3))
    small = sum_small.finish()
    small_ref[...] = small[0:16]
    own = w3[pl.ds(pl.multiple_of(band * share, share), share), :]
    parts = jnp.concatenate([small[15:18], small[18:21], small[21:24]], axis=1)
    high = parts.astype(BF16)
    low = (parts - high.astype(F32)).astype(BF16)
    embed = dot_nt(jnp.concatenate([high, low], axis=0), own)
    rest = small[9:12] + small[12:15]
    mine = 0.0
    for owner in range(size):
        mine = mine + jnp.where(band == owner, rest[:, owner * share : owner * share + share], 0.0)
    small_ref[9:12, 0:share] = mine + embed[0:3] + embed[3:6]

    for window in range(WINDOWS):
        gt_copy(window).wait()

    @pl.when(band > 0)
    def _():
        for window in range(WINDOWS):
            halo(window).wait_send()

    @pl.when(band < size - 1)
    def _():
        for window in range(WINDOWS):
            up_copy(window).wait_send()


def emit_kernel(
    out_in, gt_in, qkv_in, gin_in, gback_in, gout_in, small_in,
    out_h, gt_h, gq, gk, gv, gout, gin, gbi, gback, gbb, gg1, gs1, gg2, gs2, gemb,
    qkv, small, large, sems, large_sems,
    *, size,
):
    pairs = (
        (small_in, small), (qkv_in, qkv), (gback_in, gback), (gin_in, gin), (gout_in, gout),
    )
    moves = []
    for index, (source, target) in enumerate(((out_in, out_h), (gt_in, gt_h))):
        for row in range(0, BLOCK_ROWS, 2):
            rows, held = pl.ds(row, 2), large.at[index, pl.ds(row, 2)]
            sem = index * 4 + row // 2
            moves.append(
                (
                    pltpu.make_async_copy(source.at[rows], held, large_sems.at[0, sem]),
                    pltpu.make_async_copy(held, target.at[rows], large_sems.at[1, sem]),
                )
            )
    for load, _ in moves:
        load.start()
    copies = [
        pltpu.make_async_copy(source, target, sems.at[index])
        for index, (source, target) in enumerate(pairs)
    ]
    for copy in copies:
        copy.start()
    for load, store in moves:
        load.wait()
        store.start()
    copies[0].wait()
    band = lax.axis_index("band")
    share, back_share = gq.shape[0], gbi.shape[0]
    mine = 0.0
    for owner in range(size):
        mine = mine + jnp.where(band == owner, small[:, owner * share : owner * share + share], 0.0)
    for row, ref in ((2, gbb), (3, gg1), (4, gs1), (0, gg2), (1, gs2)):
        ref[...] = mine[row : row + 1].reshape(-1)
    gemb[...] = small[9:12, 0:share]
    per_row = small.shape[1] // back_share
    bias = 0.0
    for owner in range(size):
        at = owner % per_row * back_share
        row = small[5 + owner // per_row : 6 + owner // per_row, at : at + back_share]
        bias = bias + jnp.where(band == owner, row, 0.0)
    gbi[...] = bias.reshape(-1)
    copies[1].wait()
    for pair in range(4):
        for index, ref in enumerate((gq, gk, gv)):
            ref[:, pair * 128 : pair * 128 + 128] = qkv[pair, :, index * 128 : index * 128 + 128]
    for copy in copies[2:]:
        copy.wait()
    for _, store in moves:
        store.wait()


def shards(
    tokens, row_place, row_width, cotangent, chan_embed, w_query, w_key, w_value, w_out, w_in,
    bias_in, w_back, bias_back, gain_first, shift_first, gain_second, shift_second,
):
    width = tokens.shape[3]
    ff = w_in.shape[1]
    tok = tokens.reshape(BLOCK_ROWS, ROW_POS, width)
    cot = cotangent.reshape(BLOCK_ROWS, ROW_POS, width)
    shape = jax.ShapeDtypeStruct
    size, groups = lax.axis_size("band"), lax.axis_size("grp")
    dma = pltpu.SemaphoreType.DMA
    share, back_share = width // size, ff // size
    stages = size // 2 + 2 * groups
    in_split = ff // groups % 128 == 0
    back_split = width // groups % 128 == 0
    rows = shape((BLOCK_ROWS, ROW_POS, width), BF16)

    def later(split, total_rows, columns):
        return pltpu.VMEM((total_rows // 2, columns // groups if split else columns), BF16)

    def across(split, total_rows, columns):
        if split:
            return pltpu.VMEM((groups - 1, total_rows // 2, columns // groups), BF16)
        return pltpu.VMEM((groups, total_rows // size, columns), BF16)

    flat = pltpu.VMEM((width, LEN), BF16)
    out, gt, _, qkv, gin, gback, gout, small = pl.pallas_call(
        functools.partial(
            layer_kernel, size=size, groups=groups, in_split=in_split, back_split=back_split
        ),
        name="layer_forward_and_back",
        out_shape=(
            rows,
            rows,
            shape((WINDOWS, 2, 2 * SPAN, 4 * QUERIES), BF16),
            shape((4, share, 384), F32),
            shape((share, ff), F32),
            shape((back_share, width), F32),
            shape((share, width), F32),
            shape((16, width), F32),
        ),
        in_specs=[smem()] * 2 + [vmem()] * 7 + [hbm()] * 8,
        out_specs=(hbm(),) * 3 + (vmem(),) * 5,
        scratch_shapes=[
            pltpu.VMEM(rows.shape, BF16),
            pltpu.VMEM(rows.shape, BF16),
            pltpu.VMEM((4, width, width), BF16),
            pltpu.VMEM((width, width), BF16),
            pltpu.VMEM((width, width), BF16),
            pltpu.VMEM((2, ff, width), BF16),
            pltpu.VMEM((2, width, ff), BF16),
            flat,
            flat,
            flat,
            flat,
            flat,
            pltpu.VMEM((4, PADDED, 128), BF16),
            pltpu.VMEM((4, PADDED, 128), BF16),
            pltpu.VMEM((8, HEAD_DIM + 16, PADDED), BF16),
            pltpu.VMEM((8, HEAD_DIM + 16, PADDED), BF16),
            pltpu.VMEM((2, ff, LEN), BF16),
            pltpu.VMEM((SPAN, QUERIES), F32),
            pltpu.VMEM((SPAN, 128), BF16),
            pltpu.VMEM((128, QUERIES), BF16),
            pltpu.VMEM((ROW_POS, width), BF16),
            pltpu.VMEM((5, width, 128), BF16),
            pltpu.VMEM((ff, 128), BF16),
            pltpu.VMEM((width, QUERIES), F32),
            flat,
            pltpu.VMEM((2 * PADDED // 128, 128, 128), F32),
            flat,
            pltpu.VMEM((8, LEN), F32),
            pltpu.VMEM((8, LEN), F32),
            pltpu.VMEM((width // 2, ff), BF16),
            later(in_split, width, ff),
            across(in_split, width, ff),
            pltpu.VMEM((groups, share, ff // groups), F32),
            pltpu.VMEM((ff // 2, width), BF16),
            later(back_split, ff, width),
            across(back_split, ff, width),
            pltpu.VMEM((groups, back_share, width // groups), F32),
            pltpu.VMEM((width // 2, width), BF16),
            pltpu.VMEM((width // 2, width), BF16),
            pltpu.VMEM((groups, share, width), BF16),
            pltpu.VMEM((4, width // 2, 384), BF16),
            pltpu.VMEM((4, width // 2, 384), BF16),
            pltpu.VMEM((4, groups, share, 384), BF16),
            pltpu.VMEM((3, 24, width), F32),
            pltpu.VMEM((size // 2 + groups - 1, 24, width), F32),
            pltpu.VMEM((4, 8, 384), F32),
            dma((8,)),
            dma((2, 2)),
            dma((WINDOWS, 2)),
            dma((WINDOWS,)),
            dma((WINDOWS,)),
            dma((WINDOWS,)),
            dma((WINDOWS,)),
            dma((WINDOWS,)),
            dma((stages,)),
            dma((stages,)),
            dma((stages,)),
            dma((stages,)),
            dma((stages,)),
            dma((stages,)),
            dma((4, stages)),
            dma((4, stages)),
            dma((stages,)),
            dma((stages,)),
        ],
        compiler_params=pltpu.CompilerParams(
            vmem_limit_bytes=LIMIT, collective_id=0, has_side_effects=True
        ),
    )(
        row_place, row_width, chan_embed, bias_in, bias_back, gain_first, shift_first, gain_second,
        shift_second, tok, cot, w_query, w_key, w_value, w_out, w_in, w_back,
    )
    vector = shape((share,), F32)
    square = shape((share, width), F32)
    out, gt, gq, gk, gv, gout, gin, gbi, gback, gbb, gg1, gs1, gg2, gs2, gemb = pl.pallas_call(
        functools.partial(emit_kernel, size=size),
        name="emit_shares",
        out_shape=(
            rows, rows, square, square, square, square, shape((share, ff), F32),
            shape((back_share,), F32), shape((back_share, width), F32),
            vector, vector, vector, vector, vector, shape((3, share), F32),
        ),
        in_specs=[hbm()] * 7,
        out_specs=(hbm(),) * 2 + (vmem(),) * 3 + (vmem(), vmem(), vmem(), vmem()) + (vmem(),) * 6,
        scratch_shapes=[
            pltpu.VMEM((4, share, 384), F32),
            pltpu.VMEM((16, width), F32),
            pltpu.VMEM((2,) + rows.shape, BF16),
            dma((5,)),
            dma((2, 8)),
        ],
        compiler_params=pltpu.CompilerParams(vmem_limit_bytes=LIMIT),
    )(out, gt, qkv, gin, gback, gout, small)
    return (
        out.reshape(tokens.shape),
        gt.reshape(tokens.shape),
        gq, gk, gv, gout, gin, gbi, gback, gbb, gg1, gs1, gg2, gs2, gemb,
    )


def solution(mesh):
    tall = P("grp", "band", None, None)
    return jax.shard_map(
        shards,
        mesh=mesh,
        in_specs=(tall, P("grp", "band"), P("grp", "band"), tall) + (P(),) * 13,
        out_specs=(tall, tall)
        + (P("band", None),) * 5
        + (P("band"), P("band", None))
        + (P("band"),) * 5
        + (P(None, "band"),),
        check_vma=False,
    )
```

```python
import functools

import jax
import jax.numpy as jnp
from jax import lax
from jax.experimental import pallas as pl
from jax.experimental.pallas import tpu as pltpu
from jax.sharding import PartitionSpec as P

HEAD_DIM = 64
ROW_POS = 192
BLOCK_ROWS = 8
BLOCK_COLS = 32
FLANK_COLS = 16
WINDOWS = ROW_POS // BLOCK_COLS
BLOCKS = ROW_POS // FLANK_COLS
TILE = BLOCK_ROWS * FLANK_COLS
QUERIES = 2 * TILE
SPAN = 4 * TILE
LEN = BLOCK_ROWS * ROW_POS
PADDED = LEN + 2 * TILE

norm_eps = 1e-06
big_negative = -1e30
F32 = jnp.float32
BF16 = jnp.bfloat16
LOG2_E = 1.4426950408889634
GELU_SCALE = 0.7978845608028654
GELU_CUBE = 0.044715


def dot(left, right):
    return jnp.dot(left, right, preferred_element_type=F32)


def dot_nt(left, right):
    return lax.dot_general(left, right, (((1,), (1,)), ((), ())), preferred_element_type=F32)


def iota(shape, dim):
    return lax.broadcasted_iota(jnp.int32, shape, dim)


def identity(size):
    return jnp.where(iota((size, size), 0) == iota((size, size), 1), 1.0, 0.0).astype(BF16)


def transposed(eye, value):
    step = eye.shape[0]
    parts = [
        dot_nt(eye, value[:, at : at + step]).astype(BF16) for at in range(0, value.shape[1], step)
    ]
    return jnp.concatenate(parts, axis=0)


def column(eye, row):
    step = eye.shape[0]
    ones = jnp.ones((128, step), BF16)
    parts = [
        dot_nt(jnp.where(eye > 0, row[:, at : at + step], 0).astype(BF16), ones)
        for at in range(0, row.shape[1], step)
    ]
    return jnp.concatenate(parts, axis=0)


def wide(value):
    return jnp.concatenate([value, value], axis=1)


def halves(value):
    return value[:, :128] + value[:, 128:]


def fill_embed(embed_ref, rows_ref):
    embed = embed_ref[...].astype(F32)
    channel = lax.rem(iota(rows_ref.shape, 0), 3)
    rows_ref[...] = jnp.where(
        channel == 0, embed[0:1], jnp.where(channel == 1, embed[1:2], embed[2:3])
    ).astype(BF16)


def block_rows(rows_ref, block):
    return rows_ref[:, pl.ds(pl.multiple_of(block * FLANK_COLS, FLANK_COLS), FLANK_COLS), :]


def raw_window(rows_ref, window):
    parts = [block_rows(rows_ref, 2 * window + half).reshape(TILE, -1) for half in range(2)]
    return jnp.concatenate(parts, axis=0)


def embed_window(embed_rows, window):
    parts = []
    for half in range(2):
        at = pl.multiple_of((2 * window + half) % 3 * FLANK_COLS, FLANK_COLS)
        part = embed_rows[pl.ds(at, FLANK_COLS), :][None]
        parts.append(jnp.broadcast_to(part, (BLOCK_ROWS,) + part.shape[1:]).reshape(TILE, -1))
    return jnp.concatenate(parts, axis=0)


def start_window(rows_ref, embed_rows, window):
    return raw_window(rows_ref, window).astype(F32) + embed_window(embed_rows, window).astype(F32)


def norm_stats(value):
    center = value - jnp.mean(value, axis=0, keepdims=True)
    spread = jnp.mean(center * center, axis=0, keepdims=True)
    inverse = lax.rsqrt(spread + norm_eps)
    return center * inverse, inverse


def norm_back(normed, inverse, grad, gain):
    scaled = grad * gain
    first = jnp.mean(scaled, axis=0, keepdims=True)
    second = jnp.mean(scaled * normed, axis=0, keepdims=True)
    return (scaled - first - normed * second) * inverse


def vmem():
    return pl.BlockSpec(memory_space=pltpu.VMEM)


def smem():
    return pl.BlockSpec(memory_space=pltpu.SMEM)


def hbm():
    return pl.BlockSpec(memory_space=pl.ANY)


LIMIT = 62 * 1024 * 1024


def head_of_pair(value, half):
    keep = (iota(value.shape, 0) // HEAD_DIM) == half
    return jnp.where(keep, value, jnp.zeros_like(value))


def clear_pads_rows(ref):
    pad = jnp.zeros((ref.shape[0], TILE, ref.shape[2]), ref.dtype)
    ref[:, 0:TILE, :] = pad
    ref[:, PADDED - TILE : PADDED, :] = pad


def reversed_bits(index, count):
    place, bit = 0, 1
    while bit < count:
        place = place + (index // bit) % 2 * (count // (2 * bit))
        bit *= 2
    return place


def levels(count):
    return count.bit_length() - 1


def first_share(band, bits, count):
    start = 0
    for level in range(bits):
        start = start + (band // (1 << level)) % 2 * (count >> (level + 1))
    return start


class Reduction:
    def __init__(
        self, buf, shape, recv, later, across, gathered, send_sem, recv_sem, place, direct=False
    ):
        self.buf, self.recv, self.later = buf, recv, later
        self.across, self.gathered = across, gathered
        self.send_sem, self.recv_sem = send_sem, recv_sem
        self.band, self.grp, self.size, self.groups = place
        self.depth = depth = levels(self.size)
        self.rows = shape[0] // self.size
        halvings = [("halve", bit) for bit in range(1, depth)]
        self.stages = [("halve", 0)]
        if gathered is not None:
            self.stages += [("split", 1)] + halvings + [("gather", depth)]
        elif direct:
            self.stages += [("direct", 1), ("sum", depth)]
        else:
            self.stages += halvings + [("sum", depth)]
        self.part = shape[1] // self.groups
        self.dtype = buf.dtype

    def start_of(self, bits):
        return first_share(self.band, bits, self.size)

    def columns_of(self, member):
        return pl.ds(pl.multiple_of(member * self.part, 128), self.part)

    def columns(self, stage):
        split = [kind for kind, _ in self.stages[:stage]].count("split")
        return self.columns_of(self.grp) if split else slice(None)

    def shares(self, first, count=1):
        return pl.ds(pl.multiple_of(first * self.rows, self.rows), count * self.rows)

    def landing(self, bits):
        return self.later if bits else self.recv

    def landing_rows(self, bits, index, count):
        return self.shares(index + (self.size >> (bits + 1) if bits else 0), count)

    def copies(self, stage):
        kind, bits = self.stages[stage]
        columns = self.columns(stage)
        pieces = []
        if kind == "halve":
            half = self.size >> (bits + 1)
            bit = (self.band // (1 << bits)) % 2
            pieces.append(
                (
                    self.buf.at[self.shares(self.start_of(bits) + (1 - bit) * half, half), columns],
                    self.landing(bits).at[self.landing_rows(bits, 0, half)],
                    bits,
                    (self.band + (1 << bits) * (1 - 2 * bit), self.grp),
                )
            )
        if kind == "direct":
            for step in range(1, self.size // 2):
                partner = (self.band + 2 * step) % self.size
                source = self.buf.at[self.shares(reversed_bits(partner, self.size))]
                place = (partner, self.grp)
                pieces.append((source, self.later.at[self.shares(step)], step, place))
        for step in range(1, self.groups):
            partner = (self.grp + step) % self.groups
            place = (self.band, partner)
            if kind == "sum":
                source, target = self.buf.at[self.shares(self.start_of(bits))], self.across.at[step]
                pieces.append((source, target, self.size // 2 + step - 1, place))
            if kind == "split":
                rows = self.shares(self.start_of(bits), self.size >> bits)
                source = self.buf.at[rows, self.columns_of(partner)]
                pieces.append((source, self.across.at[step - 1], self.depth + step - 1, place))
            if kind == "gather":
                source, target = self.gathered.at[0], self.gathered.at[step]
                pieces.append((source, target, self.depth + self.groups + step - 2, place))
        return [
            pltpu.make_async_remote_copy(
                src_ref=source,
                dst_ref=target,
                send_sem=self.send_sem(sem),
                recv_sem=self.recv_sem(sem),
                device_id=place,
                device_id_type=pl.DeviceIdType.MESH,
            )
            for source, target, sem, place in pieces
        ]

    def start(self, stage):
        for copy in self.copies(stage):
            copy.start()

    def advance(self, stage):
        for copy in self.copies(stage):
            copy.wait()
        kind, bits = self.stages[stage]
        if kind == "halve":
            columns = self.columns(stage)
            half, keep = self.size >> (bits + 1), self.start_of(bits + 1)

            @pl.loop(0, half)
            def _(index):
                mine = self.shares(keep + index)
                total = self.buf[mine, columns].astype(F32)
                total = total + self.landing(bits)[self.landing_rows(bits, index, 1), :].astype(F32)
                self.buf[mine, columns] = total.astype(self.dtype)
        elif kind == "direct":
            mine = self.shares(self.start_of(self.depth))
            total = self.buf[mine, :].astype(F32)
            for step in range(1, self.size // 2):
                total = total + self.later[step * self.rows : (step + 1) * self.rows, :].astype(F32)
            self.buf[mine, :] = total.astype(self.dtype)
        else:
            columns = self.columns_of(self.grp)
            keep = self.start_of(bits)

            @pl.loop(0, self.size >> bits)
            def _(index):
                mine = self.shares(keep + index)
                total = self.buf[mine, columns].astype(F32)
                for step in range(self.groups - 1):
                    total = total + self.across[step, self.shares(index), :].astype(F32)
                self.buf[mine, columns] = total.astype(self.dtype)

        if self.stages[stage + 1][0] == "gather":
            mine = self.shares(self.start_of(self.depth))
            self.gathered[0] = self.buf[mine, self.columns_of(self.grp)].astype(F32)
        self.start(stage + 1)

    def finish(self, out):
        last = len(self.stages) - 1
        for copy in self.copies(last):
            copy.wait()
        if self.stages[last][0] == "sum":
            self.across[0] = self.buf[self.shares(self.start_of(self.depth)), :]
            total = 0.0
            for member in range(self.groups):
                step = (self.grp + self.groups - member) % self.groups
                total = total + self.across[step].astype(F32)
            out(total)
        else:
            for step in range(self.groups):
                member = (self.grp + self.groups - step) % self.groups
                out(self.gathered[step], self.columns_of(member))


def store_pairs(ref, at, value):
    for pair in range(value.shape[1] // 128):
        ref[pair, pl.ds(at, value.shape[0]), :] = value[:, pair * 128 : (pair + 1) * 128]


def store_heads(ref, at, value):
    for head in range(value.shape[0] // HEAD_DIM):
        rows = slice(head * HEAD_DIM, head * HEAD_DIM + HEAD_DIM)
        ref[head, 0:HEAD_DIM, pl.ds(at, value.shape[1])] = value[rows]


def clear_pads_lanes(ref):
    pad = jnp.zeros(ref.shape[:2] + (TILE,), ref.dtype)
    ref[:, :, 0:TILE] = pad
    ref[:, :, PADDED - TILE : PADDED] = pad


def gelu_and_slope(u):
    square = u * u
    cube = (GELU_SCALE * GELU_CUBE) * square
    h = 0.5 * jnp.tanh(u * (GELU_SCALE + cube)) + 0.5
    g = u * (2.0 * GELU_SCALE + 6.0 * cube)
    return u * h, h * (1.0 + (1.0 - h) * g)


class Steps:
    def __init__(self, reduction, write):
        self.reduction, self.write, self.stage = reduction, write, 0

    def __call__(self):
        if self.stage < len(self.reduction.stages) - 1:
            self.reduction.advance(self.stage)
            self.stage += 1

    def last(self):
        while self.stage < len(self.reduction.stages) - 1:
            self()
        self.reduction.finish(self.write)


def layer_kernel(
    place_ref, width_ref, embed_ref, bi_ref, bb_ref, g1_ref, s1_ref, g2_ref, s2_ref, tok_h, cot_h, wq_h, wk_h, wv_h, wo_h, wi_h, wb_h,
    out_h, gt_h, e_h, qkv_ref, gin_ref, gback_ref, gout_ref, small_ref,
    tok, side, w4, wta, wtb, ww, wt, xt, xut, qt, ot, da, rows_a, rows_b, cols_a, cols_b, hd,
    bias_low, embed_rows, cols, bi_col, n1_buf, inv_buf, d_o, acc, below,
    inv, dd,
    in_recv, in_later, in_across, in_parts, back_recv, back_later, back_across, back_parts,
    out_recv, out_later, out_across,
    qkv_recv, qkv_later, qkv_across, small, small_buf, small_recv, small_later, small_across, embed_sum,
    load_sem, e_out_sem, e_in_sem, out_sem, up_ss, up_rs, halo_ss, halo_rs,
    in_ss, in_rs, back_ss, back_rs, go_ss, go_rs, qkv_ss, qkv_rs, small_ss, small_rs,
    *, size, groups, in_split, back_split,
):
    band, grp = lax.axis_index("band"), lax.axis_index("grp")
    place = (band, grp, size, groups)
    depth = levels(size)
    MESH = pl.DeviceIdType.MESH
    wq, wk, wv, wo = (w4.at[index] for index in range(4))
    wit, wb, wi, wbt = ww.at[0], ww.at[1], wt.at[0], wt.at[1]
    width, ff = wi_h.shape

    sources = (tok_h, wq_h, wk_h, wv_h, wo_h, wi_h, wb_h, cot_h)
    targets = (tok, wq, wk, wv, wo, wi, wb, side)
    loads = [
        pltpu.make_async_copy(source, target, load_sem.at[index])
        for index, (source, target) in enumerate(zip(sources, targets))
    ]
    for load in loads[:7]:
        load.start()
    barrier = pltpu.get_barrier_semaphore()
    odd = band % 2
    pl.semaphore_signal(barrier, inc=1, device_id=(band + 1 - 2 * odd, grp), device_id_type=MESH)
    for step in range(1, size // 2):
        pl.semaphore_signal(
            barrier, inc=1, device_id=((band + 2 * step) % size, grp), device_id_type=MESH
        )
    for step in range(1, groups):
        pl.semaphore_signal(
            barrier, inc=1, device_id=(band, (grp + step) % groups), device_id_type=MESH
        )
    beyond = (odd == 1) & (band < size - 1) | (odd == 0) & (band > 0)

    @pl.when(beyond)
    def _():
        pl.semaphore_signal(
            barrier, inc=1, device_id=(band + 2 * odd - 1, grp), device_id_type=MESH
        )

    pl.semaphore_wait(barrier, size // 2 + groups - 1 + jnp.where(beyond, 1, 0))

    def up_copy(window):
        columns = pl.ds(pl.multiple_of(window * BLOCK_COLS, BLOCK_COLS), BLOCK_COLS)
        return pltpu.make_async_remote_copy(
            src_ref=tok_h.at[:, columns, :], dst_ref=side.at[:, columns, :],
            send_sem=up_ss.at[window], recv_sem=up_rs.at[window],
            device_id=(jnp.minimum(band + 1, size - 1), grp), device_id_type=MESH,
        )

    def halo(window):
        here = pl.ds(pl.multiple_of(window * QUERIES, QUERIES), QUERIES)
        return pltpu.make_async_remote_copy(
            src_ref=dxu.at[:, here], dst_ref=below.at[:, here],
            send_sem=halo_ss.at[window], recv_sem=halo_rs.at[window],
            device_id=(jnp.maximum(band - 1, 0), grp), device_id_type=MESH,
        )

    @pl.when(band < size - 1)
    def _():
        for window in range(WINDOWS):
            up_copy(window).start()

    @pl.when(band == 0)
    def _():
        side[...] = jnp.zeros_like(side)

    keys, keys_up, vt, vt_up, qs = rows_a, rows_b, cols_a, cols_b, da
    bias_up, ones_row = d_o.at[:, pl.ds(0, 128)], d_o.at[pl.ds(0, 128), pl.ds(128, QUERIES)]
    eye = identity(256)
    fill_embed(embed_ref, embed_rows)
    clear_pads_rows(keys)
    clear_pads_rows(keys_up)
    clear_pads_lanes(vt)
    clear_pads_lanes(vt_up)
    sums = jnp.where(iota((16, PADDED), 0) == 0, 1.0, 0.0).astype(BF16)
    for head in range(8):
        vt[head, HEAD_DIM:, :] = sums
        vt_up[head, HEAD_DIM:, :] = sums
    ones_row[...] = jnp.where(iota(ones_row.shape, 0) == 0, 1.0, 0.0).astype(BF16)
    for load in loads[:4]:
        load.wait()
    wta[...] = transposed(eye, wq[...])
    wtb[...] = transposed(eye, wv[...])
    has_up = jnp.where(band > 0, 1.0, 0.0)

    @pl.loop(0, WINDOWS)
    def _(window):
        at = pl.multiple_of(window * QUERIES, QUERIES)
        padded_at = pl.multiple_of(window * QUERIES + TILE, TILE)
        low = start_window(tok, embed_rows, window).astype(BF16)
        low_t = transposed(eye, low)
        xt[:, pl.ds(at, QUERIES)] = low_t
        q_low = dot(wta[...], low_t).astype(BF16)
        store_pairs(keys, padded_at, dot(low, wk[...]).astype(BF16))
        store_heads(vt, padded_at, dot(wtb[...], low_t).astype(BF16))
        qt[:, pl.ds(at, QUERIES)] = q_low * BF16(0.125)
        qs[:, pl.ds(at, QUERIES)] = (q_low.astype(F32) * (0.125 * LOG2_E)).astype(BF16)

    def prepare_upper(window):
        @pl.when(band > 0)
        def _():
            up_copy(window).wait_recv()

        at = pl.multiple_of(window * QUERIES, QUERIES)
        padded_at = pl.multiple_of(window * QUERIES + TILE, TILE)
        upper = (start_window(side, embed_rows, window) * has_up).astype(BF16)
        upper_t = transposed(eye, upper)
        xut[:, pl.ds(at, QUERIES)] = upper_t
        store_pairs(keys_up, padded_at, dot(upper, wk[...]).astype(BF16))
        store_heads(vt_up, padded_at, dot(wtb[...], upper_t).astype(BF16))

    first_block = place_ref[0, 0] > 0
    row_limit = width_ref[0, 0]
    mask_shape = (SPAN, QUERIES)
    memory, query = iota(mask_shape, 0), iota(mask_shape, 1)
    memory_col = (memory // TILE) * FLANK_COLS + memory % FLANK_COLS - FLANK_COLS
    query_col = (query // TILE) * FLANK_COLS + query % FLANK_COLS
    memory_row = (memory % TILE) // FLANK_COLS
    query_row = (query % TILE) // FLANK_COLS

    def prepare_masks(window):
        column_at = memory_col + window * BLOCK_COLS
        inside = (column_at >= 0) & (column_at < row_limit)
        earlier = (memory_row < query_row) | ((memory_row == query_row) & (memory_col <= query_col))
        itself = (memory_row == query_row) & (memory_col == query_col)
        bias_low[...] = jnp.where((inside & earlier) | itself, 0.0, big_negative)
        first = iota(bias_up.shape, 1) == 0
        closed = jnp.where(inside[:, 0:128] & first_block, 0.0, big_negative)
        bias_up[...] = jnp.where(first, closed, 0.0).astype(BF16)

    def e_out(window, half):
        slot = window % 2
        return pltpu.make_async_copy(
            hd.at[slot, pl.ds(half * 2 * SPAN, 2 * SPAN), pl.ds(0, 4 * QUERIES)],
            e_h.at[window, half],
            e_out_sem.at[slot, half],
        )

    prepare_upper(0)

    @pl.loop(0, WINDOWS)
    def _(window):
        @pl.when(window < WINDOWS - 1)
        def _():
            prepare_upper(window + 1)

        prepare_masks(window)

        @pl.when(window > 1)
        def _():
            for half in range(2):
                e_out(window - 2, half).wait()

        slot = window % 2
        at = pl.multiple_of(window * QUERIES, QUERIES)
        here, span = pl.ds(at, QUERIES), pl.ds(at, SPAN)

        def scores(head):
            pair = head // 2
            q_head = head_of_pair(qs[pair * 128 : pair * 128 + 128, here], head % 2)
            upper = dot(
                jnp.concatenate([keys_up[pair, span, :], bias_up[...]], axis=1),
                jnp.concatenate([q_head, ones_row[...]], axis=0),
            )
            lower = dot(keys[pair, span, :], q_head) + bias_low[...]
            shape = (SPAN // 8, 8, QUERIES)
            top = jnp.maximum(
                jnp.max(upper.reshape(shape), axis=0), jnp.max(lower.reshape(shape), axis=0)
            )
            return upper, lower, jnp.max(top, axis=0, keepdims=True)

        def mix(head, e_up, e_low):
            mixed = dot(vt_up[head, :, span], e_up) + dot(vt[head, :, span], e_low)
            inverse = 1.0 / mixed[HEAD_DIM : HEAD_DIM + 1]
            rows = slice(head * HEAD_DIM, head * HEAD_DIM + HEAD_DIM)
            ot[rows, here] = (mixed[0:HEAD_DIM] * inverse).astype(BF16)
            inv[head : head + 1, here] = inverse

        current, raised = scores(0), None
        for head in range(8):
            upcoming = scores(head + 1) if head < 7 else None
            upper, lower, peak = current
            e_up = jnp.exp2(upper - peak).astype(BF16)
            e_low = jnp.exp2(lower - peak).astype(BF16)
            at_row, at_lane = head % 2 * 2 * SPAN, head // 2 * QUERIES
            hd[slot, at_row : at_row + SPAN, at_lane : at_lane + QUERIES] = e_up
            hd[slot, at_row + SPAN : at_row + 2 * SPAN, at_lane : at_lane + QUERIES] = e_low
            if head > 0:
                mix(head - 1, *raised)
            raised = (e_up, e_low)
            current = upcoming
        mix(7, *raised)
        for half in range(2):
            e_out(window, half).start()

    loads[7].start()
    for load in loads[4:7]:
        load.wait()
    wta[...] = transposed(eye, wo[...])
    wit[...] = transposed(eye, wi[...])
    wbt[...] = transposed(eye, wb[...])
    for index, ref in enumerate((bb_ref, g1_ref, s1_ref, g2_ref, s2_ref)):
        cols[index] = column(eye, ref[...].reshape(1, -1)).astype(BF16)
    bi_col[...] = column(eye, bi_ref[...].reshape(1, -1)).astype(BF16)
    acc[...] = jnp.zeros_like(acc)
    for window in range(WINDOWS - 2, WINDOWS):
        for half in range(2):
            e_out(window, half).wait()
    loads[7].wait()
    hl, dh = hd.at[0], hd.at[1]
    dr2_buf = bias_low
    heads = width // HEAD_DIM

    def broadcast(index):
        return wide(cols[index].astype(F32))

    def gather(index, value):
        blocks = pl.ds(index * width // 128, width // 128)
        acc[blocks] += halves(value).reshape(width // 128, 128, 128)

    def out_copy(window):
        columns = pl.ds(pl.multiple_of(window * BLOCK_COLS, BLOCK_COLS), BLOCK_COLS)
        return pltpu.make_async_copy(
            tok.at[:, columns, :], out_h.at[:, columns, :], out_sem.at[window]
        )

    part = 256
    parts = [slice(at, at + part) for at in range(0, ff, part)]

    def columns_at(window):
        return pl.ds(pl.multiple_of(window * QUERIES, QUERIES), QUERIES)

    def forward_start(window):
        raw = raw_window(tok, window)
        embed = embed_window(embed_rows, window)
        start = jnp.concatenate(
            [
                dot_nt(eye, raw[:, half * 256 : half * 256 + 256])
                + dot_nt(eye, embed[:, half * 256 : half * 256 + 256])
                for half in range(2)
            ],
            axis=0,
        )
        here = columns_at(window)
        n1, inv1 = norm_stats(start + dot(wta[...], ot[:, here]))
        low = (n1 * broadcast(1) + broadcast(2)).astype(BF16)
        n1_buf[window % 2] = n1.astype(BF16)
        inv_buf[window % 2, 0:1, :] = inv1
        cols_a[:, 0:HEAD_DIM, here] = low.reshape(heads, HEAD_DIM, QUERIES)
        return low

    def activate(window, index, product):
        u = product + wide(bi_col[parts[index], :].astype(F32))
        active, slope = gelu_and_slope(u)
        hl[parts[index], columns_at(window)] = active.astype(BF16)
        dh[parts[index], columns_at(window)] = slope.astype(BF16)

    def forward_end(window, f):
        y1 = n1_buf[window % 2].astype(F32) * broadcast(1) + broadcast(2)
        n2, inv2 = norm_stats(y1 + f + broadcast(0))
        g2 = broadcast(3)
        result = (n2 * g2 + broadcast(4)).astype(BF16)
        result = dot_nt(eye, result).astype(BF16)
        raw_cot = raw_window(side, window)
        for half in range(2):
            at = pl.multiple_of((2 * window + half) * FLANK_COLS, FLANK_COLS)
            tok[:, pl.ds(at, FLANK_COLS), :] = result[half * TILE : half * TILE + TILE].reshape(
                BLOCK_ROWS, FLANK_COLS, -1
            )
        cot = jnp.concatenate(
            [dot_nt(eye, raw_cot[:, half * 256 : half * 256 + 256]) for half in range(2)], axis=0
        )
        gather(0, cot * n2)
        gather(1, cot)
        dr2 = norm_back(n2, inv2, cot, g2)
        dr2_buf[...] = dr2
        cols_b[:, 0:HEAD_DIM, columns_at(window)] = dr2.astype(BF16).reshape(
            heads, HEAD_DIM, QUERIES
        )

    def back_hidden(window, index, df_low):
        here = columns_at(window)
        slope = dh[parts[index], here].astype(F32)
        dh[parts[index], here] = (dot(wb[parts[index], :], df_low) * slope).astype(BF16)

    def back_input(window, quarter):
        rows = slice(quarter * ff // 4, (quarter + 1) * ff // 4)
        return dot(wi[:, rows], dh[rows, columns_at(window)])

    def back_end(window, dy1):
        here = columns_at(window)
        n1 = n1_buf[window % 2].astype(F32)
        gather(2, dy1 * n1)
        gather(3, dy1)
        dr1 = norm_back(n1, inv_buf[window % 2, 0:1, :], dy1, broadcast(1))
        da_low = dr1.astype(BF16)
        da[:, here] = da_low
        grad_o = dot(wo[...], da_low)
        product = grad_o * ot[:, here].astype(F32)
        for head in range(heads):
            rows = slice(head * HEAD_DIM, head * HEAD_DIM + HEAD_DIM)
            inverse = inv[head : head + 1, here]
            d_o[rows, here] = (grad_o[rows] * inverse).astype(BF16)
            dd[head : head + 1, here] = jnp.sum(product[rows], axis=0, keepdims=True) * inverse

    def step(back, ahead):
        df_low, dy1 = None, None
        if back is not None:
            df_low = cols_b[:, 0:HEAD_DIM, columns_at(back)].reshape(width, QUERIES)
            dy1 = dr2_buf[...]
            for index in range(2):
                back_hidden(back, index, df_low)
        if ahead is not None:
            low = forward_start(ahead)
            upcoming = dot(wit[parts[0], :], low)
        for index in range(len(parts)):
            if ahead is not None:
                current = upcoming
                if index + 1 < len(parts):
                    upcoming = dot(wit[parts[index + 1], :], low)
            if back is not None:
                if index < 3:
                    back_hidden(back, 2 * index + 2, df_low)
                    back_hidden(back, 2 * index + 3, df_low)
                elif index < 7:
                    dy1 = dy1 + back_input(back, index - 3)
            if ahead is not None:
                activate(ahead, index, current)
        if ahead is not None:
            f = dot(wbt[...], hl[:, columns_at(ahead)])
        if back is not None:
            back_end(back, dy1)
        if ahead is not None:
            forward_end(ahead, f)
            out_copy(ahead).start()

    assert len(parts) == 8
    step(None, 0)

    @pl.loop(0, WINDOWS - 1)
    def _(window):
        step(window, window + 1)

    step(WINDOWS - 1, None)

    small[...] = jnp.zeros_like(small)
    small_buf[...] = jnp.zeros_like(small_buf)
    ones = jnp.ones((8, 256), BF16)
    for index, row in enumerate((0, 1, 3, 4)):
        value = acc[pl.ds(index * width // 128, width // 128)].reshape(width, 128)
        high = value.astype(BF16)
        split = jnp.concatenate([high, (value - high.astype(F32)).astype(BF16)], axis=1)
        small[row : row + 1, :] = dot_nt(ones, split)[0:1]

    def e_in(pair, part, window, half):
        if window < 4:
            target = ww.at[0, pl.ds(window * SPAN, SPAN), pl.ds(half * QUERIES, QUERIES)]
        else:
            at = (2 * (window - 4) + half) * QUERIES
            target = wt.at[1, :, pl.ds(at, QUERIES)]
        source = e_h.at[
            window, half, pl.ds(part * SPAN, SPAN), pl.ds(pl.multiple_of(pair * QUERIES, QUERIES), QUERIES)
        ]
        return pltpu.make_async_copy(source, target, e_in_sem.at[window, half])

    def e_tile(window, half, first, last):
        if window < 4:
            return ww[0, window * SPAN + first : window * SPAN + last, half * QUERIES : (half + 1) * QUERIES]
        at = (2 * (window - 4) + half) * QUERIES
        return wt[1, first:last, at : at + QUERIES]

    items = [(window, half) for window in range(WINDOWS) for half in range(2)]
    for window, half in items:
        e_in(0, 0, window, half).start()

    qkv_at = 3 * width
    gback, gin = ww.at[1], wt.at[0]
    gout = wt.at[1, :, pl.ds(4 * QUERIES, width)]
    sum_back = Reduction(
        gback, (ff, width), back_recv, back_later, back_across, back_parts if back_split else None,
        lambda k: back_ss.at[k], lambda k: back_rs.at[k], place,
    )
    sum_out = Reduction(
        gout, (width, width), out_recv, out_later, out_across, None,
        lambda k: go_ss.at[k], lambda k: go_rs.at[k], place,
    )
    sum_in = Reduction(
        gin, (width, ff), in_recv, in_later, in_across, in_parts if in_split else None,
        lambda k: in_ss.at[k], lambda k: in_rs.at[k], place,
    )

    def write_in(value, columns=slice(None)):
        gin_ref[:, columns] = value

    def write_back(value, columns=slice(None)):
        gback_ref[:, columns] = value

    def write_out(value):
        gout_ref[...] = value

    def write_qkv(pair):
        def write(value):
            qkv_ref[pair] = value

        return write

    def sum_qkv(pair):
        return Reduction(
            hd.at[1, pl.ds(qkv_at, width), pl.ds(pl.multiple_of(pair * 384, 128), 384)],
            (width, 384), qkv_recv.at[pair], qkv_later.at[pair], qkv_across.at[pair], None,
            lambda k: qkv_ss.at[pair, k], lambda k: qkv_rs.at[pair, k], place, True,
        )

    sum_small = Reduction(
        small_buf, (16 * size, 128), small_recv, small_later, small_across, None,
        lambda k: small_ss.at[k], lambda k: small_rs.at[k], place, True,
    )
    share, back_share = width // size, ff // size
    ones_rows = jnp.where(iota((16, LEN), 0) == 0, 1.0, 0.0).astype(BF16)

    tall = 512

    @pl.loop(0, ff // tall)
    def _(index):
        rows = pl.ds(pl.multiple_of(index * tall, tall), tall)
        df = cols_b[:, 0:HEAD_DIM, 0:LEN].reshape(width, LEN)
        grad = dot_nt(jnp.concatenate([hl[rows, :], ones_rows], axis=0), df)
        shares = tall // back_share
        for piece in range(shares):
            at = reversed_bits(index * shares + piece, size) * back_share
            gback[pl.ds(pl.multiple_of(at, back_share), back_share), :] = grad[
                piece * back_share : (piece + 1) * back_share
            ].astype(BF16)
        small[2:3, :] = grad[tall : tall + 1]

    sum_back.start(0)

    def scatter_shares(ref, grad, first_lane):
        low = grad.astype(BF16)
        for owner in range(size):
            at = pl.multiple_of(reversed_bits(owner, size) * share, share)
            ref[pl.ds(at, share), first_lane : first_lane + grad.shape[1]] = low[
                owner * share : owner * share + share
            ]

    scatter_shares(gout, dot_nt(ot[...], da[...]), 0)
    sum_out.start(0)
    step_back = Steps(sum_back, write_back)
    step_out = Steps(sum_out, write_out)
    step_in = Steps(sum_in, write_in)

    yl_rows = jnp.concatenate([cols_a[:, 0:HEAD_DIM, 0:LEN].reshape(width, LEN), ones_rows], axis=0)
    for index in range(ff // 256):
        at = index * 256
        grad = dot_nt(yl_rows, dh[at : at + 256, :])
        scatter_shares(gin, grad[0:width], at)
        row, lane = 5 + at // width, at % width
        small[row : row + 1, lane : lane + 256] = grad[width : width + 1]
        if index == 1:
            step_back()
        if index == 3:
            step_out()
    sum_in.start(0)

    vals, vals_up, kt, kt_up = rows_a, rows_b, cols_a, cols_b
    w3 = ot
    d3, w2 = hd.at[0, pl.ds(0, 3 * width)], hd.at[0, pl.ds(3 * width, width), pl.ds(0, 2 * width)]
    d2, dxu = hd.at[1, pl.ds(0, 2 * width)], hd.at[1, pl.ds(2 * width, width)]
    wtb[...] = transposed(eye, wk[...])
    for pair in range(4):
        lanes = slice(pair * 128, pair * 128 + 128)
        for index, ref in enumerate((wq, wk, wv)):
            w3[:, pair * 384 + index * 128 : pair * 384 + index * 128 + 128] = ref[:, lanes]
        for index, ref in enumerate((wk, wv)):
            w2[:, pair * 256 + index * 128 : pair * 256 + index * 128 + 128] = ref[:, lanes]
    clear_pads_lanes(kt)
    clear_pads_lanes(kt_up)

    @pl.loop(0, WINDOWS)
    def _(window):
        @pl.when(window == 2)
        def _():
            step_in()

        here = pl.ds(pl.multiple_of(window * QUERIES, QUERIES), QUERIES)
        padded_at = pl.multiple_of(window * QUERIES + TILE, TILE)
        low = transposed(eye, xt[:, here])
        upper = transposed(eye, xut[:, here])
        store_pairs(vals, padded_at, dot(low, wv[...]).astype(BF16))
        store_heads(kt, padded_at, dot(wtb[...], xt[:, here]).astype(BF16))
        store_pairs(vals_up, padded_at, dot(upper, wv[...]).astype(BF16))
        store_heads(kt_up, padded_at, dot(wtb[...], xut[:, here]).astype(BF16))

    blocks = PADDED // 128

    shape = (8, LEN)
    channel = (iota(shape, 1) // TILE + iota(shape, 1) % FLANK_COLS) % 3
    chosen = jnp.where(channel == iota(shape, 0), 1.0, 0.0).astype(BF16)

    def pass_over(pair, part, v_rows, k_cols):
        for window, half in items:
            e_in(pair, part, window, half).wait()
        feats = pl.ds(pl.multiple_of(pair * 128, 128), 128)
        follow = pair + 1
        next_pair, next_part = follow % 4, jnp.minimum(part + follow // 4, 1)

        def limits(window):
            first = TILE if window == 0 else 0
            last = SPAN - TILE if window == WINDOWS - 1 else SPAN
            return first, last

        def grad_probs(window, half):
            first, last = limits(window)
            here = slice(window * QUERIES, window * QUERIES + QUERIES)
            rows = slice(window * QUERIES + first, window * QUERIES + last)
            return dot(v_rows[pair, rows, :], head_of_pair(d_o[feats, here], half))

        def add_blocks(base, window, half, value):
            first, last = limits(window)
            rows = slice(half * HEAD_DIM, half * HEAD_DIM + HEAD_DIM)
            for at in range(first, last, 128):
                block = (window * QUERIES + at) // 128
                piece = value[:, at - first : at - first + 128]
                if window > 0 and at < SPAN - QUERIES:
                    piece = piece + acc[base + block, rows, :]
                acc[base + block, rows, :] = piece

        upcoming = grad_probs(*items[0])
        for index, (window, half) in enumerate(items):
            current = upcoming
            if index + 1 < len(items):
                upcoming = grad_probs(*items[index + 1])
            first, last = limits(window)
            here = slice(window * QUERIES, window * QUERIES + QUERIES)
            span = slice(window * QUERIES + first, window * QUERIES + last)
            head = 2 * pair + half
            mine = pl.ds(pl.multiple_of(pair * 128 + half * HEAD_DIM, HEAD_DIM), HEAD_DIM)
            e = e_tile(window, half, first, last)
            ds = (e.astype(F32) * (current - dd[pl.ds(head, 1), here])).astype(BF16)
            dq = dot(k_cols[head, 0:HEAD_DIM, span], ds)
            at = pl.ds(pl.multiple_of(pair * 384 + half * HEAD_DIM, HEAD_DIM), HEAD_DIM)
            if part == 0:
                d3[at, here] = dq.astype(BF16)
            else:
                d3[at, here] = ((dq + d3[at, here].astype(F32)) * 0.125).astype(BF16)
            add_blocks(0, window, half, dot_nt(qt[mine, here], ds))
            add_blocks(blocks, window, half, dot_nt(d_o[mine, here], e))
            e_in(next_pair, next_part, window, half).start()

    def take_blocks(ref, at, base):
        for block in range(1, blocks - 1):
            ref[pl.ds(at, 128), block * 128 - 128 : block * 128] = acc[base + block].astype(BF16)

    @pl.loop(0, 4)
    def _(pair):
        pass_over(pair, 0, vals_up, kt_up)
        at = pl.multiple_of(pair * 256, 256)
        take_blocks(d2, at, 0)
        take_blocks(d2, at + 128, blocks)

        @pl.when(pair == 0)
        def _():
            step_back()
            step_out()

        @pl.when(pair == 2)
        def _():
            step_back()
            step_out()
            step_in()

        @pl.when(pair == 3)
        def _():
            step_back()
            step_out()

    def send_halo(window):
        @pl.when(band > 0)
        def _():
            halo(window).start()

    for window in range(WINDOWS):
        here = slice(window * QUERIES, window * QUERIES + QUERIES)
        dxu[:, here] = dot(w2[...], d2[:, here]).astype(BF16)
        if window < 2:
            send_halo(window)

    embed_sum[0:8, :] = dot_nt(chosen, da[...]) + dot_nt(chosen, dxu[...]) * has_up
    embed_sum[8:16, :] = jnp.zeros((8, width), F32)

    @pl.loop(0, 4)
    def _(pair):
        pass_over(pair, 1, vals, kt)

        for turn in range(4):

            @pl.when(pair == turn)
            def _(turn=turn):
                if turn == 0:
                    step_back()
                if turn < 3:
                    step_in()
                if turn > 0:
                    sum_qkv(turn - 1).advance(0)
                if turn < 2:
                    send_halo(2 * turn + 2)
                    send_halo(2 * turn + 3)

        at = pl.multiple_of(pair * 384, 128)
        take_blocks(d3, at + 128, 0)
        take_blocks(d3, at + 256, blocks)
        grads = dot_nt(xt[...], d3[pl.ds(at, 384), :])
        grads_up = dot_nt(xut[...], d2[pl.ds(pl.multiple_of(pair * 256, 256), 256), :])
        lanes = pl.ds(pl.multiple_of(pair * 384, 128), 128)
        low_q = grads[:, 0:128].astype(BF16)
        low_kv = (grads[:, 128:384] + grads_up).astype(BF16)
        for owner in range(size):
            rows = slice(owner * share, owner * share + share)
            to = pl.ds(pl.multiple_of(qkv_at + reversed_bits(owner, size) * share, share), share)
            hd[1, to, lanes] = low_q[rows]
            hd[1, to, pl.ds(pl.multiple_of(pair * 384 + 128, 128), 256)] = low_kv[rows]
        sum_qkv(pair).start(0)
        totals = dot_nt(chosen, d3[pl.ds(at, 384), :])
        high = totals.astype(BF16)
        low = (totals - high.astype(F32)).astype(BF16)
        embed_sum[...] += dot_nt(
            jnp.concatenate([high, low], axis=0), w3[:, pl.ds(pl.multiple_of(pair * 384, 128), 384)]
        )

    rows = jnp.concatenate([small[0:8], embed_sum[0:8] + embed_sum[8:16]], axis=0)
    for owner in range(size):
        at = pl.multiple_of(reversed_bits(owner, size) * 16, 16)
        small_buf[pl.ds(at, 16), 0:share] = rows[:, owner * share : owner * share + share]
        row, lane = 5 + owner * back_share // width, owner * back_share % width
        small_buf[pl.ds(at + 5, 1), 0:back_share] = small[row : row + 1, lane : lane + back_share]
    sum_small.start(0)
    for window, half in items:
        e_in(0, 1, window, half).wait()

    @pl.when(band == size - 1)
    def _():
        below[...] = jnp.zeros_like(below)

    for window in range(WINDOWS):
        out_copy(window).wait()

    def gt_copy(window):
        columns = pl.ds(pl.multiple_of(window * BLOCK_COLS, BLOCK_COLS), BLOCK_COLS)
        return pltpu.make_async_copy(
            side.at[:, columns, :], gt_h.at[:, columns, :], out_sem.at[window]
        )

    @pl.loop(0, WINDOWS)
    def _(window):
        @pl.when(band < size - 1)
        def _():
            halo(window).wait_recv()

        here = pl.ds(pl.multiple_of(window * QUERIES, QUERIES), QUERIES)
        dx = da[:, here].astype(F32) + dot(w3[...], d3[:, here]) + below[:, here].astype(F32)
        rows = dot_nt(eye, dx.astype(BF16)).astype(BF16)
        for half in range(2):
            at = pl.multiple_of((2 * window + half) * FLANK_COLS, FLANK_COLS)
            side[:, pl.ds(at, FLANK_COLS), :] = rows[half * TILE : half * TILE + TILE].reshape(
                BLOCK_ROWS, FLANK_COLS, -1
            )
        gt_copy(window).start()

        @pl.when(window == 0)
        def _():
            sum_qkv(0).advance(1)

        @pl.when(window == 1)
        def _():
            sum_qkv(3).advance(0)
            sum_small.advance(0)

        @pl.when(window == 2)
        def _():
            sum_qkv(1).advance(1)
            step_back.last()

        @pl.when(window == 3)
        def _():
            step_in.last()

        @pl.when(window == 4)
        def _():
            step_out.last()
            sum_qkv(2).advance(1)
            sum_qkv(0).finish(write_qkv(0))

    sum_qkv(3).advance(1)
    sum_small.advance(1)
    sum_qkv(1).finish(write_qkv(1))
    sum_qkv(2).finish(write_qkv(2))

    def write_small(value):
        small_ref[...] = value

    sum_qkv(3).finish(write_qkv(3))
    sum_small.finish(write_small)

    for window in range(WINDOWS):
        gt_copy(window).wait()

    @pl.when(band > 0)
    def _():
        for window in range(WINDOWS):
            halo(window).wait_send()

    @pl.when(band < size - 1)
    def _():
        for window in range(WINDOWS):
            up_copy(window).wait_send()


def emit_kernel(
    out_in, gt_in, qkv_in, gin_in, gback_in, gout_in, small_in,
    out_h, gt_h, gq, gk, gv, gout, gin, gbi, gback, gbb, gg1, gs1, gg2, gs2, gemb,
    qkv, small, large, sems, large_sems,
):
    pairs = (
        (small_in, small), (qkv_in, qkv), (gback_in, gback), (gin_in, gin), (gout_in, gout),
    )
    moves = []
    for index, (source, target) in enumerate(((out_in, out_h), (gt_in, gt_h))):
        for row in range(0, BLOCK_ROWS, 2):
            rows, held = pl.ds(row, 2), large.at[index, pl.ds(row, 2)]
            sem = index * 4 + row // 2
            moves.append(
                (
                    pltpu.make_async_copy(source.at[rows], held, large_sems.at[0, sem]),
                    pltpu.make_async_copy(held, target.at[rows], large_sems.at[1, sem]),
                )
            )
    for load, _ in moves:
        load.start()
    copies = [
        pltpu.make_async_copy(source, target, sems.at[index])
        for index, (source, target) in enumerate(pairs)
    ]
    for copy in copies:
        copy.start()
    for load, store in moves:
        load.wait()
        store.start()
    copies[0].wait()
    share, back_share = gq.shape[0], gbi.shape[0]
    for row, ref in ((2, gbb), (3, gg1), (4, gs1), (0, gg2), (1, gs2)):
        ref[...] = small[row : row + 1, 0:share].reshape(-1)
    gemb[...] = small[8:11, 0:share]
    gbi[...] = small[5:6, 0:back_share].reshape(-1)
    copies[1].wait()
    for pair in range(4):
        for index, ref in enumerate((gq, gk, gv)):
            ref[:, pair * 128 : pair * 128 + 128] = qkv[pair, :, index * 128 : index * 128 + 128]
    for copy in copies[2:]:
        copy.wait()
    for _, store in moves:
        store.wait()


def shards(
    tokens, row_place, row_width, cotangent, chan_embed, w_query, w_key, w_value, w_out, w_in,
    bias_in, w_back, bias_back, gain_first, shift_first, gain_second, shift_second,
):
    width = tokens.shape[3]
    ff = w_in.shape[1]
    tok = tokens.reshape(BLOCK_ROWS, ROW_POS, width)
    cot = cotangent.reshape(BLOCK_ROWS, ROW_POS, width)
    shape = jax.ShapeDtypeStruct
    size, groups = lax.axis_size("band"), lax.axis_size("grp")
    dma = pltpu.SemaphoreType.DMA
    share, back_share = width // size, ff // size
    stages = size // 2 + 2 * groups
    in_split = ff // groups % 128 == 0
    back_split = width // groups % 128 == 0
    rows = shape((BLOCK_ROWS, ROW_POS, width), BF16)

    def later(split, total_rows, columns):
        return pltpu.VMEM((total_rows // 2, columns // groups if split else columns), BF16)

    def across(split, total_rows, columns):
        if split:
            return pltpu.VMEM((groups - 1, total_rows // 2, columns // groups), BF16)
        return pltpu.VMEM((groups, total_rows // size, columns), BF16)

    flat = pltpu.VMEM((width, LEN), BF16)
    out, gt, _, qkv, gin, gback, gout, small = pl.pallas_call(
        functools.partial(
            layer_kernel, size=size, groups=groups, in_split=in_split, back_split=back_split
        ),
        name="layer_forward_and_back",
        out_shape=(
            rows,
            rows,
            shape((WINDOWS, 2, 2 * SPAN, 4 * QUERIES), BF16),
            shape((4, share, 384), F32),
            shape((share, ff), F32),
            shape((back_share, width), F32),
            shape((share, width), F32),
            shape((16, 128), F32),
        ),
        in_specs=[smem()] * 2 + [vmem()] * 7 + [hbm()] * 8,
        out_specs=(hbm(),) * 3 + (vmem(),) * 5,
        scratch_shapes=[
            pltpu.VMEM(rows.shape, BF16),
            pltpu.VMEM(rows.shape, BF16),
            pltpu.VMEM((4, width, width), BF16),
            pltpu.VMEM((width, width), BF16),
            pltpu.VMEM((width, width), BF16),
            pltpu.VMEM((2, ff, width), BF16),
            pltpu.VMEM((2, width, ff), BF16),
            flat,
            flat,
            flat,
            flat,
            flat,
            pltpu.VMEM((4, PADDED, 128), BF16),
            pltpu.VMEM((4, PADDED, 128), BF16),
            pltpu.VMEM((8, HEAD_DIM + 16, PADDED), BF16),
            pltpu.VMEM((8, HEAD_DIM + 16, PADDED), BF16),
            pltpu.VMEM((2, ff, LEN), BF16),
            pltpu.VMEM((SPAN, QUERIES), F32),
            pltpu.VMEM((3 * FLANK_COLS, width), BF16),
            pltpu.VMEM((5, width, 128), BF16),
            pltpu.VMEM((ff, 128), BF16),
            pltpu.VMEM((2, width, QUERIES), BF16),
            pltpu.VMEM((2, 8, QUERIES), F32),
            flat,
            pltpu.VMEM((2 * PADDED // 128, 128, 128), F32),
            flat,
            pltpu.VMEM((8, LEN), F32),
            pltpu.VMEM((8, LEN), F32),
            pltpu.VMEM((width // 2, ff), BF16),
            later(in_split, width, ff),
            across(in_split, width, ff),
            pltpu.VMEM((groups, share, ff // groups), F32),
            pltpu.VMEM((ff // 2, width), BF16),
            later(back_split, ff, width),
            across(back_split, ff, width),
            pltpu.VMEM((groups, back_share, width // groups), F32),
            pltpu.VMEM((width // 2, width), BF16),
            pltpu.VMEM((width // 2, width), BF16),
            pltpu.VMEM((groups, share, width), BF16),
            pltpu.VMEM((4, width // 2, 384), BF16),
            pltpu.VMEM((4, width // 2, 384), BF16),
            pltpu.VMEM((4, groups, share, 384), BF16),
            pltpu.VMEM((16, width), F32),
            pltpu.VMEM((16 * size, 128), F32),
            pltpu.VMEM((8 * size, 128), F32),
            pltpu.VMEM((8 * size, 128), F32),
            pltpu.VMEM((groups, 16, 128), F32),
            pltpu.VMEM((16, width), F32),
            dma((8,)),
            dma((2, 2)),
            dma((WINDOWS, 2)),
            dma((WINDOWS,)),
            dma((WINDOWS,)),
            dma((WINDOWS,)),
            dma((WINDOWS,)),
            dma((WINDOWS,)),
            dma((stages,)),
            dma((stages,)),
            dma((stages,)),
            dma((stages,)),
            dma((stages,)),
            dma((stages,)),
            dma((4, stages)),
            dma((4, stages)),
            dma((stages,)),
            dma((stages,)),
        ],
        compiler_params=pltpu.CompilerParams(
            vmem_limit_bytes=LIMIT, collective_id=0, has_side_effects=True
        ),
    )(
        row_place, row_width, chan_embed, bias_in, bias_back, gain_first, shift_first, gain_second,
        shift_second, tok, cot, w_query, w_key, w_value, w_out, w_in, w_back,
    )
    vector = shape((share,), F32)
    square = shape((share, width), F32)
    out, gt, gq, gk, gv, gout, gin, gbi, gback, gbb, gg1, gs1, gg2, gs2, gemb = pl.pallas_call(
        emit_kernel,
        name="emit_shares",
        out_shape=(
            rows, rows, square, square, square, square, shape((share, ff), F32),
            shape((back_share,), F32), shape((back_share, width), F32),
            vector, vector, vector, vector, vector, shape((3, share), F32),
        ),
        in_specs=[hbm()] * 7,
        out_specs=(hbm(),) * 2 + (vmem(),) * 3 + (vmem(), vmem(), vmem(), vmem()) + (vmem(),) * 6,
        scratch_shapes=[
            pltpu.VMEM((4, share, 384), F32),
            pltpu.VMEM((16, 128), F32),
            pltpu.VMEM((2,) + rows.shape, BF16),
            dma((5,)),
            dma((2, 8)),
        ],
        compiler_params=pltpu.CompilerParams(vmem_limit_bytes=LIMIT),
    )(out, gt, qkv, gin, gback, gout, small)
    return (
        out.reshape(tokens.shape),
        gt.reshape(tokens.shape),
        gq, gk, gv, gout, gin, gbi, gback, gbb, gg1, gs1, gg2, gs2, gemb,
    )


def solution(mesh):
    tall = P("grp", "band", None, None)
    return jax.shard_map(
        shards,
        mesh=mesh,
        in_specs=(tall, P("grp", "band"), P("grp", "band"), tall) + (P(),) * 13,
        out_specs=(tall, tall)
        + (P("band", None),) * 5
        + (P("band"), P("band", None))
        + (P("band"),) * 5
        + (P(None, "band"),),
        check_vma=False,
    )
```

```python
import functools

import jax
import jax.numpy as jnp
from jax import lax
from jax.experimental import pallas as pl
from jax.experimental.pallas import tpu as pltpu
from jax.sharding import PartitionSpec as P

HEAD_DIM = 64
ROW_POS = 192
BLOCK_ROWS = 8
BLOCK_COLS = 32
FLANK_COLS = 16
WINDOWS = ROW_POS // BLOCK_COLS
BLOCKS = ROW_POS // FLANK_COLS
TILE = BLOCK_ROWS * FLANK_COLS
QUERIES = 2 * TILE
SPAN = 4 * TILE
LEN = BLOCK_ROWS * ROW_POS
PADDED = LEN + 2 * TILE

norm_eps = 1e-06
big_negative = -1e30
F32 = jnp.float32
BF16 = jnp.bfloat16
LOG2_E = 1.4426950408889634
GELU_SCALE = 0.7978845608028654
GELU_CUBE = 0.044715


def dot(left, right):
    return jnp.dot(left, right, preferred_element_type=F32)


def dot_nt(left, right):
    return lax.dot_general(left, right, (((1,), (1,)), ((), ())), preferred_element_type=F32)


def iota(shape, dim):
    return lax.broadcasted_iota(jnp.int32, shape, dim)


def identity(size):
    return jnp.where(iota((size, size), 0) == iota((size, size), 1), 1.0, 0.0).astype(BF16)


def transposed(eye, value):
    step = eye.shape[0]
    parts = [
        dot_nt(eye, value[:, at : at + step]).astype(BF16) for at in range(0, value.shape[1], step)
    ]
    return jnp.concatenate(parts, axis=0)


def column(eye, row):
    step = eye.shape[0]
    ones = jnp.ones((128, step), BF16)
    parts = [
        dot_nt(jnp.where(eye > 0, row[:, at : at + step], 0).astype(BF16), ones)
        for at in range(0, row.shape[1], step)
    ]
    return jnp.concatenate(parts, axis=0)


def wide(value):
    return jnp.concatenate([value, value], axis=1)


def halves(value):
    return value[:, :128] + value[:, 128:]


def fill_embed(embed_ref, rows_ref):
    embed = embed_ref[...].astype(F32)
    channel = lax.rem(iota(rows_ref.shape, 0), 3)
    rows_ref[...] = jnp.where(
        channel == 0, embed[0:1], jnp.where(channel == 1, embed[1:2], embed[2:3])
    ).astype(BF16)


def block_rows(rows_ref, block):
    return rows_ref[:, pl.ds(pl.multiple_of(block * FLANK_COLS, FLANK_COLS), FLANK_COLS), :]


def raw_window(rows_ref, window):
    parts = [block_rows(rows_ref, 2 * window + half).reshape(TILE, -1) for half in range(2)]
    return jnp.concatenate(parts, axis=0)


def embed_window(embed_rows, window):
    parts = []
    for half in range(2):
        at = pl.multiple_of((2 * window + half) % 3 * FLANK_COLS, FLANK_COLS)
        part = embed_rows[pl.ds(at, FLANK_COLS), :][None]
        parts.append(jnp.broadcast_to(part, (BLOCK_ROWS,) + part.shape[1:]).reshape(TILE, -1))
    return jnp.concatenate(parts, axis=0)


def start_window(rows_ref, embed_rows, window):
    return raw_window(rows_ref, window).astype(F32) + embed_window(embed_rows, window).astype(F32)


def norm_stats(value):
    center = value - jnp.mean(value, axis=0, keepdims=True)
    spread = jnp.mean(center * center, axis=0, keepdims=True)
    inverse = lax.rsqrt(spread + norm_eps)
    return center * inverse, inverse


def norm_back(normed, inverse, grad, gain):
    scaled = grad * gain
    first = jnp.mean(scaled, axis=0, keepdims=True)
    second = jnp.mean(scaled * normed, axis=0, keepdims=True)
    return (scaled - first - normed * second) * inverse


def vmem():
    return pl.BlockSpec(memory_space=pltpu.VMEM)


def smem():
    return pl.BlockSpec(memory_space=pltpu.SMEM)


def hbm():
    return pl.BlockSpec(memory_space=pl.ANY)


LIMIT = 62 * 1024 * 1024


def head_of_pair(value, half):
    keep = (iota(value.shape, 0) // HEAD_DIM) == half
    return jnp.where(keep, value, jnp.zeros_like(value))


def clear_pads_rows(ref):
    pad = jnp.zeros((ref.shape[0], TILE, ref.shape[2]), ref.dtype)
    ref[:, 0:TILE, :] = pad
    ref[:, PADDED - TILE : PADDED, :] = pad


def reversed_bits(index, count):
    place, bit = 0, 1
    while bit < count:
        place = place + (index // bit) % 2 * (count // (2 * bit))
        bit *= 2
    return place


def levels(count):
    return count.bit_length() - 1


def first_share(band, bits, count):
    start = 0
    for level in range(bits):
        start = start + (band // (1 << level)) % 2 * (count >> (level + 1))
    return start


class Reduction:
    def __init__(
        self, buf, shape, recv, later, across, gathered, send_sem, recv_sem, place, direct=False,
        late=False,
    ):
        self.buf, self.recv, self.later = buf, recv, later
        self.across, self.gathered = across, gathered
        self.send_sem, self.recv_sem = send_sem, recv_sem
        self.band, self.grp, self.size, self.groups = place
        self.depth = depth = levels(self.size)
        self.rows = shape[0] // self.size
        halvings = [("halve", bit) for bit in range(1, depth)]
        self.stages = [("halve", 0)]
        if gathered is not None:
            self.stages += halvings[:1] if late else []
            self.stages += [("split", 2 if late else 1)] + halvings[1 if late else 0 :]
            self.stages += [("gather", depth)]
        elif direct:
            self.stages += [("direct", 1), ("sum", depth)]
        else:
            self.stages += halvings + [("sum", depth)]
        self.part = shape[1] // self.groups
        self.dtype = buf.dtype

    def start_of(self, bits):
        return first_share(self.band, bits, self.size)

    def columns_of(self, member):
        return pl.ds(pl.multiple_of(member * self.part, 128), self.part)

    def columns(self, stage):
        split = [kind for kind, _ in self.stages[:stage]].count("split")
        return self.columns_of(self.grp) if split else slice(None)

    def width(self, stage):
        split = [kind for kind, _ in self.stages[:stage]].count("split")
        return slice(0, self.part) if split else slice(None)

    def shares(self, first, count=1):
        return pl.ds(pl.multiple_of(first * self.rows, self.rows), count * self.rows)

    def landing(self, bits):
        return self.later if bits else self.recv

    def landing_rows(self, bits, index, count):
        return self.shares(index + (self.size >> (bits + 1) if bits else 0), count)

    def copies(self, stage):
        kind, bits = self.stages[stage]
        columns = self.columns(stage)
        pieces = []
        if kind == "halve":
            half = self.size >> (bits + 1)
            bit = (self.band // (1 << bits)) % 2
            pieces.append(
                (
                    self.buf.at[self.shares(self.start_of(bits) + (1 - bit) * half, half), columns],
                    self.landing(bits).at[self.landing_rows(bits, 0, half), self.width(stage)],
                    bits,
                    (self.band + (1 << bits) * (1 - 2 * bit), self.grp),
                )
            )
        if kind == "direct":
            for step in range(1, self.size // 2):
                partner = (self.band + 2 * step) % self.size
                source = self.buf.at[self.shares(reversed_bits(partner, self.size))]
                place = (partner, self.grp)
                pieces.append((source, self.later.at[self.shares(step)], step, place))
        for step in range(1, self.groups):
            partner = (self.grp + step) % self.groups
            place = (self.band, partner)
            if kind == "sum":
                source, target = self.buf.at[self.shares(self.start_of(bits))], self.across.at[step]
                pieces.append((source, target, self.size // 2 + step - 1, place))
            if kind == "split":
                rows = self.shares(self.start_of(bits), self.size >> bits)
                source = self.buf.at[rows, self.columns_of(partner)]
                pieces.append((source, self.across.at[step - 1], self.depth + step - 1, place))
            if kind == "gather":
                source, target = self.gathered.at[0], self.gathered.at[step]
                pieces.append((source, target, self.depth + self.groups + step - 2, place))
        return [
            pltpu.make_async_remote_copy(
                src_ref=source,
                dst_ref=target,
                send_sem=self.send_sem(sem),
                recv_sem=self.recv_sem(sem),
                device_id=place,
                device_id_type=pl.DeviceIdType.MESH,
            )
            for source, target, sem, place in pieces
        ]

    def start(self, stage):
        for copy in self.copies(stage):
            copy.start()

    def advance(self, stage):
        for copy in self.copies(stage):
            copy.wait()
        kind, bits = self.stages[stage]
        if kind == "halve":
            columns = self.columns(stage)
            half, keep = self.size >> (bits + 1), self.start_of(bits + 1)

            @pl.loop(0, half)
            def _(index):
                mine = self.shares(keep + index)
                total = self.buf[mine, columns].astype(F32)
                landed = self.landing(bits)[self.landing_rows(bits, index, 1), self.width(stage)]
                total = total + landed.astype(F32)
                self.buf[mine, columns] = total.astype(self.dtype)
        elif kind == "direct":
            mine = self.shares(self.start_of(self.depth))
            total = self.buf[mine, :].astype(F32)
            for step in range(1, self.size // 2):
                total = total + self.later[step * self.rows : (step + 1) * self.rows, :].astype(F32)
            self.buf[mine, :] = total.astype(self.dtype)
        else:
            columns = self.columns_of(self.grp)
            keep = self.start_of(bits)

            @pl.loop(0, self.size >> bits)
            def _(index):
                mine = self.shares(keep + index)
                total = self.buf[mine, columns].astype(F32)
                for step in range(self.groups - 1):
                    total = total + self.across[step, self.shares(index), :].astype(F32)
                self.buf[mine, columns] = total.astype(self.dtype)

        if self.stages[stage + 1][0] == "gather":
            mine = self.shares(self.start_of(self.depth))
            self.gathered[0] = self.buf[mine, self.columns_of(self.grp)].astype(F32)
        self.start(stage + 1)

    def finish(self, out):
        last = len(self.stages) - 1
        for copy in self.copies(last):
            copy.wait()
        if self.stages[last][0] == "sum":
            self.across[0] = self.buf[self.shares(self.start_of(self.depth)), :]
            total = 0.0
            for member in range(self.groups):
                step = (self.grp + self.groups - member) % self.groups
                total = total + self.across[step].astype(F32)
            out(total)
        else:
            for step in range(self.groups):
                member = (self.grp + self.groups - step) % self.groups
                out(self.gathered[step], self.columns_of(member))


def store_pairs(ref, at, value):
    for pair in range(value.shape[1] // 128):
        ref[pair, pl.ds(at, value.shape[0]), :] = value[:, pair * 128 : (pair + 1) * 128]


def store_heads(ref, at, value):
    for head in range(value.shape[0] // HEAD_DIM):
        rows = slice(head * HEAD_DIM, head * HEAD_DIM + HEAD_DIM)
        ref[head, 0:HEAD_DIM, pl.ds(at, value.shape[1])] = value[rows]


def clear_pads_lanes(ref):
    pad = jnp.zeros(ref.shape[:2] + (TILE,), ref.dtype)
    ref[:, :, 0:TILE] = pad
    ref[:, :, PADDED - TILE : PADDED] = pad


def gelu_and_slope(u):
    square = u * u
    cube = (GELU_SCALE * GELU_CUBE) * square
    h = 0.5 * jnp.tanh(u * (GELU_SCALE + cube)) + 0.5
    g = u * (2.0 * GELU_SCALE + 6.0 * cube)
    return u * h, h * (1.0 + (1.0 - h) * g)


class Steps:
    def __init__(self, reduction, write):
        self.reduction, self.write, self.stage = reduction, write, 0

    def __call__(self):
        if self.stage < len(self.reduction.stages) - 1:
            self.reduction.advance(self.stage)
            self.stage += 1

    def last(self):
        while self.stage < len(self.reduction.stages) - 1:
            self()
        self.reduction.finish(self.write)


def layer_kernel(
    place_ref, width_ref, embed_ref, bi_ref, bb_ref, g1_ref, s1_ref, g2_ref, s2_ref, tok_h, cot_h, wq_h, wk_h, wv_h, wo_h, wi_h, wb_h,
    out_h, gt_h, e_h, qkv_ref, gin_ref, gback_ref, gout_ref, small_ref,
    tok, side, w4, wta, wtb, ww, wt, xt, xut, qt, ot, da, rows_a, rows_b, cols_a, cols_b, hd,
    bias_low, embed_rows, cols, bi_col, n1_buf, inv_buf, d_o, acc, below,
    inv, dd,
    in_recv, in_later, in_across, in_parts, back_recv, back_later, back_across, back_parts,
    out_recv, out_later, out_across,
    qkv_recv, qkv_later, qkv_across, small, small_buf, small_recv, small_later, small_across, embed_sum,
    load_sem, e_out_sem, e_in_sem, out_sem, up_ss, up_rs, halo_ss, halo_rs,
    in_ss, in_rs, back_ss, back_rs, go_ss, go_rs, qkv_ss, qkv_rs, small_ss, small_rs,
    *, size, groups, in_split, back_split,
):
    band, grp = lax.axis_index("band"), lax.axis_index("grp")
    place = (band, grp, size, groups)
    depth = levels(size)
    MESH = pl.DeviceIdType.MESH
    wq, wk, wv, wo = (w4.at[index] for index in range(4))
    wit, wb, wi, wbt = ww.at[0], ww.at[1], wt.at[0], wt.at[1]
    width, ff = wi_h.shape

    sources = (tok_h, wq_h, wk_h, wv_h, wo_h, wi_h, wb_h, cot_h)
    targets = (tok, wq, wk, wv, wo, wi, wb, side)
    loads = [
        pltpu.make_async_copy(source, target, load_sem.at[index])
        for index, (source, target) in enumerate(zip(sources, targets))
    ]
    for load in loads[:7]:
        load.start()
    barrier = pltpu.get_barrier_semaphore()
    odd = band % 2
    pl.semaphore_signal(barrier, inc=1, device_id=(band + 1 - 2 * odd, grp), device_id_type=MESH)
    for step in range(1, size // 2):
        pl.semaphore_signal(
            barrier, inc=1, device_id=((band + 2 * step) % size, grp), device_id_type=MESH
        )
    for step in range(1, groups):
        pl.semaphore_signal(
            barrier, inc=1, device_id=(band, (grp + step) % groups), device_id_type=MESH
        )
    beyond = (odd == 1) & (band < size - 1) | (odd == 0) & (band > 0)

    @pl.when(beyond)
    def _():
        pl.semaphore_signal(
            barrier, inc=1, device_id=(band + 2 * odd - 1, grp), device_id_type=MESH
        )

    pl.semaphore_wait(barrier, size // 2 + groups - 1 + jnp.where(beyond, 1, 0))

    def up_copy(window):
        columns = pl.ds(pl.multiple_of(window * BLOCK_COLS, BLOCK_COLS), BLOCK_COLS)
        return pltpu.make_async_remote_copy(
            src_ref=tok_h.at[:, columns, :], dst_ref=side.at[:, columns, :],
            send_sem=up_ss.at[window], recv_sem=up_rs.at[window],
            device_id=(jnp.minimum(band + 1, size - 1), grp), device_id_type=MESH,
        )

    def halo(window):
        here = pl.ds(pl.multiple_of(window * QUERIES, QUERIES), QUERIES)
        return pltpu.make_async_remote_copy(
            src_ref=dxu.at[:, here], dst_ref=below.at[:, here],
            send_sem=halo_ss.at[window], recv_sem=halo_rs.at[window],
            device_id=(jnp.maximum(band - 1, 0), grp), device_id_type=MESH,
        )

    @pl.when(band < size - 1)
    def _():
        for window in range(WINDOWS):
            up_copy(window).start()

    @pl.when(band == 0)
    def _():
        side[...] = jnp.zeros_like(side)

    keys, keys_up, vt, vt_up, qs = rows_a, rows_b, cols_a, cols_b, da
    bias_up, ones_row = d_o.at[:, pl.ds(0, 128)], d_o.at[pl.ds(0, 128), pl.ds(128, QUERIES)]
    eye = identity(256)
    fill_embed(embed_ref, embed_rows)
    clear_pads_rows(keys)
    clear_pads_rows(keys_up)
    clear_pads_lanes(vt)
    clear_pads_lanes(vt_up)
    sums = jnp.where(iota((16, PADDED), 0) == 0, 1.0, 0.0).astype(BF16)
    for head in range(8):
        vt[head, HEAD_DIM:, :] = sums
        vt_up[head, HEAD_DIM:, :] = sums
    ones_row[...] = jnp.where(iota(ones_row.shape, 0) == 0, 1.0, 0.0).astype(BF16)
    for load in loads[:4]:
        load.wait()
    wta[...] = transposed(eye, wq[...])
    wtb[...] = transposed(eye, wv[...])
    has_up = jnp.where(band > 0, 1.0, 0.0)

    @pl.loop(0, WINDOWS)
    def _(window):
        at = pl.multiple_of(window * QUERIES, QUERIES)
        padded_at = pl.multiple_of(window * QUERIES + TILE, TILE)
        low = start_window(tok, embed_rows, window).astype(BF16)
        low_t = transposed(eye, low)
        xt[:, pl.ds(at, QUERIES)] = low_t
        q_low = dot(wta[...], low_t).astype(BF16)
        store_pairs(keys, padded_at, dot(low, wk[...]).astype(BF16))
        store_heads(vt, padded_at, dot(wtb[...], low_t).astype(BF16))
        qt[:, pl.ds(at, QUERIES)] = q_low * BF16(0.125)
        qs[:, pl.ds(at, QUERIES)] = (q_low.astype(F32) * (0.125 * LOG2_E)).astype(BF16)

    def await_upper(window):
        @pl.when((band > 0) & (window < WINDOWS))
        def _():
            up_copy(window).wait_recv()

    def prepare_upper(window):
        at = pl.multiple_of(window * QUERIES, QUERIES)
        padded_at = pl.multiple_of(window * QUERIES + TILE, TILE)
        upper = (start_window(side, embed_rows, window) * has_up).astype(BF16)
        upper_t = transposed(eye, upper)
        xut[:, pl.ds(at, QUERIES)] = upper_t
        store_pairs(keys_up, padded_at, dot(upper, wk[...]).astype(BF16))
        store_heads(vt_up, padded_at, dot(wtb[...], upper_t).astype(BF16))

    mask_shape = (SPAN, QUERIES)
    memory, query = iota(mask_shape, 0), iota(mask_shape, 1)
    memory_col = (memory // TILE) * FLANK_COLS + memory % FLANK_COLS - FLANK_COLS
    query_col = (query // TILE) * FLANK_COLS + query % FLANK_COLS
    memory_row = (memory % TILE) // FLANK_COLS
    query_row = (query % TILE) // FLANK_COLS
    same_row = memory_row == query_row
    itself = same_row & (memory_col == query_col)
    earlier = (memory_row < query_row) | (same_row & (memory_col <= query_col))
    code_low, code_up = d_o.at[:, pl.ds(512, QUERIES)], d_o.at[:, pl.ds(768, 128)]
    code = jnp.where(itself, 1024, jnp.where(earlier, memory_col, -1024))
    code_low[...] = code.astype(F32).astype(BF16)
    code = jnp.where(query[:, 0:128] == 0, memory_col[:, 0:128], 1024)
    code_up[...] = code.astype(F32).astype(BF16)
    row_limit = width_ref[0, 0]
    upper_limit = jnp.where(place_ref[0, 0] > 0, row_limit, 0)

    def bias_of(code_ref, window, limit):
        code = code_ref[...].astype(F32)
        first = (-window * BLOCK_COLS).astype(F32)
        last = (limit - window * BLOCK_COLS).astype(F32)
        allowed = ((code >= first) & (code < last)) | (code > 512.0)
        return jnp.where(allowed, 0.0, big_negative)

    def prepare_masks(window):
        bias_low[...] = bias_of(code_low, window, row_limit)
        bias_up[...] = bias_of(code_up, window, upper_limit).astype(BF16)

    def e_out(window, half):
        slot = window % 2
        return pltpu.make_async_copy(
            hd.at[slot, pl.ds(half * 2 * SPAN, 2 * SPAN), pl.ds(0, 4 * QUERIES)],
            e_h.at[window, half],
            e_out_sem.at[slot, half],
        )

    for window in range(2):
        await_upper(window)
        prepare_upper(window)
    prepare_masks(jnp.int32(0))

    @pl.loop(0, WINDOWS)
    def _(window):
        @pl.when(window == 1)
        def _():
            await_upper(2)
            prepare_upper(2)

        @pl.when(window > 0)
        def _():
            await_upper(window + 2)

        @pl.when(window > 1)
        def _():
            for half in range(2):
                e_out(window - 2, half).wait()

        slot = window % 2
        at = pl.multiple_of(window * QUERIES, QUERIES)
        here, span = pl.ds(at, QUERIES), pl.ds(at, SPAN)

        def scores(head):
            pair = head // 2
            q_head = head_of_pair(qs[pair * 128 : pair * 128 + 128, here], head % 2)
            upper = dot(
                jnp.concatenate([keys_up[pair, span, :], bias_up[...]], axis=1),
                jnp.concatenate([q_head, ones_row[...]], axis=0),
            )
            lower = dot(keys[pair, span, :], q_head) + bias_low[...]
            shape = (SPAN // 8, 8, QUERIES)
            top = jnp.maximum(
                jnp.max(upper.reshape(shape), axis=0), jnp.max(lower.reshape(shape), axis=0)
            )
            return upper, lower, jnp.max(top, axis=0, keepdims=True)

        def mix(head, e_up, e_low):
            mixed = dot(vt_up[head, :, span], e_up) + dot(vt[head, :, span], e_low)
            inverse = 1.0 / mixed[HEAD_DIM : HEAD_DIM + 1]
            rows = slice(head * HEAD_DIM, head * HEAD_DIM + HEAD_DIM)
            ot[rows, here] = (mixed[0:HEAD_DIM] * inverse).astype(BF16)
            inv[head : head + 1, here] = inverse

        current, raised = scores(0), None
        for head in range(8):
            upcoming = scores(head + 1) if head < 7 else None
            if head == 6:
                prepare_upper(jnp.where(window == 0, 1, jnp.minimum(window + 2, WINDOWS - 1)))
                prepare_masks(jnp.minimum(window + 1, WINDOWS - 1))
            upper, lower, peak = current
            e_up = jnp.exp2(upper - peak).astype(BF16)
            e_low = jnp.exp2(lower - peak).astype(BF16)
            at_row, at_lane = head % 2 * 2 * SPAN, head // 2 * QUERIES
            hd[slot, at_row : at_row + SPAN, at_lane : at_lane + QUERIES] = e_up
            hd[slot, at_row + SPAN : at_row + 2 * SPAN, at_lane : at_lane + QUERIES] = e_low
            if head > 0:
                mix(head - 1, *raised)
            raised = (e_up, e_low)
            current = upcoming
        mix(7, *raised)
        for half in range(2):
            e_out(window, half).start()

    loads[7].start()
    for load in loads[4:7]:
        load.wait()
    wta[...] = transposed(eye, wo[...])
    wit[...] = transposed(eye, wi[...])
    wbt[...] = transposed(eye, wb[...])
    for index, ref in enumerate((bb_ref, g1_ref, s1_ref, g2_ref, s2_ref)):
        cols[index] = column(eye, ref[...].reshape(1, -1)).astype(BF16)
    bi_col[...] = column(eye, bi_ref[...].reshape(1, -1)).astype(BF16)
    acc[...] = jnp.zeros_like(acc)
    for window in range(WINDOWS - 2, WINDOWS):
        for half in range(2):
            e_out(window, half).wait()
    loads[7].wait()
    hl, dh = hd.at[0], hd.at[1]
    dr2_buf = bias_low
    heads = width // HEAD_DIM

    def broadcast(index):
        return wide(cols[index].astype(F32))

    def gather(index, value):
        blocks = pl.ds(index * width // 128, width // 128)
        acc[blocks] += halves(value).reshape(width // 128, 128, 128)

    def out_copy(window):
        columns = pl.ds(pl.multiple_of(window * BLOCK_COLS, BLOCK_COLS), BLOCK_COLS)
        return pltpu.make_async_copy(
            tok.at[:, columns, :], out_h.at[:, columns, :], out_sem.at[window]
        )

    part = 256
    parts = [slice(at, at + part) for at in range(0, ff, part)]

    def columns_at(window):
        return pl.ds(pl.multiple_of(window * QUERIES, QUERIES), QUERIES)

    def forward_start(window):
        raw = raw_window(tok, window)
        embed = embed_window(embed_rows, window)
        start = jnp.concatenate(
            [
                dot_nt(eye, raw[:, half * 256 : half * 256 + 256])
                + dot_nt(eye, embed[:, half * 256 : half * 256 + 256])
                for half in range(2)
            ],
            axis=0,
        )
        here = columns_at(window)
        n1, inv1 = norm_stats(start + dot(wta[...], ot[:, here]))
        low = (n1 * broadcast(1) + broadcast(2)).astype(BF16)
        n1_buf[window % 2] = n1.astype(BF16)
        inv_buf[window % 2, 0:1, :] = inv1
        cols_a[:, 0:HEAD_DIM, here] = low.reshape(heads, HEAD_DIM, QUERIES)
        return low

    def activate(window, index, product):
        u = product + wide(bi_col[parts[index], :].astype(F32))
        active, slope = gelu_and_slope(u)
        hl[parts[index], columns_at(window)] = active.astype(BF16)
        dh[parts[index], columns_at(window)] = slope.astype(BF16)

    def forward_end(window, f):
        y1 = n1_buf[window % 2].astype(F32) * broadcast(1) + broadcast(2)
        n2, inv2 = norm_stats(y1 + f + broadcast(0))
        g2 = broadcast(3)
        result = (n2 * g2 + broadcast(4)).astype(BF16)
        result = dot_nt(eye, result).astype(BF16)
        raw_cot = raw_window(side, window)
        for half in range(2):
            at = pl.multiple_of((2 * window + half) * FLANK_COLS, FLANK_COLS)
            tok[:, pl.ds(at, FLANK_COLS), :] = result[half * TILE : half * TILE + TILE].reshape(
                BLOCK_ROWS, FLANK_COLS, -1
            )
        cot = jnp.concatenate(
            [dot_nt(eye, raw_cot[:, half * 256 : half * 256 + 256]) for half in range(2)], axis=0
        )
        gather(0, cot * n2)
        gather(1, cot)
        dr2 = norm_back(n2, inv2, cot, g2)
        dr2_buf[...] = dr2
        cols_b[:, 0:HEAD_DIM, columns_at(window)] = dr2.astype(BF16).reshape(
            heads, HEAD_DIM, QUERIES
        )

    def back_hidden(window, index, df_low):
        here = columns_at(window)
        slope = dh[parts[index], here].astype(F32)
        dh[parts[index], here] = (dot(wb[parts[index], :], df_low) * slope).astype(BF16)

    def back_input(window, quarter):
        rows = slice(quarter * ff // 4, (quarter + 1) * ff // 4)
        return dot(wi[:, rows], dh[rows, columns_at(window)])

    def back_end(window, dy1):
        here = columns_at(window)
        n1 = n1_buf[window % 2].astype(F32)
        gather(2, dy1 * n1)
        gather(3, dy1)
        dr1 = norm_back(n1, inv_buf[window % 2, 0:1, :], dy1, broadcast(1))
        da_low = dr1.astype(BF16)
        da[:, here] = da_low
        grad_o = dot(wo[...], da_low)
        product = grad_o * ot[:, here].astype(F32)
        for head in range(heads):
            rows = slice(head * HEAD_DIM, head * HEAD_DIM + HEAD_DIM)
            inverse = inv[head : head + 1, here]
            d_o[rows, here] = (grad_o[rows] * inverse).astype(BF16)
            dd[head : head + 1, here] = jnp.sum(product[rows], axis=0, keepdims=True) * inverse

    def step(back, ahead):
        df_low, dy1 = None, None
        if back is not None:
            df_low = cols_b[:, 0:HEAD_DIM, columns_at(back)].reshape(width, QUERIES)
            dy1 = dr2_buf[...]
            for index in range(2):
                back_hidden(back, index, df_low)
        if ahead is not None:
            low = forward_start(ahead)
            upcoming = dot(wit[parts[0], :], low)
        for index in range(len(parts)):
            if ahead is not None:
                current = upcoming
                if index + 1 < len(parts):
                    upcoming = dot(wit[parts[index + 1], :], low)
            if back is not None:
                if index < 3:
                    back_hidden(back, 2 * index + 2, df_low)
                    back_hidden(back, 2 * index + 3, df_low)
                elif index < 7:
                    dy1 = dy1 + back_input(back, index - 3)
            if ahead is not None:
                activate(ahead, index, current)
        if ahead is not None:
            f = dot(wbt[...], hl[:, columns_at(ahead)])
        if back is not None:
            back_end(back, dy1)
        if ahead is not None:
            forward_end(ahead, f)
            out_copy(ahead).start()

    assert len(parts) == 8
    step(None, 0)

    @pl.loop(0, WINDOWS - 1)
    def _(window):
        step(window, window + 1)

    step(WINDOWS - 1, None)

    small[...] = jnp.zeros_like(small)
    small_buf[...] = jnp.zeros_like(small_buf)
    ones = jnp.ones((8, 256), BF16)
    for index, row in enumerate((0, 1, 3, 4)):
        value = acc[pl.ds(index * width // 128, width // 128)].reshape(width, 128)
        high = value.astype(BF16)
        split = jnp.concatenate([high, (value - high.astype(F32)).astype(BF16)], axis=1)
        small[row : row + 1, :] = dot_nt(ones, split)[0:1]

    def e_in(pair, part, window, half):
        if window < 4:
            target = ww.at[0, pl.ds(window * SPAN, SPAN), pl.ds(half * QUERIES, QUERIES)]
        else:
            at = (2 * (window - 4) + half) * QUERIES
            target = wt.at[1, :, pl.ds(at, QUERIES)]
        source = e_h.at[
            window, half, pl.ds(part * SPAN, SPAN), pl.ds(pl.multiple_of(pair * QUERIES, QUERIES), QUERIES)
        ]
        return pltpu.make_async_copy(source, target, e_in_sem.at[window, half])

    def e_tile(window, half, first, last):
        if window < 4:
            return ww[0, window * SPAN + first : window * SPAN + last, half * QUERIES : (half + 1) * QUERIES]
        at = (2 * (window - 4) + half) * QUERIES
        return wt[1, first:last, at : at + QUERIES]

    items = [(window, half) for window in range(WINDOWS) for half in range(2)]
    for window, half in items:
        e_in(0, 0, window, half).start()

    qkv_at = 3 * width
    gback, gin = ww.at[1], wt.at[0]
    gout = wt.at[1, :, pl.ds(4 * QUERIES, width)]
    sum_back = Reduction(
        gback, (ff, width), back_recv, back_later, back_across, back_parts if back_split else None,
        lambda k: back_ss.at[k], lambda k: back_rs.at[k], place,
    )
    sum_out = Reduction(
        gout, (width, width), out_recv, out_later, out_across, None,
        lambda k: go_ss.at[k], lambda k: go_rs.at[k], place,
    )
    sum_in = Reduction(
        gin, (width, ff), in_recv, in_later, in_across, in_parts if in_split else None,
        lambda k: in_ss.at[k], lambda k: in_rs.at[k], place,
    )

    def write_in(value, columns=slice(None)):
        gin_ref[:, columns] = value

    def write_back(value, columns=slice(None)):
        gback_ref[:, columns] = value

    def write_out(value):
        gout_ref[...] = value

    def write_qkv(pair):
        def write(value):
            qkv_ref[pair] = value

        return write

    def sum_qkv(pair, direct=False):
        return Reduction(
            hd.at[1, pl.ds(qkv_at, width), pl.ds(pl.multiple_of(pair * 384, 128), 384)],
            (width, 384), qkv_recv.at[pair], qkv_later.at[pair], qkv_across.at[pair], None,
            lambda k: qkv_ss.at[pair, k], lambda k: qkv_rs.at[pair, k], place, direct,
        )

    sum_small = Reduction(
        small_buf, (16 * size, 128), small_recv, small_later, small_across, None,
        lambda k: small_ss.at[k], lambda k: small_rs.at[k], place, True,
    )
    share, back_share = width // size, ff // size
    ones_rows = jnp.where(iota((16, LEN), 0) == 0, 1.0, 0.0).astype(BF16)

    tall = 512

    @pl.loop(0, ff // tall)
    def _(index):
        rows = pl.ds(pl.multiple_of(index * tall, tall), tall)
        df = cols_b[:, 0:HEAD_DIM, 0:LEN].reshape(width, LEN)
        grad = dot_nt(jnp.concatenate([hl[rows, :], ones_rows], axis=0), df)
        shares = tall // back_share
        for piece in range(shares):
            at = reversed_bits(index * shares + piece, size) * back_share
            gback[pl.ds(pl.multiple_of(at, back_share), back_share), :] = grad[
                piece * back_share : (piece + 1) * back_share
            ].astype(BF16)
        small[2:3, :] = grad[tall : tall + 1]

    sum_back.start(0)

    def scatter_shares(ref, grad, first_lane):
        low = grad.astype(BF16)
        for owner in range(size):
            at = pl.multiple_of(reversed_bits(owner, size) * share, share)
            ref[pl.ds(at, share), first_lane : first_lane + grad.shape[1]] = low[
                owner * share : owner * share + share
            ]

    scatter_shares(gout, dot_nt(ot[...], da[...]), 0)
    sum_out.start(0)
    step_back = Steps(sum_back, write_back)
    step_out = Steps(sum_out, write_out)
    step_in = Steps(sum_in, write_in)

    yl_rows = jnp.concatenate([cols_a[:, 0:HEAD_DIM, 0:LEN].reshape(width, LEN), ones_rows], axis=0)
    for index in range(ff // 256):
        at = index * 256
        grad = dot_nt(yl_rows, dh[at : at + 256, :])
        scatter_shares(gin, grad[0:width], at)
        row, lane = 5 + at // width, at % width
        small[row : row + 1, lane : lane + 256] = grad[width : width + 1]
        if index == 1:
            step_back()
        if index == 3:
            step_out()
    sum_in.start(0)

    vals, vals_up, kt, kt_up = rows_a, rows_b, cols_a, cols_b
    w3 = ot
    d3, w2 = hd.at[0, pl.ds(0, 3 * width)], hd.at[0, pl.ds(3 * width, width), pl.ds(0, 2 * width)]
    d2, dxu = hd.at[1, pl.ds(0, 2 * width)], hd.at[1, pl.ds(2 * width, width)]
    wtb[...] = transposed(eye, wk[...])
    for pair in range(4):
        lanes = slice(pair * 128, pair * 128 + 128)
        for index, ref in enumerate((wq, wk, wv)):
            w3[:, pair * 384 + index * 128 : pair * 384 + index * 128 + 128] = ref[:, lanes]
        for index, ref in enumerate((wk, wv)):
            w2[:, pair * 256 + index * 128 : pair * 256 + index * 128 + 128] = ref[:, lanes]
    clear_pads_lanes(kt)
    clear_pads_lanes(kt_up)

    @pl.loop(0, WINDOWS)
    def _(window):
        @pl.when(window == 2)
        def _():
            step_in()

        here = pl.ds(pl.multiple_of(window * QUERIES, QUERIES), QUERIES)
        padded_at = pl.multiple_of(window * QUERIES + TILE, TILE)
        low = transposed(eye, xt[:, here])
        upper = transposed(eye, xut[:, here])
        store_pairs(vals, padded_at, dot(low, wv[...]).astype(BF16))
        store_heads(kt, padded_at, dot(wtb[...], xt[:, here]).astype(BF16))
        store_pairs(vals_up, padded_at, dot(upper, wv[...]).astype(BF16))
        store_heads(kt_up, padded_at, dot(wtb[...], xut[:, here]).astype(BF16))

    blocks = PADDED // 128

    shape = (8, LEN)
    channel = (iota(shape, 1) // TILE + iota(shape, 1) % FLANK_COLS) % 3
    chosen = jnp.where(channel == iota(shape, 0), 1.0, 0.0).astype(BF16)

    def pass_over(pair, part, v_rows, k_cols):
        feats = pl.ds(pl.multiple_of(pair * 128, 128), 128)
        follow = pair + 1
        next_pair, next_part = follow % 4, jnp.minimum(part + follow // 4, 1)

        def limits(window):
            first = TILE if window == 0 else 0
            last = SPAN - TILE if window == WINDOWS - 1 else SPAN
            return first, last

        def grad_probs(window, half):
            first, last = limits(window)
            here = slice(window * QUERIES, window * QUERIES + QUERIES)
            rows = slice(window * QUERIES + first, window * QUERIES + last)
            return dot(v_rows[pair, rows, :], head_of_pair(d_o[feats, here], half))

        def add_blocks(base, window, half, value):
            first, last = limits(window)
            rows = slice(half * HEAD_DIM, half * HEAD_DIM + HEAD_DIM)
            for at in range(first, last, 128):
                block = (window * QUERIES + at) // 128
                piece = value[:, at - first : at - first + 128]
                if window > 0 and at < SPAN - QUERIES:
                    piece = piece + acc[base + block, rows, :]
                acc[base + block, rows, :] = piece

        upcoming = grad_probs(*items[0])
        for index, (window, half) in enumerate(items):
            if index % 6 == 0:
                for coming in items[index : index + 6]:
                    e_in(pair, part, *coming).wait()
            current = upcoming
            if index + 1 < len(items):
                upcoming = grad_probs(*items[index + 1])
            first, last = limits(window)
            here = slice(window * QUERIES, window * QUERIES + QUERIES)
            span = slice(window * QUERIES + first, window * QUERIES + last)
            head = 2 * pair + half
            mine = pl.ds(pl.multiple_of(pair * 128 + half * HEAD_DIM, HEAD_DIM), HEAD_DIM)
            e = e_tile(window, half, first, last)
            ds = (e.astype(F32) * (current - dd[pl.ds(head, 1), here])).astype(BF16)
            dq = dot(k_cols[head, 0:HEAD_DIM, span], ds)
            at = pl.ds(pl.multiple_of(pair * 384 + half * HEAD_DIM, HEAD_DIM), HEAD_DIM)
            if part == 0:
                d3[at, here] = dq.astype(BF16)
            else:
                d3[at, here] = ((dq + d3[at, here].astype(F32)) * 0.125).astype(BF16)
            add_blocks(0, window, half, dot_nt(qt[mine, here], ds))
            add_blocks(blocks, window, half, dot_nt(d_o[mine, here], e))
            if index % 6 == 5:
                for done in items[index - 5 : index + 1]:
                    e_in(next_pair, next_part, *done).start()

    def take_blocks(ref, at, base):
        for block in range(1, blocks - 1):
            ref[pl.ds(at, 128), block * 128 - 128 : block * 128] = acc[base + block].astype(BF16)

    @pl.loop(0, 4)
    def _(pair):
        pass_over(pair, 0, vals_up, kt_up)
        at = pl.multiple_of(pair * 256, 256)
        take_blocks(d2, at, 0)
        take_blocks(d2, at + 128, blocks)

        @pl.when(pair == 0)
        def _():
            step_back()
            step_out()

        @pl.when(pair == 2)
        def _():
            step_back()
            step_out()
            step_in()

        @pl.when(pair == 3)
        def _():
            step_back()
            step_out()

    def send_halo(window):
        @pl.when(band > 0)
        def _():
            halo(window).start()

    for window in range(WINDOWS):
        here = slice(window * QUERIES, window * QUERIES + QUERIES)
        dxu[:, here] = dot(w2[...], d2[:, here]).astype(BF16)
        if window < 2:
            send_halo(window)

    embed_sum[0:8, :] = dot_nt(chosen, da[...]) + dot_nt(chosen, dxu[...]) * has_up
    embed_sum[8:16, :] = jnp.zeros((8, width), F32)

    @pl.loop(0, 4)
    def _(pair):
        pass_over(pair, 1, vals, kt)

        for turn in range(4):

            @pl.when(pair == turn)
            def _(turn=turn):
                if turn == 0:
                    step_back()
                if turn < 3:
                    step_in()
                if turn > 0:
                    sum_qkv(turn - 1, turn != 2).advance(0)
                if turn == 3:
                    sum_qkv(1).advance(1)
                if turn < 2:
                    send_halo(2 * turn + 2)
                    send_halo(2 * turn + 3)

        at = pl.multiple_of(pair * 384, 128)
        take_blocks(d3, at + 128, 0)
        take_blocks(d3, at + 256, blocks)
        grads = dot_nt(xt[...], d3[pl.ds(at, 384), :])
        grads_up = dot_nt(xut[...], d2[pl.ds(pl.multiple_of(pair * 256, 256), 256), :])
        lanes = pl.ds(pl.multiple_of(pair * 384, 128), 128)
        low_q = grads[:, 0:128].astype(BF16)
        low_kv = (grads[:, 128:384] + grads_up).astype(BF16)
        for owner in range(size):
            rows = slice(owner * share, owner * share + share)
            to = pl.ds(pl.multiple_of(qkv_at + reversed_bits(owner, size) * share, share), share)
            hd[1, to, lanes] = low_q[rows]
            hd[1, to, pl.ds(pl.multiple_of(pair * 384 + 128, 128), 256)] = low_kv[rows]
        sum_qkv(pair).start(0)
        totals = dot_nt(chosen, d3[pl.ds(at, 384), :])
        high = totals.astype(BF16)
        low = (totals - high.astype(F32)).astype(BF16)
        embed_sum[...] += dot_nt(
            jnp.concatenate([high, low], axis=0), w3[:, pl.ds(pl.multiple_of(pair * 384, 128), 384)]
        )

    rows = jnp.concatenate([small[0:8], embed_sum[0:8] + embed_sum[8:16]], axis=0)
    for owner in range(size):
        at = pl.multiple_of(reversed_bits(owner, size) * 16, 16)
        small_buf[pl.ds(at, 16), 0:share] = rows[:, owner * share : owner * share + share]
        row, lane = 5 + owner * back_share // width, owner * back_share % width
        small_buf[pl.ds(at + 5, 1), 0:back_share] = small[row : row + 1, lane : lane + back_share]
    sum_small.start(0)
    for window, half in items:
        e_in(0, 1, window, half).wait()

    @pl.when(band == size - 1)
    def _():
        below[...] = jnp.zeros_like(below)

    for window in range(WINDOWS):
        out_copy(window).wait()

    def gt_copy(window):
        columns = pl.ds(pl.multiple_of(window * BLOCK_COLS, BLOCK_COLS), BLOCK_COLS)
        return pltpu.make_async_copy(
            side.at[:, columns, :], gt_h.at[:, columns, :], out_sem.at[window]
        )

    @pl.loop(0, WINDOWS)
    def _(window):
        @pl.when(band < size - 1)
        def _():
            halo(window).wait_recv()

        here = pl.ds(pl.multiple_of(window * QUERIES, QUERIES), QUERIES)
        dx = da[:, here].astype(F32) + dot(w3[...], d3[:, here]) + below[:, here].astype(F32)
        rows = dot_nt(eye, dx.astype(BF16)).astype(BF16)
        for half in range(2):
            at = pl.multiple_of((2 * window + half) * FLANK_COLS, FLANK_COLS)
            side[:, pl.ds(at, FLANK_COLS), :] = rows[half * TILE : half * TILE + TILE].reshape(
                BLOCK_ROWS, FLANK_COLS, -1
            )
        gt_copy(window).start()

        @pl.when(window == 0)
        def _():
            sum_qkv(0, True).advance(1)

        @pl.when(window == 1)
        def _():
            sum_qkv(3, True).advance(0)
            sum_small.advance(0)
            sum_qkv(1).advance(2)

        @pl.when(window == 2)
        def _():
            step_back.last()

        @pl.when(window == 3)
        def _():
            step_in.last()

        @pl.when(window == 4)
        def _():
            step_out.last()
            sum_qkv(2, True).advance(1)

        @pl.when(window == 5)
        def _():
            sum_qkv(1).advance(3)

    for stage in range(4, depth):
        sum_qkv(1).advance(stage)
    sum_qkv(3, True).advance(1)
    sum_small.advance(1)
    sum_qkv(0, True).finish(write_qkv(0))
    sum_qkv(1).finish(write_qkv(1))
    sum_qkv(2, True).finish(write_qkv(2))

    def write_small(value):
        small_ref[...] = value

    sum_qkv(3, True).finish(write_qkv(3))
    sum_small.finish(write_small)

    for window in range(WINDOWS):
        gt_copy(window).wait()

    @pl.when(band > 0)
    def _():
        for window in range(WINDOWS):
            halo(window).wait_send()

    @pl.when(band < size - 1)
    def _():
        for window in range(WINDOWS):
            up_copy(window).wait_send()


def emit_kernel(
    out_in, gt_in, qkv_in, gin_in, gback_in, gout_in, small_in,
    out_h, gt_h, gq, gk, gv, gout, gin, gbi, gback, gbb, gg1, gs1, gg2, gs2, gemb,
    qkv, small, large, sems, large_sems,
):
    pairs = (
        (small_in, small), (qkv_in, qkv), (gback_in, gback), (gin_in, gin), (gout_in, gout),
    )
    moves = []
    for index, (source, target) in enumerate(((out_in, out_h), (gt_in, gt_h))):
        for row in range(0, BLOCK_ROWS, 2):
            rows, held = pl.ds(row, 2), large.at[index, pl.ds(row, 2)]
            sem = index * 4 + row // 2
            moves.append(
                (
                    pltpu.make_async_copy(source.at[rows], held, large_sems.at[0, sem]),
                    pltpu.make_async_copy(held, target.at[rows], large_sems.at[1, sem]),
                )
            )
    for load, _ in moves:
        load.start()
    copies = [
        pltpu.make_async_copy(source, target, sems.at[index])
        for index, (source, target) in enumerate(pairs)
    ]
    for copy in copies:
        copy.start()
    for load, store in moves:
        load.wait()
        store.start()
    copies[0].wait()
    share, back_share = gq.shape[0], gbi.shape[0]
    for row, ref in ((2, gbb), (3, gg1), (4, gs1), (0, gg2), (1, gs2)):
        ref[...] = small[row : row + 1, 0:share].reshape(-1)
    gemb[...] = small[8:11, 0:share]
    gbi[...] = small[5:6, 0:back_share].reshape(-1)
    copies[1].wait()
    for pair in range(4):
        for index, ref in enumerate((gq, gk, gv)):
            ref[:, pair * 128 : pair * 128 + 128] = qkv[pair, :, index * 128 : index * 128 + 128]
    for copy in copies[2:]:
        copy.wait()
    for _, store in moves:
        store.wait()


def shards(
    tokens, row_place, row_width, cotangent, chan_embed, w_query, w_key, w_value, w_out, w_in,
    bias_in, w_back, bias_back, gain_first, shift_first, gain_second, shift_second,
):
    width = tokens.shape[3]
    ff = w_in.shape[1]
    tok = tokens.reshape(BLOCK_ROWS, ROW_POS, width)
    cot = cotangent.reshape(BLOCK_ROWS, ROW_POS, width)
    shape = jax.ShapeDtypeStruct
    size, groups = lax.axis_size("band"), lax.axis_size("grp")
    dma = pltpu.SemaphoreType.DMA
    share, back_share = width // size, ff // size
    stages = size // 2 + 2 * groups
    in_split = ff // groups % 128 == 0
    back_split = width // groups % 128 == 0
    rows = shape((BLOCK_ROWS, ROW_POS, width), BF16)

    def later(split, total_rows, columns):
        return pltpu.VMEM((total_rows // 2, columns // groups if split else columns), BF16)

    def across(split, total_rows, columns):
        if split:
            return pltpu.VMEM((groups - 1, total_rows // 2, columns // groups), BF16)
        return pltpu.VMEM((groups, total_rows // size, columns), BF16)

    flat = pltpu.VMEM((width, LEN), BF16)
    out, gt, _, qkv, gin, gback, gout, small = pl.pallas_call(
        functools.partial(
            layer_kernel, size=size, groups=groups, in_split=in_split, back_split=back_split
        ),
        name="layer_forward_and_back",
        out_shape=(
            rows,
            rows,
            shape((WINDOWS, 2, 2 * SPAN, 4 * QUERIES), BF16),
            shape((4, share, 384), F32),
            shape((share, ff), F32),
            shape((back_share, width), F32),
            shape((share, width), F32),
            shape((16, 128), F32),
        ),
        in_specs=[smem()] * 2 + [vmem()] * 7 + [hbm()] * 8,
        out_specs=(hbm(),) * 3 + (vmem(),) * 5,
        scratch_shapes=[
            pltpu.VMEM(rows.shape, BF16),
            pltpu.VMEM(rows.shape, BF16),
            pltpu.VMEM((4, width, width), BF16),
            pltpu.VMEM((width, width), BF16),
            pltpu.VMEM((width, width), BF16),
            pltpu.VMEM((2, ff, width), BF16),
            pltpu.VMEM((2, width, ff), BF16),
            flat,
            flat,
            flat,
            flat,
            flat,
            pltpu.VMEM((4, PADDED, 128), BF16),
            pltpu.VMEM((4, PADDED, 128), BF16),
            pltpu.VMEM((8, HEAD_DIM + 16, PADDED), BF16),
            pltpu.VMEM((8, HEAD_DIM + 16, PADDED), BF16),
            pltpu.VMEM((2, ff, LEN), BF16),
            pltpu.VMEM((SPAN, QUERIES), F32),
            pltpu.VMEM((3 * FLANK_COLS, width), BF16),
            pltpu.VMEM((5, width, 128), BF16),
            pltpu.VMEM((ff, 128), BF16),
            pltpu.VMEM((2, width, QUERIES), BF16),
            pltpu.VMEM((2, 8, QUERIES), F32),
            flat,
            pltpu.VMEM((2 * PADDED // 128, 128, 128), F32),
            flat,
            pltpu.VMEM((8, LEN), F32),
            pltpu.VMEM((8, LEN), F32),
            pltpu.VMEM((width // 2, ff), BF16),
            later(in_split, width, ff),
            across(in_split, width, ff),
            pltpu.VMEM((groups, share, ff // groups), F32),
            pltpu.VMEM((ff // 2, width), BF16),
            later(back_split, ff, width),
            across(back_split, ff, width),
            pltpu.VMEM((groups, back_share, width // groups), F32),
            pltpu.VMEM((width // 2, width), BF16),
            pltpu.VMEM((width // 2, width), BF16),
            pltpu.VMEM((groups, share, width), BF16),
            pltpu.VMEM((4, width // 2, 384), BF16),
            pltpu.VMEM((4, width // 2, 384), BF16),
            pltpu.VMEM((4, groups, share, 384), BF16),
            pltpu.VMEM((16, width), F32),
            pltpu.VMEM((16 * size, 128), F32),
            pltpu.VMEM((8 * size, 128), F32),
            pltpu.VMEM((8 * size, 128), F32),
            pltpu.VMEM((groups, 16, 128), F32),
            pltpu.VMEM((16, width), F32),
            dma((8,)),
            dma((2, 2)),
            dma((WINDOWS, 2)),
            dma((WINDOWS,)),
            dma((WINDOWS,)),
            dma((WINDOWS,)),
            dma((WINDOWS,)),
            dma((WINDOWS,)),
            dma((stages,)),
            dma((stages,)),
            dma((stages,)),
            dma((stages,)),
            dma((stages,)),
            dma((stages,)),
            dma((4, stages)),
            dma((4, stages)),
            dma((stages,)),
            dma((stages,)),
        ],
        compiler_params=pltpu.CompilerParams(
            vmem_limit_bytes=LIMIT, collective_id=0, has_side_effects=True
        ),
    )(
        row_place, row_width, chan_embed, bias_in, bias_back, gain_first, shift_first, gain_second,
        shift_second, tok, cot, w_query, w_key, w_value, w_out, w_in, w_back,
    )
    vector = shape((share,), F32)
    square = shape((share, width), F32)
    out, gt, gq, gk, gv, gout, gin, gbi, gback, gbb, gg1, gs1, gg2, gs2, gemb = pl.pallas_call(
        emit_kernel,
        name="emit_shares",
        out_shape=(
            rows, rows, square, square, square, square, shape((share, ff), F32),
            shape((back_share,), F32), shape((back_share, width), F32),
            vector, vector, vector, vector, vector, shape((3, share), F32),
        ),
        in_specs=[hbm()] * 7,
        out_specs=(hbm(),) * 2 + (vmem(),) * 3 + (vmem(), vmem(), vmem(), vmem()) + (vmem(),) * 6,
        scratch_shapes=[
            pltpu.VMEM((4, share, 384), F32),
            pltpu.VMEM((16, 128), F32),
            pltpu.VMEM((2,) + rows.shape, BF16),
            dma((5,)),
            dma((2, 8)),
        ],
        compiler_params=pltpu.CompilerParams(vmem_limit_bytes=LIMIT),
    )(out, gt, qkv, gin, gback, gout, small)
    return (
        out.reshape(tokens.shape),
        gt.reshape(tokens.shape),
        gq, gk, gv, gout, gin, gbi, gback, gbb, gg1, gs1, gg2, gs2, gemb,
    )


def solution(mesh):
    tall = P("grp", "band", None, None)
    return jax.shard_map(
        shards,
        mesh=mesh,
        in_specs=(tall, P("grp", "band"), P("grp", "band"), tall) + (P(),) * 13,
        out_specs=(tall, tall)
        + (P("band", None),) * 5
        + (P("band"), P("band", None))
        + (P("band"),) * 5
        + (P(None, "band"),),
        check_vma=False,
    )
```
